32 devices in a mesh: grp: 4 (over y, x), slab: 8 (over z, core).
Axes of the slice: x: 2, y: 2, z: 4, core: 2. Of those that a mesh axis runs over, the one named last changes fastest.
Arguments:
- margin: bfloat16 [128, 5, 128, 128], P(('grp', 'slab')), may hold values from -2 to 2
- factor: bfloat16 [128, 5, 128, 128], P(('grp', 'slab')), may hold values from -2 to 2
- pattern: int32 [128, 5], P(('grp', 'slab')), may hold values from 0 to 1, as said below
Outputs:
- refined: bfloat16 [128, 5, 128, 128], P(('grp', 'slab'))
- defect_norm: float32 [], replicated
The draws below stay inside these ranges and needn't reach their ends.
Inputs may be any that keep to these rules, and one draw needn't show every extreme that they name: The pattern is symmetric: pattern[j, o] equals pattern[j + o - 2, 4 - o]. The diagonal block (o = 2) is always present and blocks whose row lies outside the matrix are absent; the share of present blocks varies from region to region.
All inputs are finite; a program needn't handle non-finite values.
Results may differ from the reference program's by a relative error of at most 0.0054.
Values may be sent and summed in bfloat16 or wider, within the bound.
No kernel may reach another device: no remote copies, remote signals or barrier semaphores. Data moves between devices by JAX's collectives and lax.ppermute only.
A program may use at most 64 MiB of HBM per device.

```python
import jax
import jax.numpy as jnp
from jax import lax

B = 128
W = 2
CB = 4
QB = 32
NB = 128


def rough_blocks(key, shape):
    return jax.random.truncated_normal(key, -4.0, 4.0, shape, jnp.float32)


def region_length():
    return max(QB // 2, 1)


def draw_margin(key, part):
    span = region_length()
    region_count = NB // span + 1
    log_level = jax.random.uniform(jax.random.fold_in(key, 103), (region_count,), jnp.float32, jnp.log(0.15), jnp.log(1.0))
    level = jnp.exp(log_level)
    growth = level[jnp.arange(NB) // span] / B ** 0.5
    upper_blocks = rough_blocks(jax.random.fold_in(key, 101), (NB, W, B, B)) * growth[:, None, None, None]
    diag_noise = rough_blocks(jax.random.fold_in(key, 102), (NB, B, B)) * (0.3 / B ** 0.5)
    diagonal = jnp.eye(B, dtype=jnp.float32)[None] + 0.5 * (diag_noise + jnp.swapaxes(diag_noise, 1, 2))
    pieces = []
    for distance in range(W, 0, -1):
        pieces.append(upper_blocks[:, distance - 1])
    pieces.append(diagonal)
    for distance in range(1, W + 1):
        shifted_up = jnp.concatenate([upper_blocks[distance:, distance - 1], jnp.zeros((distance, B, B), jnp.float32)], axis=0)
        pieces.append(jnp.swapaxes(shifted_up, 1, 2))
    return jnp.stack(pieces, axis=1).astype(jnp.bfloat16)


def draw_factor(key, part):
    spread_scale = 0.3
    blocks = rough_blocks(jax.random.fold_in(key, 201), (NB, 2 * W + 1, B, B)) * (spread_scale / B ** 0.5)
    centre = (jnp.arange(2 * W + 1) == W).astype(jnp.float32)[None, :, None, None] * jnp.eye(B, dtype=jnp.float32)[None, None]
    return (blocks + centre).astype(jnp.bfloat16)


def draw_pattern(key, part):
    span = region_length()
    region = jax.random.randint(jax.random.fold_in(key, 301), (NB // span + 1,), 3, 10)
    keep_level = region[jnp.arange(NB) // span]
    coin_draw = jax.random.randint(jax.random.fold_in(key, 302), (NB, W), 0, 10)
    upper_present = (coin_draw < keep_level[:, None]).astype(jnp.int32)
    column_index = jnp.arange(NB)
    pieces = []
    for distance in range(W, 0, -1):
        pieces.append(upper_present[:, distance - 1] * (column_index >= distance).astype(jnp.int32))
    pieces.append(jnp.ones((NB,), jnp.int32))
    for distance in range(1, W + 1):
        pieces.append(jnp.concatenate([upper_present[distance:, distance - 1], jnp.zeros((distance,), jnp.int32)], axis=0))
    return jnp.stack(pieces, axis=1).astype(jnp.int32)


def setup_inputs(seed: int = 0) -> dict:
    streams_of = jax.random.split(jax.random.key(seed), 4)
    return {
        "margin": draw_margin(jax.random.fold_in(streams_of[3], 71), 0),
        "factor": draw_factor(jax.random.fold_in(streams_of[3], 71), 0),
        "pattern": draw_pattern(jax.random.fold_in(streams_of[3], 71), 0),
    }


def image_terms(band_half):
    return [[(inner_lag, outer_lag - inner_lag + band_half, inner_lag + band_half) for inner_lag in range(max(-band_half, outer_lag - band_half), min(band_half, outer_lag + band_half) + 1)] for outer_lag in range(-2 * band_half, 2 * band_half + 1)]

def defect_terms(band_half):
    return [[(outer_lag, inner_lag - outer_lag + band_half, inner_lag + 2 * band_half) for inner_lag in range(outer_lag - band_half, outer_lag + band_half + 1)] for outer_lag in range(-band_half, band_half + 1)]

def near_terms(band_half):
    return [[(inner_lag, outer_lag - inner_lag + band_half, inner_lag + band_half) for inner_lag in range(max(-band_half, outer_lag - band_half), min(band_half, outer_lag + band_half) + 1)] for outer_lag in range(-band_half, band_half + 1)]

def band_product(left_ext, right_own, term_list, transpose_left, columns):
    left_stack = jnp.stack([left_ext[W + column_shift:W + column_shift + columns, left_offset] for column_shift, left_offset, right_offset in term_list], axis=1).astype(jnp.float32)
    right_stack = jnp.stack([right_own[:, right_offset] for column_shift, left_offset, right_offset in term_list], axis=1).astype(jnp.float32)
    einsum_form = 'cbkm,cbkn->cmn' if transpose_left else 'cbmk,cbkn->cmn'
    return jnp.einsum(einsum_form, left_stack, right_stack)

def stack_offsets(left_ext, right_own, term_lists, transpose_left, columns):
    outputs = [band_product(left_ext, right_own, term_list, transpose_left, columns) for term_list in term_lists]
    return jnp.stack(outputs, axis=1)

def reference(margin, factor, pattern):
    present = pattern.astype(jnp.bfloat16)[:, :, None, None]
    block_rows = jnp.arange(NB, dtype=jnp.int32)[:, None] + jnp.arange(2 * W + 1, dtype=jnp.int32)[None, :] - W
    own_quarter = (jnp.arange(NB, dtype=jnp.int32) // QB)[:, None]
    in_quarter = (block_rows // QB == own_quarter).astype(jnp.bfloat16)[:, :, None, None]
    s_eff = margin * present
    z_eff = factor * present * in_quarter
    centre = (jnp.arange(2 * W + 1, dtype=jnp.int32) == W).astype(jnp.float32)[None, :, None, None] * jnp.eye(B, dtype=jnp.float32)[None, None]
    pad_spec = ((W, W), (0, 0), (0, 0), (0, 0))
    s_pad = jnp.pad(s_eff, pad_spec)
    z_pad = jnp.pad(z_eff, pad_spec)
    group_ids = jnp.arange(NB // CB, dtype=jnp.int32)

    def first_pass(group):
        start = (group * CB).astype(jnp.int32)
        s_ext = lax.dynamic_slice_in_dim(s_pad, start, CB + 2 * W, 0)
        z_ext = lax.dynamic_slice_in_dim(z_pad, start, CB + 2 * W, 0)
        mask_here = lax.dynamic_slice_in_dim(present, start, CB, 0).astype(jnp.float32)
        applied = stack_offsets(s_ext, z_ext[W:W + CB], image_terms(W), False, CB).astype(jnp.bfloat16)
        return (mask_here * (centre - stack_offsets(z_ext, applied, defect_terms(W), True, CB))).astype(jnp.bfloat16)
    defect_all = lax.map(first_pass, group_ids).reshape(NB, 2 * W + 1, B, B)
    squares_sum = jnp.sum(jnp.square(defect_all.astype(jnp.float32)))
    defect_norm = jnp.sqrt(squares_sum / (NB * B))
    d_pad = jnp.pad(defect_all, pad_spec)

    def second_pass(group):
        start = (group * CB).astype(jnp.int32)
        d_ext = lax.dynamic_slice_in_dim(d_pad, start, CB + 2 * W, 0)
        z_ext = lax.dynamic_slice_in_dim(z_pad, start, CB + 2 * W, 0)
        mask_here = lax.dynamic_slice_in_dim(present, start, CB, 0).astype(jnp.float32)
        d_own = d_ext[W:W + CB]
        square = (mask_here * stack_offsets(d_ext, d_own, near_terms(W), False, CB)).astype(jnp.bfloat16)
        first_part = stack_offsets(z_ext, d_own, near_terms(W), False, CB)
        second_part = stack_offsets(z_ext, square, near_terms(W), False, CB)
        z_own = z_ext[W:W + CB].astype(jnp.float32)
        return (mask_here * (z_own + 0.5 * first_part + 0.375 * second_part)).astype(jnp.bfloat16)
    refined = lax.map(second_pass, group_ids).reshape(NB, 2 * W + 1, B, B)
    return (refined, defect_norm)
```

```python
import jax
import jax.numpy as jnp
from jax import lax
from jax.sharding import PartitionSpec as P


def padded(cells, sides, width):
    for axis, dim in sides:
        count = lax.axis_size(axis)
        ends = count - 1
        head = lax.slice_in_dim(cells, 0, width, axis=dim)
        tail = lax.slice_in_dim(cells, cells.shape[dim] - width, cells.shape[dim], axis=dim)
        cells = jnp.concatenate(
            [
                lax.ppermute(tail, axis, [(i, (i + 1) % count) for i in range(ends)]),
                cells,
                lax.ppermute(head, axis, [((i + 1) % count, i) for i in range(ends)]),
            ],
            axis=dim,
        )
    return cells


def image_terms(band_half):
    return [
        [
            (inner_lag, outer_lag - inner_lag + band_half, inner_lag + band_half)
            for inner_lag in range(
                max(-band_half, outer_lag - band_half), min(band_half, outer_lag + band_half) + 1
            )
        ]
        for outer_lag in range(-2 * band_half, 2 * band_half + 1)
    ]


def defect_terms(band_half):
    return [
        [
            (outer_lag, inner_lag - outer_lag + band_half, inner_lag + 2 * band_half)
            for inner_lag in range(outer_lag - band_half, outer_lag + band_half + 1)
        ]
        for outer_lag in range(-band_half, band_half + 1)
    ]


def near_terms(band_half):
    return [
        [
            (inner_lag, outer_lag - inner_lag + band_half, inner_lag + band_half)
            for inner_lag in range(
                max(-band_half, outer_lag - band_half), min(band_half, outer_lag + band_half) + 1
            )
        ]
        for outer_lag in range(-band_half, band_half + 1)
    ]


def band_product(left_ext, right_own, term_list, transpose_left, band_half, columns):
    left_stack = jnp.stack(
        [
            left_ext[band_half + column_shift : band_half + column_shift + columns, left_offset]
            for column_shift, left_offset, right_offset in term_list
        ],
        axis=1,
    )
    right_stack = jnp.stack(
        [right_own[:, right_offset] for column_shift, left_offset, right_offset in term_list],
        axis=1,
    )
    einsum_form = "cbkm,cbkn->cmn" if transpose_left else "cbmk,cbkn->cmn"
    return jnp.einsum(einsum_form, left_stack, right_stack, preferred_element_type=jnp.float32)


def stack_offsets(left_ext, right_own, term_lists, transpose_left, band_half, columns):
    outputs = [
        band_product(left_ext, right_own, term_list, transpose_left, band_half, columns)
        for term_list in term_lists
    ]
    return jnp.stack(outputs, axis=1)


def defect_halo(defect, band_half):
    return padded(defect, ((("grp", "slab"), 0),), band_half)


def defect_measure(defect, columns, block_size):
    partial_sum = jnp.sum(jnp.square(defect.astype(jnp.float32)))
    count = lax.axis_size("grp") * lax.axis_size("slab")
    spread = jnp.broadcast_to(partial_sum, (count, 128))
    squares_sum = jnp.sum(lax.all_to_all(spread, ("grp", "slab"), 0, 0, tiled=True)[:, 0])
    entries = columns * lax.axis_size("grp") * lax.axis_size("slab") * block_size
    return jnp.sqrt(squares_sum / entries)


def per_device(margin, factor, pattern):
    columns = margin.shape[0]
    offsets = margin.shape[1]
    band_half = (offsets - 1) // 2
    block_size = margin.shape[2]
    present = pattern.astype(jnp.bfloat16)[:, :, None, None]
    mask_here = present.astype(jnp.float32)
    first_col = lax.axis_index(("grp", "slab")) * columns
    quarter_len = columns * lax.axis_size("slab")
    block_rows = (
        first_col
        + jnp.arange(columns, dtype=jnp.int32)[:, None]
        + jnp.arange(offsets, dtype=jnp.int32)[None, :]
        - band_half
    )
    in_quarter = (block_rows // quarter_len == lax.axis_index("grp")).astype(jnp.bfloat16)[
        :, :, None, None
    ]
    s_eff = margin * present
    z_eff = factor * present * in_quarter
    centre = (jnp.arange(offsets, dtype=jnp.int32) == band_half).astype(jnp.float32)[
        None, :, None, None
    ] * jnp.eye(block_size, dtype=jnp.float32)[None, None]
    joined = jnp.concatenate((s_eff, z_eff), axis=1)
    joined_ext = padded(joined, ((("grp", "slab"), 0),), band_half)
    s_ext = joined_ext[:, :offsets]
    z_ext = joined_ext[:, offsets:]
    applied = stack_offsets(s_ext, z_eff, image_terms(band_half), False, band_half, columns).astype(
        jnp.bfloat16
    )
    defect = (
        mask_here
        * (
            centre
            - stack_offsets(z_ext, applied, defect_terms(band_half), True, band_half, columns)
        )
    ).astype(jnp.bfloat16)
    defect_norm = defect_measure(defect, columns, block_size)
    d_ext = defect_halo(defect, band_half)
    square = (
        mask_here * stack_offsets(d_ext, defect, near_terms(band_half), False, band_half, columns)
    ).astype(jnp.bfloat16)
    first_part = stack_offsets(z_ext, defect, near_terms(band_half), False, band_half, columns)
    second_part = stack_offsets(z_ext, square, near_terms(band_half), False, band_half, columns)
    refined = (
        mask_here * (z_eff.astype(jnp.float32) + 0.5 * first_part + 0.375 * second_part)
    ).astype(jnp.bfloat16)
    return (refined, defect_norm)


def solution(mesh):
    return jax.shard_map(
        per_device,
        mesh=mesh,
        in_specs=(
            P(("grp", "slab"), None, None, None),
            P(("grp", "slab"), None, None, None),
            P(("grp", "slab"), None),
        ),
        out_specs=(P(("grp", "slab"), None, None, None), P()),
        check_vma=False,
    )
```

```python
import functools

import jax
import jax.numpy as jnp
from jax import lax
from jax.experimental import pallas as pl
from jax.experimental.pallas import tpu as pltpu
from jax.sharding import PartitionSpec as P

AXES = ("grp", "slab")
ANY = pl.BlockSpec(memory_space=pl.ANY)
VMEM = pl.BlockSpec(memory_space=pltpu.VMEM)
SMEM = pl.BlockSpec(memory_space=pltpu.SMEM)
VMEM_LIMIT = 40 * 1024 * 1024


def place():
    slab = lax.axis_index("slab")
    return lax.axis_index("grp"), slab, lax.rem(slab, 2)


def keep(flag, block):
    return jnp.where(flag, block, jnp.zeros_like(block))


def in_quarter(row, quarter_len):
    return jnp.logical_and(row >= 0, row < quarter_len)


def factor_present(pattern, slab, columns, quarter_len, column, offset, band_half):
    row = slab * columns + column + offset - band_half
    return jnp.logical_and(pattern[column, offset] != 0, in_quarter(row, quarter_len))


def pack_kernel(quarter_len, margin, factor, pattern, near, far, cross, cells, sems):
    columns, offsets = margin.shape[0], margin.shape[1]
    band_half = (offsets - 1) // 2
    _, slab, odd = place()
    last = columns - band_half
    near_first = jnp.where(odd == 1, 0, last)
    far_first = last - near_first
    starts = (near_first, far_first)
    loads = []
    for side, first in enumerate(starts):
        for kind, source in enumerate((margin, factor)):
            copy = pltpu.make_async_copy(
                source.at[pl.ds(first, band_half)], cells.at[side, kind], sems.at[side, kind]
            )
            copy.start()
            loads.append(copy)
    for side in (1, 0):
        for kind in range(2):
            loads[2 * side + kind].wait()
            for t in range(band_half):
                for o in range(offsets):
                    column = starts[side] + t
                    if kind == 0:
                        flag = pattern[column, o] != 0
                    else:
                        flag = factor_present(
                            pattern, slab, columns, quarter_len, column, o, band_half
                        )
                    block = keep(flag, cells[side, kind, t, o])
                    (near, far)[side][kind, t, o] = block
                    u = t + o - band_half
                    if side == 1 and kind == 1 and 0 <= u < band_half:
                        cross[t, u] = block


def pack(margin, factor, pattern, quarter_len):
    columns, offsets, block, _ = margin.shape
    band_half = (offsets - 1) // 2
    message = jax.ShapeDtypeStruct((2, band_half, offsets, block, block), margin.dtype)
    return pl.pallas_call(
        functools.partial(pack_kernel, quarter_len),
        out_shape=(
            message,
            message,
            jax.ShapeDtypeStruct((band_half, band_half, block, block), margin.dtype),
        ),
        in_specs=[ANY, ANY, SMEM],
        out_specs=(VMEM, VMEM, VMEM),
        scratch_shapes=[
            pltpu.VMEM((2,) + message.shape, margin.dtype),
            pltpu.SemaphoreType.DMA((2, 2)),
        ],
        compiler_params=pltpu.CompilerParams(vmem_limit_bytes=VMEM_LIMIT),
        name="pack",
    )(margin, factor, pattern)


def spread_column(dense, first_row, first_lane, block, band_half, offsets, read):
    zeros = jnp.zeros((block, block), dense.dtype)
    for t in range(band_half):
        for a in range(3 * band_half):
            o = a - t
            value = read(t, o) if 0 <= o < offsets else zeros
            dense[
                first_row + a * block : first_row + (a + 1) * block,
                first_lane + t * block : first_lane + (t + 1) * block,
            ] = value


def defect_kernel(
    quarter_len,
    margin,
    factor,
    pattern,
    near,
    far,
    cross,
    defect,
    near_out,
    far_out,
    spread,
    own,
    halo,
    crossed,
    s_dense,
    z_dense,
    z_turned,
    image,
    sems,
):
    columns, offsets, block, _ = margin.shape
    band_half = (offsets - 1) // 2
    tile = band_half * block
    count = columns // band_half
    _, slab, odd = place()
    near_side = 1 - odd
    far_side = odd
    copies = [
        pltpu.make_async_copy(margin, own.at[0], sems.at[0]),
        pltpu.make_async_copy(factor, own.at[1], sems.at[1]),
        pltpu.make_async_copy(near, halo.at[near_side], sems.at[2]),
        pltpu.make_async_copy(far, halo.at[far_side], sems.at[3]),
        pltpu.make_async_copy(cross, crossed, sems.at[4]),
    ]
    for copy in copies:
        copy.start()
    copies[0].wait()
    copies[1].wait()

    def spot(pair):
        return (pair + 1) * tile

    def own_margin(c, t, o):
        column = c * band_half + t
        return keep(pattern[column, o] != 0, own[0, column, o])

    def own_factor(c, t, o):
        column = c * band_half + t
        flag = factor_present(pattern, slab, columns, quarter_len, column, o, band_half)
        return keep(flag, own[1, column, o])

    def turn(pair):
        for r in (pair - 1, pair, pair + 1):
            cell = z_dense[(r + 2) * tile : (r + 3) * tile, spot(pair) : spot(pair) + tile]
            z_turned[spot(pair) : spot(pair) + tile, (r + 2) * tile : (r + 3) * tile] = cell.T

    for c in range(count):
        for dense, read in ((s_dense, own_margin), (z_dense, own_factor)):
            spread_column(
                dense, spot(c), spot(c), block, band_half, offsets, functools.partial(read, c)
            )
        turn(c)
    for copy in copies[2:]:
        copy.wait()
    for t in range(band_half):
        for u in range(band_half):
            o = u - t + band_half
            halo[far_side, 1, t, o] = halo[far_side, 1, t, o] + crossed[t, u]
    for side, pair in ((0, -1), (1, count)):
        for kind, dense in ((0, s_dense), (1, z_dense)):
            spread_column(
                dense,
                spot(pair),
                spot(pair),
                block,
                band_half,
                offsets,
                lambda t, o: halo[side, kind, t, o],
            )
        turn(pair)

    eye = (
        lax.broadcasted_iota(jnp.int32, (block, block), 0)
        == lax.broadcasted_iota(jnp.int32, (block, block), 1)
    ).astype(jnp.float32)
    squares = jnp.zeros((8, block), jnp.float32)
    for c in range(count):
        for r in range(c - 2, c + 3):
            low, high = max(r - 1, c - 1), min(r + 1, c + 1) + 1
            image[c, (r - c + 2) * tile : (r - c + 3) * tile] = jnp.dot(
                s_dense[(r + 2) * tile : (r + 3) * tile, spot(low) : spot(high)],
                z_dense[(low + 2) * tile : (high + 2) * tile, spot(c) : spot(c) + tile],
                preferred_element_type=jnp.float32,
            ).astype(image.dtype)
        for i in range(c - 1, c + 2):
            product = jnp.dot(
                z_turned[spot(i) : spot(i) + tile, (i + 1) * tile : (i + 4) * tile],
                image[c, (i - c + 1) * tile : (i - c + 4) * tile],
                preferred_element_type=jnp.float32,
            )
            for u in range(band_half):
                for t in range(band_half):
                    o = (i - c) * band_half + u - t + band_half
                    rows = slice((i - c + 1) * tile + u * block, (i - c + 1) * tile + (u + 1) * block)
                    lanes = slice(t * block, (t + 1) * block)
                    if not 0 <= o < offsets:
                        defect[c, rows, lanes] = jnp.zeros((block, block), defect.dtype)
                        continue
                    value = -product[u * block : (u + 1) * block, lanes]
                    if o == band_half:
                        value = eye + value
                    value = keep(pattern[c * band_half + t, o] != 0, value).astype(defect.dtype)
                    defect[c, rows, lanes] = value
                    wide = value.astype(jnp.float32)
                    squares = squares + jnp.sum((wide * wide).reshape(-1, 8, block), axis=0)
    spread[...] = jnp.broadcast_to(jnp.sum(squares, axis=0, keepdims=True)[None], spread.shape)

    @pl.when(odd == 1)
    def _():
        near_out[...] = defect[0, : 2 * tile]
        far_out[...] = defect[count - 1, tile:]

    @pl.when(odd == 0)
    def _():
        near_out[...] = defect[count - 1, tile:]
        far_out[...] = defect[0, : 2 * tile]


def defect_step(margin, factor, pattern, near, far, cross, quarter_len, devices):
    columns, offsets, block, _ = margin.shape
    band_half = (offsets - 1) // 2
    tile = band_half * block
    count = columns // band_half
    kind = margin.dtype
    message = jax.ShapeDtypeStruct((2 * tile, tile), kind)
    products = count * 18
    return pl.pallas_call(
        functools.partial(defect_kernel, quarter_len),
        out_shape=(
            jax.ShapeDtypeStruct((count, 3 * tile, tile), kind),
            message,
            message,
            jax.ShapeDtypeStruct((devices, 1, block), jnp.float32),
        ),
        in_specs=[ANY, ANY, SMEM, ANY, ANY, ANY],
        out_specs=(VMEM, VMEM, VMEM, VMEM),
        scratch_shapes=[
            pltpu.VMEM((2,) + margin.shape, kind),
            pltpu.VMEM((2,) + near.shape, kind),
            pltpu.VMEM(cross.shape, kind),
            pltpu.VMEM(((count + 4) * tile, (count + 2) * tile), kind),
            pltpu.VMEM(((count + 4) * tile, (count + 2) * tile), kind),
            pltpu.VMEM(((count + 2) * tile, (count + 4) * tile), kind),
            pltpu.VMEM((count, 5 * tile, tile), kind),
            pltpu.SemaphoreType.DMA((5,)),
        ],
        compiler_params=pltpu.CompilerParams(vmem_limit_bytes=VMEM_LIMIT),
        cost_estimate=pl.CostEstimate(
            flops=products * 2 * tile**3, bytes_accessed=4 * 2**20, transcendentals=0
        ),
        name="defect",
    )(margin, factor, pattern, near, far, cross)


def refine_kernel(
    quarter_len,
    entries,
    factor,
    pattern,
    near,
    far,
    cross,
    defect,
    near_defect,
    far_defect,
    gathered,
    refined,
    norm,
    own,
    halo,
    crossed,
    z_dense,
    d_dense,
    square,
    sems,
):
    columns, offsets, block, _ = factor.shape
    band_half = (offsets - 1) // 2
    tile = band_half * block
    count = columns // band_half
    _, slab, odd = place()
    near_side = 1 - odd
    far_side = odd
    edge = count * tile
    near_row = pl.multiple_of(near_side * edge, tile)
    near_lane = pl.multiple_of(near_side * (edge + tile), tile)
    far_row = pl.multiple_of(far_side * edge, tile)
    far_lane = pl.multiple_of(far_side * (edge + tile), tile)
    copies = [
        pltpu.make_async_copy(factor, own, sems.at[0]),
        pltpu.make_async_copy(near.at[1], halo.at[near_side], sems.at[1]),
        pltpu.make_async_copy(far.at[1], halo.at[far_side], sems.at[2]),
        pltpu.make_async_copy(cross, crossed, sems.at[3]),
        pltpu.make_async_copy(
            near_defect,
            d_dense.at[pl.ds(near_row, 2 * tile), pl.ds(near_lane, tile)],
            sems.at[4],
        ),
        pltpu.make_async_copy(
            far_defect, d_dense.at[pl.ds(far_row, 2 * tile), pl.ds(far_lane, tile)], sems.at[5]
        ),
    ]
    for c in range(count):
        copies.append(
            pltpu.make_async_copy(
                defect.at[c],
                d_dense.at[c * tile : (c + 3) * tile, (c + 1) * tile : (c + 2) * tile],
                sems.at[6 + c],
            )
        )
    for copy in copies:
        copy.start()
    total = jnp.sum(gathered[...]) * (1.0 / entries)
    norm[...] = jnp.sqrt(jnp.full(norm.shape, total, jnp.float32))

    def own_factor(c, t, o):
        column = c * band_half + t
        flag = factor_present(pattern, slab, columns, quarter_len, column, o, band_half)
        return keep(flag, own[column, o])

    copies[0].wait()
    for c in range(count):
        spread_column(
            z_dense,
            (c + 1) * tile,
            (c + 1) * tile,
            block,
            band_half,
            offsets,
            functools.partial(own_factor, c),
        )
    for copy in copies[1:4]:
        copy.wait()
    for t in range(band_half):
        for u in range(band_half):
            o = u - t + band_half
            halo[far_side, t, o] = halo[far_side, t, o] + crossed[t, u]
    for side, pair in ((0, -1), (1, count)):
        spread_column(
            z_dense,
            (pair + 1) * tile,
            (pair + 1) * tile,
            block,
            band_half,
            offsets,
            lambda t, o: halo[side, t, o],
        )
    for copy in copies[4:]:
        copy.wait()

    for c in range(count):
        lanes_c = slice((c + 1) * tile, (c + 2) * tile)
        for i in range(c - 1, c + 2):
            low, high = max(i, c) - 1, min(i, c) + 2
            product = jnp.dot(
                d_dense[(i + 1) * tile : (i + 2) * tile, (low + 1) * tile : (high + 1) * tile],
                d_dense[(low + 1) * tile : (high + 1) * tile, lanes_c],
                preferred_element_type=jnp.float32,
            )
            for u in range(band_half):
                for t in range(band_half):
                    o = (i - c) * band_half + u - t + band_half
                    rows = slice((i - c + 1) * tile + u * block, (i - c + 1) * tile + (u + 1) * block)
                    lanes = slice(t * block, (t + 1) * block)
                    if not 0 <= o < offsets:
                        square[c, rows, lanes] = jnp.zeros((block, block), square.dtype)
                        continue
                    value = product[u * block : (u + 1) * block, lanes]
                    square[c, rows, lanes] = keep(
                        pattern[c * band_half + t, o] != 0, value
                    ).astype(square.dtype)
        for i in range(c - 1, c + 2):
            low, high = max(i, c) - 1, min(i, c) + 2
            left = z_dense[(i + 2) * tile : (i + 3) * tile, (low + 1) * tile : (high + 1) * tile]
            first = jnp.dot(
                left,
                d_dense[(low + 1) * tile : (high + 1) * tile, lanes_c],
                preferred_element_type=jnp.float32,
            )
            second = jnp.dot(
                left,
                square[c, (low - c + 1) * tile : (high - c + 1) * tile],
                preferred_element_type=jnp.float32,
            )
            for u in range(band_half):
                for t in range(band_half):
                    o = (i - c) * band_half + u - t + band_half
                    if not 0 <= o < offsets:
                        continue
                    part = (slice(u * block, (u + 1) * block), slice(t * block, (t + 1) * block))
                    base = z_dense[
                        (i + 2) * tile + u * block : (i + 2) * tile + (u + 1) * block,
                        (c + 1) * tile + t * block : (c + 1) * tile + (t + 1) * block,
                    ].astype(jnp.float32)
                    value = base + 0.5 * first[part] + 0.375 * second[part]
                    column = c * band_half + t
                    refined[column, o] = keep(pattern[column, o] != 0, value).astype(refined.dtype)


def refine_step(
    factor, pattern, near, far, cross, defect, near_defect, far_defect, gathered, quarter_len, entries
):
    columns, offsets, block, _ = factor.shape
    band_half = (offsets - 1) // 2
    tile = band_half * block
    count = columns // band_half
    kind = factor.dtype
    products = count * 21
    return pl.pallas_call(
        functools.partial(refine_kernel, quarter_len, entries),
        out_shape=(
            jax.ShapeDtypeStruct(factor.shape, kind),
            jax.ShapeDtypeStruct((1, block), jnp.float32),
        ),
        in_specs=[ANY, SMEM, ANY, ANY, ANY, ANY, ANY, ANY, VMEM],
        out_specs=(VMEM, VMEM),
        scratch_shapes=[
            pltpu.VMEM(factor.shape, kind),
            pltpu.VMEM((2,) + near.shape[1:], kind),
            pltpu.VMEM(cross.shape, kind),
            pltpu.VMEM(((count + 4) * tile, (count + 2) * tile), kind),
            pltpu.VMEM(((count + 2) * tile, (count + 2) * tile), kind),
            pltpu.VMEM((count, 3 * tile, tile), kind),
            pltpu.SemaphoreType.DMA((6 + count,)),
        ],
        compiler_params=pltpu.CompilerParams(vmem_limit_bytes=VMEM_LIMIT),
        cost_estimate=pl.CostEstimate(
            flops=products * 2 * tile**3, bytes_accessed=4 * 2**20, transcendentals=0
        ),
        name="refine",
    )(factor, pattern, near, far, cross, defect, near_defect, far_defect, gathered)


def swaps(pairs):
    return [pair for i, j in pairs for pair in ((i, j), (j, i))]


def per_device(margin, factor, pattern):
    columns, offsets, block, _ = margin.shape
    slabs = lax.axis_size("slab")
    devices = lax.axis_size("grp") * slabs
    quarter_len = columns * slabs
    near_pairs = [(i, i + 1) for i in range(0, devices - 1, 2)]
    far_pairs = [(i, i + 1) for i in range(1, devices - 1, 2)]
    inner_pairs = [(i, j) for i, j in far_pairs if j % slabs]
    cross_pairs = [(i, j) for i, j in far_pairs if not j % slabs]
    near, far, cross = pack(margin, factor, pattern, quarter_len)
    far = lax.ppermute(far, AXES, swaps(inner_pairs))
    cross = lax.ppermute(cross, AXES, swaps(cross_pairs))
    near = lax.ppermute(near, AXES, swaps(near_pairs))
    defect, near_defect, far_defect, spread = defect_step(
        margin, factor, pattern, near, far, cross, quarter_len, devices
    )
    far_defect = lax.ppermute(far_defect, AXES, swaps(far_pairs))
    near_defect = lax.ppermute(near_defect, AXES, swaps(near_pairs))
    gathered = lax.all_to_all(spread, AXES, 0, 0, tiled=True)
    refined, norm = refine_step(
        factor,
        pattern,
        near,
        far,
        cross,
        defect,
        near_defect,
        far_defect,
        gathered,
        quarter_len,
        columns * devices * block,
    )
    return refined, norm[0, 0]


def solution(mesh):
    return jax.shard_map(
        per_device,
        mesh=mesh,
        in_specs=(
            P(AXES, None, None, None),
            P(AXES, None, None, None),
            P(AXES, None),
        ),
        out_specs=(P(AXES, None, None, None), P()),
        check_vma=False,
    )
```

```python
import functools

import jax
import jax.numpy as jnp
from jax import lax
from jax.experimental import pallas as pl
from jax.experimental.pallas import tpu as pltpu
from jax.sharding import PartitionSpec as P


AXES = ("grp", "slab")
HBM = pl.BlockSpec(memory_space=pltpu.HBM)
VMEM = pl.BlockSpec(memory_space=pltpu.VMEM)
SMEM = pl.BlockSpec(memory_space=pltpu.SMEM)
PARAMS = pltpu.CompilerParams(vmem_limit_bytes=32 * 1024 * 1024)
FLAG_ROWS = 16


class Sizes:
    def __init__(self, shape, quarter_len, devices):
        self.columns, self.offsets, self.block, _ = shape
        self.half = (self.offsets - 1) // 2
        self.tile = self.half * self.block
        self.cells = self.half * self.offsets
        self.flag_blocks = -(-self.half * self.half * FLAG_ROWS // self.block)
        self.quarter_len = quarter_len
        self.devices = devices
        self.entries = self.columns * devices * self.block

    def cost(self, products, moved):
        return pl.CostEstimate(
            flops=products * 2 * self.tile**3, bytes_accessed=moved * 2**20, transcendentals=0
        )

    def tiles(self, count, dtype):
        return jax.ShapeDtypeStruct((count, self.tile, self.tile), dtype)


def odd_device():
    return lax.rem(lax.axis_index("slab"), 2)


def half_starts(z):
    near = jnp.where(odd_device() == 1, 0, z.columns - z.half)
    return near, z.columns - z.half - near


def keep(flag, value):
    return jnp.where(flag, value, jnp.zeros_like(value))


def dot(left, right):
    return jnp.dot(left, right, preferred_element_type=jnp.float32)


def chain_tile(true_tile):
    return jnp.where(odd_device() == 1, 2 - true_tile, true_tile)


def expand(z, out, read):
    block = z.block
    for t in range(z.half):
        for a in range(3 * z.half):
            o = a - t
            u = a % z.half
            if 0 <= o < z.offsets:
                value = read(t, o)
            else:
                value = jnp.zeros((block, block), out.dtype)
            out[
                chain_tile(a // z.half),
                u * block : (u + 1) * block,
                t * block : (t + 1) * block,
            ] = value


def offset_of(z, e, t, u):
    return jnp.where(odd_device() == 1, 1 - e, e - 1) * z.half + u - t + z.half


def flag_of(z, pattern, first, e, t, u):
    o = offset_of(z, e, t, u)
    inside = jnp.logical_and(o >= 0, o < z.offsets)
    return jnp.logical_and(inside, pattern[first + t, jnp.clip(o, 0, z.offsets - 1)] != 0)


def masked(z, value, flag):
    block = z.block
    rows = []
    for u in range(z.half):
        rows.append(
            jnp.concatenate(
                [
                    keep(
                        flag(t, u),
                        value[u * block : (u + 1) * block, t * block : (t + 1) * block],
                    )
                    for t in range(z.half)
                ],
                axis=1,
            )
        )
    return jnp.concatenate(rows, axis=0)


def own_masked(z, pattern, first, e, value):
    return masked(z, value, lambda t, u: flag_of(z, pattern, first, e, t, u))


def identity(z):
    shape = (z.tile, z.tile)
    rows = lax.broadcasted_iota(jnp.int32, shape, 0)
    return (rows == lax.broadcasted_iota(jnp.int32, shape, 1)).astype(jnp.float32)


def sum_squares(z, value):
    wide = value.astype(jnp.float32)
    return jnp.sum((wide * wide).reshape(-1, 8, z.tile), axis=0)


def store_half(z, pattern, first, tiles, cells):
    block = z.block
    for t in range(z.half):
        for o in range(z.offsets):
            a = t + o
            u = a % z.half
            value = tiles[
                chain_tile(a // z.half),
                u * block : (u + 1) * block,
                t * block : (t + 1) * block,
            ]
            cells[t, o] = keep(pattern[first + t, o] != 0, value).astype(cells.dtype)


def pack_kernel(z, margin, factor, pattern_in, near, far, cross, cells, pattern, sems):
    near_first, far_first = half_starts(z)
    first_row = lax.axis_index("slab") * z.columns
    fetch = pltpu.make_async_copy(pattern_in, pattern, sems.at[4])
    fetch.start()
    plan = ((margin, far_first), (factor, far_first), (margin, near_first), (factor, near_first))
    copies = [
        pltpu.make_async_copy(source.at[pl.ds(first, z.half)], cells.at[k], sems.at[k])
        for k, (source, first) in enumerate(plan)
    ]
    for copy in copies:
        copy.start()
    fetch.wait()
    for k, (source, first) in enumerate(plan):
        copies[k].wait()
        for t in range(z.half):
            for o in range(z.offsets):
                flag = pattern[first + t, o] != 0
                if k % 2:
                    row = first_row + first + t + o - z.half
                    inside = jnp.logical_and(row >= 0, row < z.quarter_len)
                    flag = jnp.logical_and(flag, inside)
                value = keep(flag, cells[k, t, o])
                cell = t * z.offsets + o
                u = cell % z.offsets + t - z.half
                if k == 0:
                    far[cell] = value
                    near[2 * z.cells + cell] = value
                elif k == 1:
                    far[z.cells + cell] = value
                    if 0 <= u < z.half:
                        cross[t, u] = value
                else:
                    near[(k - 2) * z.cells + cell] = value
    per_block = z.block // FLAG_ROWS
    for f in range(z.flag_blocks * per_block):
        t, u = f // z.half, f % z.half
        value = jnp.zeros((FLAG_ROWS, z.block), near.dtype)
        if t < z.half:
            value = keep(pattern[near_first + t, u - t + z.half] != 0, jnp.ones_like(value))
        low = f % per_block * FLAG_ROWS
        near[3 * z.cells + f // per_block, low : low + FLAG_ROWS] = value


def pack(z, margin, factor, pattern):
    kind = margin.dtype
    return pl.pallas_call(
        functools.partial(pack_kernel, z),
        out_shape=(
            jax.ShapeDtypeStruct((3 * z.cells + z.flag_blocks, z.block, z.block), kind),
            jax.ShapeDtypeStruct((2 * z.cells, z.block, z.block), kind),
            jax.ShapeDtypeStruct((z.half, z.half, z.block, z.block), kind),
        ),
        in_specs=[HBM, HBM, HBM],
        out_specs=(VMEM, VMEM, VMEM),
        scratch_shapes=[
            pltpu.VMEM((4, z.half, z.offsets, z.block, z.block), kind),
            pltpu.SMEM(pattern.shape, pattern.dtype),
            pltpu.SemaphoreType.DMA((5,)),
        ],
        compiler_params=PARAMS,
        name="pack",
    )(margin, factor, pattern)


def inner_kernel(
    z, pattern, near, far, beside, z_cols, turned, p_part, d_part, d_near, d_beside, squares,
    s_cols, z_turned, image,
):
    near_first, _ = half_starts(z)
    kind = near.dtype

    def cells_of(ref, base):
        return lambda t, o: ref[base + t * z.offsets + o]

    expand(z, s_cols.at[0], cells_of(far, 0))
    expand(z, s_cols.at[1], cells_of(near, 0))
    expand(z, s_cols.at[2], cells_of(beside, 0))
    expand(z, s_cols.at[3], cells_of(beside, 2 * z.cells))
    expand(z, z_cols.at[0], cells_of(far, z.cells))
    expand(z, z_cols.at[1], cells_of(near, z.cells))
    expand(z, z_cols.at[2], cells_of(beside, z.cells))
    for x in range(3):
        for e in range(3):
            z_turned[x, e] = z_cols[x, e].T
    turned[0] = z_turned[0, 0]
    turned[1] = z_turned[0, 1]
    turned[2] = z_turned[1, 0]

    def image_tile(y, c):
        total = None
        for inner in range(max(c - 1, y - 1, 1), min(c + 1, y + 1) + 1):
            term = dot(s_cols[inner - 1, y - inner + 1], z_cols[c - 1, inner - c + 1])
            total = term if total is None else total + term
        return total

    def turned_sum(i, c, rows):
        total = None
        for m in rows:
            term = dot(z_turned[i - 1, m - i + 1], image[c - 1, m])
            total = term if total is None else total + term
        return total

    p_part[0] = image_tile(0, 1)
    p_part[1] = image_tile(1, 1)
    for c, rows in ((1, (2, 3)), (2, (0, 1, 2, 3, 4)), (3, (1, 2, 3, 4))):
        for y in rows:
            image[c - 1, y] = image_tile(y, c).astype(kind)
    d_part[0] = turned_sum(1, 1, (2,))
    d_part[1] = turned_sum(2, 1, (2, 3))
    eye = identity(z)
    total = jnp.zeros((8, z.tile), jnp.float32)
    for i in (1, 2, 3):
        value = -turned_sum(i, 2, (i - 1, i, i + 1))
        if i == 2:
            value = eye + value
        value = own_masked(z, pattern, near_first, i - 1, value).astype(kind)
        d_near[i - 1] = value
        total = total + sum_squares(z, value)
    squares[...] = total

    def side_flag(t, u):
        o = offset_of(z, 0, t, u)
        inside = jnp.logical_and(o >= 0, o < z.offsets)
        back = jnp.clip(z.offsets - 1 - o, 0, z.offsets - 1)
        return jnp.logical_and(inside, pattern[near_first + u, back] != 0)

    d_beside[0] = masked(z, -turned_sum(2, 3, (1, 2, 3)), side_flag).astype(kind)
    value = eye - turned_sum(3, 3, (2, 3, 4))
    block = z.block
    per_block = block // FLAG_ROWS
    for t in range(z.half):
        for u in range(z.half):
            f = t * z.half + u
            low = f % per_block * FLAG_ROWS
            flags = beside[3 * z.cells + f // per_block, low : low + FLAG_ROWS]
            flag = flags.astype(jnp.float32)[:1]
            part = (slice(u * block, (u + 1) * block), slice(t * block, (t + 1) * block))
            d_beside[1, part[0], part[1]] = (value[part] * flag).astype(kind)


def inner_step(z, pattern, near, far, beside):
    kind = near.dtype
    tile = z.tile
    return pl.pallas_call(
        functools.partial(inner_kernel, z),
        out_shape=(
            jax.ShapeDtypeStruct((3, 3, tile, tile), kind),
            z.tiles(3, kind),
            z.tiles(2, jnp.float32),
            z.tiles(2, jnp.float32),
            z.tiles(3, kind),
            z.tiles(2, kind),
            jax.ShapeDtypeStruct((8, tile), jnp.float32),
        ),
        in_specs=[SMEM, VMEM, VMEM, VMEM],
        out_specs=(VMEM,) * 7,
        scratch_shapes=[
            pltpu.VMEM((4, 3, tile, tile), kind),
            pltpu.VMEM((3, 3, tile, tile), kind),
            pltpu.VMEM((3, 5, tile, tile), kind),
        ],
        compiler_params=PARAMS,
        cost_estimate=z.cost(42, 8),
        name="inner",
    )(pattern, near, far, beside)


def outer_kernel(
    z, pattern, far, cross, z_cols, turned, p_part, d_part, squares, d_far, d_out, z_far, spread, s_far
):
    _, far_first = half_starts(z)
    kind = far.dtype

    def factor_cell(t, o):
        value = far[z.cells + t * z.offsets + o]
        u = o + t - z.half
        if 0 <= u < z.half:
            value = value + cross[t, u]
        return value

    expand(z, s_far, lambda t, o: far[t * z.offsets + o])
    expand(z, z_far, factor_cell)
    link = z_cols[0, 0]
    image = (
        dot(s_far[0], link).astype(kind),
        (dot(s_far[1], link) + p_part[0]).astype(kind),
        (dot(s_far[2], link) + p_part[1]).astype(kind),
    )
    values = (
        -(dot(z_far[0].T, image[0]) + dot(z_far[1].T, image[1]) + dot(z_far[2].T, image[2])),
        identity(z) - (dot(turned[0], image[1]) + dot(turned[1], image[2]) + d_part[0]),
        -(dot(turned[2], image[2]) + d_part[1]),
    )
    total = squares[...]
    for e, value in enumerate(values):
        value = own_masked(z, pattern, far_first, e, value).astype(kind)
        d_far[e] = value
        if e < 2:
            d_out[e] = value
        total = total + sum_squares(z, value)
    lanes = jnp.sum(total, axis=0, keepdims=True)
    folded = lanes[:, : z.block]
    for t in range(1, z.half):
        folded = folded + lanes[:, t * z.block : (t + 1) * z.block]
    spread[...] = jnp.broadcast_to(folded[None], spread.shape)


def outer_step(z, pattern, far, cross, z_cols, turned, p_part, d_part, squares):
    kind = far.dtype
    return pl.pallas_call(
        functools.partial(outer_kernel, z),
        out_shape=(
            z.tiles(3, kind),
            z.tiles(2, kind),
            z.tiles(3, kind),
            jax.ShapeDtypeStruct((z.devices, 1, z.block), jnp.float32),
        ),
        in_specs=[SMEM] + [VMEM] * 7,
        out_specs=(VMEM,) * 4,
        scratch_shapes=[pltpu.VMEM((3, z.tile, z.tile), kind)],
        compiler_params=PARAMS,
        cost_estimate=z.cost(9, 4),
        name="outer",
    )(pattern, far, cross, z_cols, turned, p_part, d_part, squares)


def middle_kernel(
    z, pattern, z_cols, z_far, d_far, d_near, d_beside, refined, base, e_part, square, tiles, cells, sem
):
    near_first, far_first = half_starts(z)
    factor = (z_far, z_cols.at[0], z_cols.at[1], z_cols.at[2])
    defect = (None, d_far, d_near, d_beside)

    def product(left, i, c, right, first=0):
        total = None
        for k in range(max(first, i - 1, c - 1), min(i + 1, c + 1) + 1):
            term = dot(left[k][i - k + 1], right[k - c + 1])
            total = term if total is None else total + term
        return total

    for i in (1, 2, 3):
        value = product(defect, i, 2, d_near, 1)
        square[i - 1] = own_masked(z, pattern, near_first, i - 1, value).astype(square.dtype)
    for i in (1, 2, 3):
        tiles[i - 1] = (
            z_cols[1, i - 1].astype(jnp.float32)
            + 0.5 * product(factor, i, 2, d_near)
            + 0.375 * product(factor, i, 2, square)
        )
    store_half(z, pattern, near_first, tiles, cells)
    copy = pltpu.make_async_copy(cells, refined.at[pl.ds(near_first, z.half)], sem)
    copy.start()
    for i in (0, 1, 2):
        base[i] = z_cols[0, i].astype(jnp.float32) + 0.5 * product(factor, i, 1, d_far)
        e_part[i] = product(defect, i, 1, d_far, 1)
    copy.wait()


def middle_step(z, pattern, z_cols, z_far, d_far, d_near, d_beside):
    kind = z_far.dtype
    shape = (z.columns, z.offsets, z.block, z.block)
    return pl.pallas_call(
        functools.partial(middle_kernel, z),
        out_shape=(
            jax.ShapeDtypeStruct(shape, kind),
            z.tiles(3, jnp.float32),
            z.tiles(3, jnp.float32),
        ),
        in_specs=[SMEM] + [VMEM] * 5,
        out_specs=(HBM, VMEM, VMEM),
        scratch_shapes=[
            pltpu.VMEM((3, z.tile, z.tile), kind),
            pltpu.VMEM((3, z.tile, z.tile), jnp.float32),
            pltpu.VMEM((z.half,) + shape[1:], kind),
            pltpu.SemaphoreType.DMA(()),
        ],
        compiler_params=PARAMS,
        cost_estimate=z.cost(33, 6),
        name="middle",
    )(pattern, z_cols, z_far, d_far, d_near, d_beside)


def last_kernel(
    z, pattern, z_cols, z_far, d_far, d_in, base, e_part, gathered, _, refined, norm, square, tiles, cells,
    sem,
):
    _, far_first = half_starts(z)
    factor = (z_far, z_cols.at[0], z_cols.at[1])
    values = (
        e_part[0] + dot(d_in[1], d_far[0]),
        e_part[1] + dot(d_in[0], d_far[0]),
        e_part[2],
    )
    for i, value in enumerate(values):
        square[i] = own_masked(z, pattern, far_first, i, value).astype(square.dtype)
    for i in (0, 1, 2):
        total = None
        for k in range(max(0, i - 1), min(2, i + 1) + 1):
            term = dot(factor[k][i - k + 1], square[k])
            total = term if total is None else total + term
        tiles[i] = base[i] + 0.375 * total
    store_half(z, pattern, far_first, tiles, cells)
    copy = pltpu.make_async_copy(cells, refined.at[pl.ds(far_first, z.half)], sem)
    copy.start()
    mean = jnp.sum(gathered[...]) * (1.0 / z.entries)
    norm[...] = jnp.sqrt(jnp.full(norm.shape, mean, jnp.float32))
    copy.wait()


def last_step(z, pattern, z_cols, z_far, d_far, d_in, base, e_part, gathered, refined):
    kind = refined.dtype
    return pl.pallas_call(
        functools.partial(last_kernel, z),
        out_shape=(
            jax.ShapeDtypeStruct(refined.shape, kind),
            jax.ShapeDtypeStruct((1, z.block), jnp.float32),
        ),
        in_specs=[SMEM] + [VMEM] * 7 + [HBM],
        out_specs=(HBM, VMEM),
        scratch_shapes=[
            pltpu.VMEM((3, z.tile, z.tile), kind),
            pltpu.VMEM((3, z.tile, z.tile), jnp.float32),
            pltpu.VMEM((z.half,) + refined.shape[1:], kind),
            pltpu.SemaphoreType.DMA(()),
        ],
        input_output_aliases={8: 0},
        compiler_params=PARAMS,
        cost_estimate=z.cost(9, 4),
        name="last",
    )(pattern, z_cols, z_far, d_far, d_in, base, e_part, gathered, refined)


def swaps(pairs):
    return [pair for i, j in pairs for pair in ((i, j), (j, i))]


def per_device(margin, factor, pattern):
    slabs = lax.axis_size("slab")
    devices = lax.axis_size("grp") * slabs
    z = Sizes(margin.shape, margin.shape[0] * slabs, devices)
    if slabs % 2 or z.columns != 2 * z.half:
        raise ValueError("sizes")
    near_pairs = [(i, i + 1) for i in range(0, devices - 1, 2)]
    far_pairs = [(i, i + 1) for i in range(1, devices - 1, 2)]
    inner_pairs = [(i, j) for i, j in far_pairs if j % slabs]
    cross_pairs = [(i, j) for i, j in far_pairs if not j % slabs]
    near, far, cross = pack(z, margin, factor, pattern)
    beyond = lax.ppermute(far, AXES, swaps(inner_pairs))
    across = lax.ppermute(cross, AXES, swaps(cross_pairs))
    beside = lax.ppermute(near, AXES, swaps(near_pairs))
    z_cols, turned, p_part, d_part, d_near, d_beside, squares = inner_step(
        z, pattern, near, far, beside
    )
    d_far, d_out, z_far, spread = outer_step(
        z, pattern, beyond, across, z_cols, turned, p_part, d_part, squares
    )
    d_in = lax.ppermute(d_out, AXES, swaps(far_pairs))
    gathered = lax.all_to_all(spread, AXES, 0, 0, tiled=True)
    refined, base, e_part = middle_step(z, pattern, z_cols, z_far, d_far, d_near, d_beside)
    refined, norm = last_step(
        z, pattern, z_cols, z_far, d_far, d_in, base, e_part, gathered, refined
    )
    return refined, norm[0, 0]


def solution(mesh):
    return jax.shard_map(
        per_device,
        mesh=mesh,
        in_specs=(
            P(AXES, None, None, None),
            P(AXES, None, None, None),
            P(AXES, None),
        ),
        out_specs=(P(AXES, None, None, None), P()),
        check_vma=False,
    )
```

```python
import functools

import jax
import jax.numpy as jnp
from jax import lax
from jax.experimental import pallas as pl
from jax.experimental.pallas import tpu as pltpu
from jax.sharding import PartitionSpec as P


AXES = ("grp", "slab")
HBM = pl.BlockSpec(memory_space=pltpu.HBM)
VMEM = pl.BlockSpec(memory_space=pltpu.VMEM)
SMEM = pl.BlockSpec(memory_space=pltpu.SMEM)
PARAMS = pltpu.CompilerParams(vmem_limit_bytes=32 * 1024 * 1024)
FLAG_ROWS = 16


class Sizes:
    def __init__(self, shape, quarter_len, devices):
        self.columns, self.offsets, self.block, _ = shape
        self.half = (self.offsets - 1) // 2
        self.tile = self.half * self.block
        self.cells = self.half * self.offsets
        self.flag_blocks = -(-self.half * self.half * FLAG_ROWS // self.block)
        self.quarter_len = quarter_len
        self.devices = devices
        self.entries = self.columns * devices * self.block

    def cost(self, products, moved):
        return pl.CostEstimate(
            flops=products * 2 * self.tile**3, bytes_accessed=moved * 2**20, transcendentals=0
        )

    def tiles(self, count, dtype):
        return jax.ShapeDtypeStruct((count, self.tile, self.tile), dtype)


def odd_device():
    return lax.rem(lax.axis_index("slab"), 2)


def half_starts(z):
    near = jnp.where(odd_device() == 1, 0, z.columns - z.half)
    return near, z.columns - z.half - near


def keep(flag, value):
    return jnp.where(flag, value, jnp.zeros_like(value))


def dot(left, right):
    return jnp.dot(left, right, preferred_element_type=jnp.float32)


def chain_tile(true_tile):
    return jnp.where(odd_device() == 1, 2 - true_tile, true_tile)


def expand(z, out, read):
    block = z.block
    for t in range(z.half):
        for a in range(3 * z.half):
            o = a - t
            u = a % z.half
            if 0 <= o < z.offsets:
                value = read(t, o)
            else:
                value = jnp.zeros((block, block), out.dtype)
            out[
                chain_tile(a // z.half),
                u * block : (u + 1) * block,
                t * block : (t + 1) * block,
            ] = value


def offset_of(z, e, t, u):
    return jnp.where(odd_device() == 1, 1 - e, e - 1) * z.half + u - t + z.half


def flag_of(z, pattern, first, e, t, u):
    o = offset_of(z, e, t, u)
    inside = jnp.logical_and(o >= 0, o < z.offsets)
    return jnp.logical_and(inside, pattern[first + t, jnp.clip(o, 0, z.offsets - 1)] != 0)


def masked(z, value, flag):
    block = z.block
    rows = []
    for u in range(z.half):
        rows.append(
            jnp.concatenate(
                [
                    keep(
                        flag(t, u),
                        value[u * block : (u + 1) * block, t * block : (t + 1) * block],
                    )
                    for t in range(z.half)
                ],
                axis=1,
            )
        )
    return jnp.concatenate(rows, axis=0)


def own_masked(z, pattern, first, e, value):
    return masked(z, value, lambda t, u: flag_of(z, pattern, first, e, t, u))


def identity(z):
    shape = (z.tile, z.tile)
    rows = lax.broadcasted_iota(jnp.int32, shape, 0)
    return (rows == lax.broadcasted_iota(jnp.int32, shape, 1)).astype(jnp.float32)


def tile_product(left, right, i, c, low, high):
    total = None
    for k in range(max(low, i - 1, c - 1), min(high, i + 1, c + 1) + 1):
        term = dot(left[k][i - k + 1], right[k - c + 1])
        total = term if total is None else total + term
    return total


def sum_squares(z, value):
    wide = value.astype(jnp.float32)
    return jnp.sum((wide * wide).reshape(-1, 8, z.tile), axis=0)


def store_half(z, tiles, cells):
    block = z.block
    for t in range(z.half):
        for o in range(z.offsets):
            a = t + o
            u = a % z.half
            value = tiles[
                chain_tile(a // z.half),
                u * block : (u + 1) * block,
                t * block : (t + 1) * block,
            ]
            cells[t, o] = value.astype(cells.dtype)


def mask_kernel(z, pattern, mask_near, mask_far):
    ones = jnp.ones((z.tile, z.tile), jnp.float32)
    for out, first in zip((mask_near, mask_far), half_starts(z)):
        for e in range(3):
            out[e] = own_masked(z, pattern, first, e, ones).astype(out.dtype)


def masks(z, pattern, kind):
    return pl.pallas_call(
        functools.partial(mask_kernel, z),
        out_shape=(z.tiles(3, kind), z.tiles(3, kind)),
        in_specs=[SMEM],
        out_specs=(VMEM, VMEM),
        compiler_params=PARAMS,
        cost_estimate=z.cost(20, 1),
        name="masks",
    )(pattern)


def pack_kernel(z, margin, factor, pattern, _near, _far, near, far, cross):
    near_first, far_first = half_starts(z)
    first_row = lax.axis_index("slab") * z.columns
    plan = ((margin, far_first), (factor, far_first), (margin, near_first), (factor, near_first))
    for k, (source, first) in enumerate(plan):
        for t in range(z.half):
            for o in range(z.offsets):
                flag = pattern[first + t, o] != 0
                if k % 2:
                    row = first_row + first + t + o - z.half
                    inside = jnp.logical_and(row >= 0, row < z.quarter_len)
                    flag = jnp.logical_and(flag, inside)
                value = keep(flag, source[first + t, o])
                cell = t * z.offsets + o
                u = o + t - z.half
                if k == 0:
                    far[cell] = value
                    near[2 * z.cells + cell] = value
                elif k == 1:
                    far[z.cells + cell] = value
                    if 0 <= u < z.half:
                        cross[t, u] = value
                else:
                    near[(k - 2) * z.cells + cell] = value
    per_block = z.block // FLAG_ROWS
    for f in range(z.flag_blocks * per_block):
        t, u = f // z.half, f % z.half
        value = jnp.zeros((FLAG_ROWS, z.block), near.dtype)
        if t < z.half:
            value = keep(pattern[near_first + t, u - t + z.half] != 0, jnp.ones_like(value))
        low = f % per_block * FLAG_ROWS
        near[3 * z.cells + f // per_block, low : low + FLAG_ROWS] = value


def pack(z, margin, factor, pattern, mask_near, mask_far):
    kind = margin.dtype
    return pl.pallas_call(
        functools.partial(pack_kernel, z),
        out_shape=(
            jax.ShapeDtypeStruct((3 * z.cells + z.flag_blocks, z.block, z.block), kind),
            jax.ShapeDtypeStruct((2 * z.cells, z.block, z.block), kind),
            jax.ShapeDtypeStruct((z.half, z.half, z.block, z.block), kind),
        ),
        in_specs=[VMEM, VMEM, SMEM, VMEM, VMEM],
        out_specs=(VMEM, VMEM, VMEM),
        compiler_params=PARAMS,
        name="pack",
    )(margin, factor, pattern, mask_near, mask_far)


def inner_kernel(
    z, pattern, near, far, beside, z_cols, turned, p_part, d_part, d_near, squares, base_near, e_near,
    s_cols, z_turned, image, d_beside,
):
    near_first, _ = half_starts(z)
    kind = near.dtype

    def cells_of(ref, base):
        return lambda t, o: ref[base + t * z.offsets + o]

    expand(z, s_cols.at[0], cells_of(far, 0))
    expand(z, s_cols.at[1], cells_of(near, 0))
    expand(z, s_cols.at[2], cells_of(beside, 0))
    expand(z, s_cols.at[3], cells_of(beside, 2 * z.cells))
    expand(z, z_cols.at[0], cells_of(far, z.cells))
    expand(z, z_cols.at[1], cells_of(near, z.cells))
    expand(z, z_cols.at[2], cells_of(beside, z.cells))
    for x in range(3):
        for e in range(3):
            z_turned[x, e] = z_cols[x, e].T
    turned[0] = z_turned[0, 0]
    turned[1] = z_turned[0, 1]
    turned[2] = z_turned[1, 0]

    def image_tile(y, c):
        total = None
        for inner in range(max(c - 1, y - 1, 1), min(c + 1, y + 1) + 1):
            term = dot(s_cols[inner - 1, y - inner + 1], z_cols[c - 1, inner - c + 1])
            total = term if total is None else total + term
        return total

    def turned_sum(i, c, rows):
        total = None
        for m in rows:
            term = dot(z_turned[i - 1, m - i + 1], image[c - 1, m])
            total = term if total is None else total + term
        return total

    p_part[0] = image_tile(0, 1)
    p_part[1] = image_tile(1, 1)
    for c, rows in ((1, (2, 3)), (2, (0, 1, 2, 3, 4)), (3, (1, 2, 3, 4))):
        for y in rows:
            image[c - 1, y] = image_tile(y, c).astype(kind)
    d_part[0] = turned_sum(1, 1, (2,))
    d_part[1] = turned_sum(2, 1, (2, 3))
    eye = identity(z)
    total = jnp.zeros((8, z.tile), jnp.float32)
    for i in (1, 2, 3):
        value = -turned_sum(i, 2, (i - 1, i, i + 1))
        if i == 2:
            value = eye + value
        value = own_masked(z, pattern, near_first, i - 1, value).astype(kind)
        d_near[i - 1] = value
        total = total + sum_squares(z, value)
    squares[...] = total

    def side_flag(t, u):
        o = offset_of(z, 0, t, u)
        inside = jnp.logical_and(o >= 0, o < z.offsets)
        back = jnp.clip(z.offsets - 1 - o, 0, z.offsets - 1)
        return jnp.logical_and(inside, pattern[near_first + u, back] != 0)

    d_beside[0] = masked(z, -turned_sum(2, 3, (1, 2, 3)), side_flag).astype(kind)
    value = eye - turned_sum(3, 3, (2, 3, 4))
    block = z.block
    per_block = block // FLAG_ROWS
    for t in range(z.half):
        for u in range(z.half):
            f = t * z.half + u
            low = f % per_block * FLAG_ROWS
            flags = beside[3 * z.cells + f // per_block, low : low + FLAG_ROWS]
            flag = flags.astype(jnp.float32)[:1]
            part = (slice(u * block, (u + 1) * block), slice(t * block, (t + 1) * block))
            d_beside[1, part[0], part[1]] = (value[part] * flag).astype(kind)

    factor = (None, z_cols.at[0], z_cols.at[1], z_cols.at[2])
    defect = (None, None, d_near, d_beside)
    for i in (1, 2, 3):
        base_near[i - 1] = z_cols[1, i - 1].astype(jnp.float32) + 0.5 * tile_product(
            factor, d_near, i, 2, 1, 3
        )
        e_near[i - 1] = tile_product(defect, d_near, i, 2, 2, 3)


def inner_step(z, pattern, near, far, beside):
    kind = near.dtype
    tile = z.tile
    return pl.pallas_call(
        functools.partial(inner_kernel, z),
        out_shape=(
            jax.ShapeDtypeStruct((3, 3, tile, tile), kind),
            z.tiles(3, kind),
            z.tiles(2, jnp.float32),
            z.tiles(2, jnp.float32),
            z.tiles(3, kind),
            jax.ShapeDtypeStruct((8, tile), jnp.float32),
            z.tiles(3, jnp.float32),
            z.tiles(3, jnp.float32),
        ),
        in_specs=[SMEM, VMEM, VMEM, VMEM],
        out_specs=(VMEM,) * 8,
        scratch_shapes=[
            pltpu.VMEM((4, 3, tile, tile), kind),
            pltpu.VMEM((3, 3, tile, tile), kind),
            pltpu.VMEM((3, 5, tile, tile), kind),
            pltpu.VMEM((2, tile, tile), kind),
        ],
        compiler_params=PARAMS,
        cost_estimate=z.cost(54, 8),
        name="inner",
    )(pattern, near, far, beside)


def outer_kernel(
    z, pattern, far, cross, z_cols, turned, p_part, d_part, squares, *refs
):
    d_far, d_out, z_far, spread, s_far = refs[-5:]
    _, far_first = half_starts(z)
    kind = far.dtype

    def factor_cell(t, o):
        value = far[z.cells + t * z.offsets + o]
        u = o + t - z.half
        if 0 <= u < z.half:
            value = value + cross[t, u]
        return value

    expand(z, s_far, lambda t, o: far[t * z.offsets + o])
    expand(z, z_far, factor_cell)
    link = z_cols[0, 0]
    image = (
        dot(s_far[0], link).astype(kind),
        (dot(s_far[1], link) + p_part[0]).astype(kind),
        (dot(s_far[2], link) + p_part[1]).astype(kind),
    )
    values = (
        -(dot(z_far[0].T, image[0]) + dot(z_far[1].T, image[1]) + dot(z_far[2].T, image[2])),
        identity(z) - (dot(turned[0], image[1]) + dot(turned[1], image[2]) + d_part[0]),
        -(dot(turned[2], image[2]) + d_part[1]),
    )
    total = squares[...]
    for e, value in enumerate(values):
        value = own_masked(z, pattern, far_first, e, value).astype(kind)
        d_far[e] = value
        if e < 2:
            d_out[e] = value
        total = total + sum_squares(z, value)
    lanes = jnp.sum(total, axis=0, keepdims=True)
    folded = lanes[:, : z.block]
    for t in range(1, z.half):
        folded = folded + lanes[:, t * z.block : (t + 1) * z.block]
    spread[...] = jnp.broadcast_to(folded[None], spread.shape)


def outer_step(z, pattern, far, cross, z_cols, turned, p_part, d_part, squares, held):
    kind = far.dtype
    return pl.pallas_call(
        functools.partial(outer_kernel, z),
        out_shape=(
            z.tiles(3, kind),
            z.tiles(2, kind),
            z.tiles(3, kind),
            jax.ShapeDtypeStruct((z.devices, 1, z.block), jnp.float32),
        ),
        in_specs=[SMEM] + [VMEM] * (7 + len(held)),
        out_specs=(VMEM,) * 4,
        scratch_shapes=[pltpu.VMEM((3, z.tile, z.tile), kind)],
        compiler_params=PARAMS,
        cost_estimate=z.cost(9, 4),
        name="outer",
    )(pattern, far, cross, z_cols, turned, p_part, d_part, squares, *held)


def middle_kernel(
    z, z_cols, z_far, d_far, d_near, base_near, e_near, mask_near, refined, base, e_part, square, tiles,
    cells, sem,
):
    near_first, _ = half_starts(z)
    factor = (z_far, z_cols.at[0], z_cols.at[1], z_cols.at[2])
    defect = (None, d_far, d_near)
    for i in (1, 2, 3):
        value = e_near[i - 1]
        if i < 3:
            value = value + dot(d_far[i], d_near[0])
        square[i - 1] = (value * mask_near[i - 1].astype(jnp.float32)).astype(square.dtype)
    for i in (1, 2, 3):
        value = base_near[i - 1] + 0.375 * tile_product(factor, square, i, 2, 1, 3)
        tiles[i - 1] = value * mask_near[i - 1].astype(jnp.float32)
    store_half(z, tiles, cells)
    copy = pltpu.make_async_copy(cells, refined.at[pl.ds(near_first, z.half)], sem)
    copy.start()
    for i in (0, 1, 2):
        base[i] = z_cols[0, i].astype(jnp.float32) + 0.5 * tile_product(factor, d_far, i, 1, 0, 2)
        e_part[i] = tile_product(defect, d_far, i, 1, 1, 2)
    copy.wait()


def middle_step(z, z_cols, z_far, d_far, d_near, base_near, e_near, mask_near):
    kind = z_far.dtype
    shape = (z.columns, z.offsets, z.block, z.block)
    return pl.pallas_call(
        functools.partial(middle_kernel, z),
        out_shape=(
            jax.ShapeDtypeStruct(shape, kind),
            z.tiles(3, jnp.float32),
            z.tiles(3, jnp.float32),
        ),
        in_specs=[VMEM] * 7,
        out_specs=(HBM, VMEM, VMEM),
        scratch_shapes=[
            pltpu.VMEM((3, z.tile, z.tile), kind),
            pltpu.VMEM((3, z.tile, z.tile), jnp.float32),
            pltpu.VMEM((z.half,) + shape[1:], kind),
            pltpu.SemaphoreType.DMA(()),
        ],
        compiler_params=PARAMS,
        cost_estimate=z.cost(21, 6),
        name="middle",
    )(z_cols, z_far, d_far, d_near, base_near, e_near, mask_near)


def last_kernel(
    z, z_cols, z_far, d_far, d_in, base, e_part, mask_far, gathered, _, refined, norm, square, tiles,
    cells, sem,
):
    _, far_first = half_starts(z)
    factor = (z_far, z_cols.at[0], z_cols.at[1])
    values = (
        e_part[0] + dot(d_in[1], d_far[0]),
        e_part[1] + dot(d_in[0], d_far[0]),
        e_part[2],
    )
    for i, value in enumerate(values):
        square[i] = (value * mask_far[i].astype(jnp.float32)).astype(square.dtype)
    for i in (0, 1, 2):
        value = base[i] + 0.375 * tile_product(factor, square, i, 1, 0, 2)
        tiles[i] = value * mask_far[i].astype(jnp.float32)
    store_half(z, tiles, cells)
    copy = pltpu.make_async_copy(cells, refined.at[pl.ds(far_first, z.half)], sem)
    copy.start()
    mean = jnp.sum(gathered[...]) * (1.0 / z.entries)
    norm[...] = jnp.sqrt(jnp.full(norm.shape, mean, jnp.float32))
    copy.wait()


def last_step(z, z_cols, z_far, d_far, d_in, base, e_part, mask_far, gathered, refined):
    kind = refined.dtype
    return pl.pallas_call(
        functools.partial(last_kernel, z),
        out_shape=(
            jax.ShapeDtypeStruct(refined.shape, kind),
            jax.ShapeDtypeStruct((1, z.block), jnp.float32),
        ),
        in_specs=[VMEM] * 8 + [HBM],
        out_specs=(HBM, VMEM),
        scratch_shapes=[
            pltpu.VMEM((3, z.tile, z.tile), kind),
            pltpu.VMEM((3, z.tile, z.tile), jnp.float32),
            pltpu.VMEM((z.half,) + refined.shape[1:], kind),
            pltpu.SemaphoreType.DMA(()),
        ],
        input_output_aliases={8: 0},
        compiler_params=PARAMS,
        cost_estimate=z.cost(9, 4),
        name="last",
    )(z_cols, z_far, d_far, d_in, base, e_part, mask_far, gathered, refined)


def swaps(pairs):
    return [pair for i, j in pairs for pair in ((i, j), (j, i))]


def per_device(margin, factor, pattern):
    slabs = lax.axis_size("slab")
    devices = lax.axis_size("grp") * slabs
    z = Sizes(margin.shape, margin.shape[0] * slabs, devices)
    if slabs % 2 or z.columns != 2 * z.half:
        raise ValueError("sizes")
    near_pairs = [(i, i + 1) for i in range(0, devices - 1, 2)]
    far_pairs = [(i, i + 1) for i in range(1, devices - 1, 2)]
    inner_pairs = [(i, j) for i, j in far_pairs if j % slabs]
    cross_pairs = [(i, j) for i, j in far_pairs if not j % slabs]
    mask_near, mask_far = masks(z, pattern, margin.dtype)
    near, far, cross = pack(z, margin, factor, pattern, mask_near, mask_far)
    beyond = lax.ppermute(far, AXES, swaps(inner_pairs))
    across = lax.ppermute(cross, AXES, swaps(cross_pairs))
    beside = lax.ppermute(near, AXES, swaps(near_pairs))
    z_cols, turned, p_part, d_part, d_near, squares, base_near, e_near = inner_step(
        z, pattern, near, far, beside
    )
    held = (d_near, base_near, e_near, mask_near, mask_far)
    d_far, d_out, z_far, spread = outer_step(
        z, pattern, beyond, across, z_cols, turned, p_part, d_part, squares, held
    )
    d_in = lax.ppermute(d_out, AXES, swaps(far_pairs))
    gathered = lax.all_to_all(spread, AXES, 0, 0, tiled=True)
    refined, base, e_part = middle_step(
        z, z_cols, z_far, d_far, d_near, base_near, e_near, mask_near
    )
    refined, norm = last_step(
        z, z_cols, z_far, d_far, d_in, base, e_part, mask_far, gathered, refined
    )
    return refined, norm[0, 0]


def solution(mesh):
    return jax.shard_map(
        per_device,
        mesh=mesh,
        in_specs=(
            P(AXES, None, None, None),
            P(AXES, None, None, None),
            P(AXES, None),
        ),
        out_specs=(P(AXES, None, None, None), P()),
        check_vma=False,
    )
```

```python
import functools

import jax
import jax.numpy as jnp
from jax import lax
from jax.experimental import pallas as pl
from jax.experimental.pallas import tpu as pltpu
from jax.sharding import PartitionSpec as P


AXES = ("grp", "slab")
HBM = pl.BlockSpec(memory_space=pltpu.HBM)
VMEM = pl.BlockSpec(memory_space=pltpu.VMEM)
SMEM = pl.BlockSpec(memory_space=pltpu.SMEM)
PARAMS = pltpu.CompilerParams(vmem_limit_bytes=32 * 1024 * 1024)
FLAG_ROWS = 16


class Sizes:
    def __init__(self, shape, quarter_len, devices):
        self.columns, self.offsets, self.block, _ = shape
        self.half = (self.offsets - 1) // 2
        self.tile = self.half * self.block
        self.cells = self.half * self.offsets
        self.flag_blocks = -(-self.half * self.half * FLAG_ROWS // self.block)
        self.quarter_len = quarter_len
        self.devices = devices
        self.entries = self.columns * devices * self.block

    def cost(self, products, moved):
        return pl.CostEstimate(
            flops=products * 2 * self.tile**3, bytes_accessed=moved * 2**20, transcendentals=0
        )

    def tiles(self, count, dtype):
        return jax.ShapeDtypeStruct((count, self.tile, self.tile), dtype)


def odd_device():
    return lax.rem(lax.axis_index("slab"), 2)


def half_starts(z):
    near = jnp.where(odd_device() == 1, 0, z.columns - z.half)
    return near, z.columns - z.half - near


def keep(flag, value):
    return jnp.where(flag, value, jnp.zeros_like(value))


def dot(left, right):
    return jnp.dot(left, right, preferred_element_type=jnp.float32)


def chain_tile(true_tile):
    return jnp.where(odd_device() == 1, 2 - true_tile, true_tile)


def expand(z, out, read):
    block = z.block
    for t in range(z.half):
        for a in range(3 * z.half):
            o = a - t
            u = a % z.half
            if 0 <= o < z.offsets:
                value = read(t, o)
            else:
                value = jnp.zeros((block, block), out.dtype)
            out[
                chain_tile(a // z.half),
                u * block : (u + 1) * block,
                t * block : (t + 1) * block,
            ] = value


def offset_of(z, e, t, u):
    return jnp.where(odd_device() == 1, 1 - e, e - 1) * z.half + u - t + z.half


def flag_of(z, pattern, first, e, t, u):
    o = offset_of(z, e, t, u)
    inside = jnp.logical_and(o >= 0, o < z.offsets)
    return jnp.logical_and(inside, pattern[first + t, jnp.clip(o, 0, z.offsets - 1)] != 0)


def masked(z, value, flag):
    block = z.block
    rows = []
    for u in range(z.half):
        rows.append(
            jnp.concatenate(
                [
                    keep(
                        flag(t, u),
                        value[u * block : (u + 1) * block, t * block : (t + 1) * block],
                    )
                    for t in range(z.half)
                ],
                axis=1,
            )
        )
    return jnp.concatenate(rows, axis=0)


def own_masked(z, pattern, first, e, value):
    return masked(z, value, lambda t, u: flag_of(z, pattern, first, e, t, u))


def identity(z):
    shape = (z.tile, z.tile)
    rows = lax.broadcasted_iota(jnp.int32, shape, 0)
    return (rows == lax.broadcasted_iota(jnp.int32, shape, 1)).astype(jnp.float32)


def tile_product(left, right, i, c, low, high):
    total = None
    for k in range(max(low, i - 1, c - 1), min(high, i + 1, c + 1) + 1):
        term = dot(left[k][i - k + 1], right[k - c + 1])
        total = term if total is None else total + term
    return total


def sum_squares(z, value):
    wide = value.astype(jnp.float32)
    return jnp.sum((wide * wide).reshape(-1, 8, z.tile), axis=0)


def store_half(z, tiles, cells):
    block = z.block
    for t in range(z.half):
        for o in range(z.offsets):
            a = t + o
            u = a % z.half
            value = tiles[
                chain_tile(a // z.half),
                u * block : (u + 1) * block,
                t * block : (t + 1) * block,
            ]
            cells[t, o] = value.astype(cells.dtype)


def mask_kernel(z, pattern, mask_near, mask_far):
    ones = jnp.ones((z.tile, z.tile), jnp.float32)
    for out, first in zip((mask_near, mask_far), half_starts(z)):
        for e in range(3):
            out[e] = own_masked(z, pattern, first, e, ones).astype(out.dtype)


def masks(z, pattern, kind):
    return pl.pallas_call(
        functools.partial(mask_kernel, z),
        out_shape=(z.tiles(3, kind), z.tiles(3, kind)),
        in_specs=[SMEM],
        out_specs=(VMEM, VMEM),
        compiler_params=PARAMS,
        cost_estimate=z.cost(20, 1),
        name="masks",
    )(pattern)


def pack_kernel(z, margin, factor, pattern, _near, _far, near, far, cross):
    near_first, far_first = half_starts(z)
    first_row = lax.axis_index("slab") * z.columns
    plan = ((margin, far_first), (factor, far_first), (margin, near_first), (factor, near_first))
    for k, (source, first) in enumerate(plan):
        for t in range(z.half):
            for o in range(z.offsets):
                flag = pattern[first + t, o] != 0
                if k % 2:
                    row = first_row + first + t + o - z.half
                    inside = jnp.logical_and(row >= 0, row < z.quarter_len)
                    flag = jnp.logical_and(flag, inside)
                value = keep(flag, source[first + t, o])
                cell = t * z.offsets + o
                u = o + t - z.half
                if k == 0:
                    far[cell] = value
                    near[2 * z.cells + cell] = value
                elif k == 1:
                    far[z.cells + cell] = value
                    if 0 <= u < z.half:
                        cross[t, u] = value
                else:
                    near[(k - 2) * z.cells + cell] = value
    per_block = z.block // FLAG_ROWS
    for f in range(z.flag_blocks * per_block):
        t, u = f // z.half, f % z.half
        value = jnp.zeros((FLAG_ROWS, z.block), near.dtype)
        if t < z.half:
            value = keep(pattern[near_first + t, u - t + z.half] != 0, jnp.ones_like(value))
        low = f % per_block * FLAG_ROWS
        near[3 * z.cells + f // per_block, low : low + FLAG_ROWS] = value


def pack(z, margin, factor, pattern, mask_near, mask_far):
    kind = margin.dtype
    return pl.pallas_call(
        functools.partial(pack_kernel, z),
        out_shape=(
            jax.ShapeDtypeStruct((3 * z.cells + z.flag_blocks, z.block, z.block), kind),
            jax.ShapeDtypeStruct((2 * z.cells, z.block, z.block), kind),
            jax.ShapeDtypeStruct((z.half, z.half, z.block, z.block), kind),
        ),
        in_specs=[VMEM, VMEM, SMEM, VMEM, VMEM],
        out_specs=(VMEM, VMEM, VMEM),
        compiler_params=PARAMS,
        name="pack",
    )(margin, factor, pattern, mask_near, mask_far)


def inner_kernel(
    z, pattern, near, far, beside, z_cols, turned, p_part, d_part, d_near, squares, base_near, e_near,
    s_cols, z_turned, image, d_beside,
):
    near_first, _ = half_starts(z)
    kind = near.dtype

    def cells_of(ref, base):
        return lambda t, o: ref[base + t * z.offsets + o]

    expand(z, s_cols.at[0], cells_of(far, 0))
    expand(z, s_cols.at[1], cells_of(near, 0))
    expand(z, s_cols.at[2], cells_of(beside, 0))
    expand(z, s_cols.at[3], cells_of(beside, 2 * z.cells))
    expand(z, z_cols.at[0], cells_of(far, z.cells))
    expand(z, z_cols.at[1], cells_of(near, z.cells))
    expand(z, z_cols.at[2], cells_of(beside, z.cells))
    for x in range(3):
        for e in range(3):
            z_turned[x, e] = z_cols[x, e].T
    turned[0] = z_turned[0, 0]
    turned[1] = z_turned[0, 1]
    turned[2] = z_turned[1, 0]

    def image_tile(y, c):
        total = None
        for inner in range(max(c - 1, y - 1, 1), min(c + 1, y + 1) + 1):
            term = dot(s_cols[inner - 1, y - inner + 1], z_cols[c - 1, inner - c + 1])
            total = term if total is None else total + term
        return total

    def turned_sum(i, c, rows):
        total = None
        for m in rows:
            term = dot(z_turned[i - 1, m - i + 1], image[c - 1, m])
            total = term if total is None else total + term
        return total

    p_part[0] = image_tile(0, 1)
    p_part[1] = image_tile(1, 1)
    for c, rows in ((1, (2, 3)), (2, (0, 1, 2, 3, 4)), (3, (1, 2, 3, 4))):
        for y in rows:
            image[c - 1, y] = image_tile(y, c).astype(kind)
    d_part[0] = turned_sum(1, 1, (2,))
    d_part[1] = turned_sum(2, 1, (2, 3))
    eye = identity(z)
    total = jnp.zeros((8, z.tile), jnp.float32)
    for i in (1, 2, 3):
        value = -turned_sum(i, 2, (i - 1, i, i + 1))
        if i == 2:
            value = eye + value
        value = own_masked(z, pattern, near_first, i - 1, value).astype(kind)
        d_near[i - 1] = value
        total = total + sum_squares(z, value)
    squares[...] = total

    def side_flag(t, u):
        o = offset_of(z, 0, t, u)
        inside = jnp.logical_and(o >= 0, o < z.offsets)
        back = jnp.clip(z.offsets - 1 - o, 0, z.offsets - 1)
        return jnp.logical_and(inside, pattern[near_first + u, back] != 0)

    d_beside[0] = masked(z, -turned_sum(2, 3, (1, 2, 3)), side_flag).astype(kind)
    value = eye - turned_sum(3, 3, (2, 3, 4))
    block = z.block
    per_block = block // FLAG_ROWS
    for t in range(z.half):
        for u in range(z.half):
            f = t * z.half + u
            low = f % per_block * FLAG_ROWS
            flags = beside[3 * z.cells + f // per_block, low : low + FLAG_ROWS]
            flag = flags.astype(jnp.float32)[:1]
            part = (slice(u * block, (u + 1) * block), slice(t * block, (t + 1) * block))
            d_beside[1, part[0], part[1]] = (value[part] * flag).astype(kind)

    factor = (None, z_cols.at[0], z_cols.at[1], z_cols.at[2])
    defect = (None, None, d_near, d_beside)
    for i in (1, 2, 3):
        base_near[i - 1] = z_cols[1, i - 1].astype(jnp.float32) + 0.5 * tile_product(
            factor, d_near, i, 2, 1, 3
        )
        e_near[i - 1] = tile_product(defect, d_near, i, 2, 2, 3)


def inner_step(z, pattern, near, far, beside):
    kind = near.dtype
    tile = z.tile
    return pl.pallas_call(
        functools.partial(inner_kernel, z),
        out_shape=(
            jax.ShapeDtypeStruct((3, 3, tile, tile), kind),
            z.tiles(3, kind),
            z.tiles(2, jnp.float32),
            z.tiles(2, jnp.float32),
            z.tiles(3, kind),
            jax.ShapeDtypeStruct((8, tile), jnp.float32),
            z.tiles(3, jnp.float32),
            z.tiles(3, jnp.float32),
        ),
        in_specs=[SMEM, VMEM, VMEM, VMEM],
        out_specs=(VMEM,) * 8,
        scratch_shapes=[
            pltpu.VMEM((4, 3, tile, tile), kind),
            pltpu.VMEM((3, 3, tile, tile), kind),
            pltpu.VMEM((3, 5, tile, tile), kind),
            pltpu.VMEM((2, tile, tile), kind),
        ],
        compiler_params=PARAMS,
        cost_estimate=z.cost(54, 8),
        name="inner",
    )(pattern, near, far, beside)


def outer_kernel(
    z, pattern, far, cross, z_cols, turned, p_part, d_part, squares, *refs
):
    d_far, d_out, z_far, all_squares, s_far = refs[-5:]
    _, far_first = half_starts(z)
    kind = far.dtype

    def factor_cell(t, o):
        value = far[z.cells + t * z.offsets + o]
        u = o + t - z.half
        if 0 <= u < z.half:
            value = value + cross[t, u]
        return value

    expand(z, s_far, lambda t, o: far[t * z.offsets + o])
    expand(z, z_far, factor_cell)
    link = z_cols[0, 0]
    image = (
        dot(s_far[0], link).astype(kind),
        (dot(s_far[1], link) + p_part[0]).astype(kind),
        (dot(s_far[2], link) + p_part[1]).astype(kind),
    )
    values = (
        -(dot(z_far[0].T, image[0]) + dot(z_far[1].T, image[1]) + dot(z_far[2].T, image[2])),
        identity(z) - (dot(turned[0], image[1]) + dot(turned[1], image[2]) + d_part[0]),
        -(dot(turned[2], image[2]) + d_part[1]),
    )
    total = squares[...]
    for e, value in enumerate(values):
        value = own_masked(z, pattern, far_first, e, value).astype(kind)
        d_far[e] = value
        if e < 2:
            d_out[e] = value
        total = total + sum_squares(z, value)
    all_squares[...] = total


def outer_step(z, pattern, far, cross, z_cols, turned, p_part, d_part, squares, held):
    kind = far.dtype
    return pl.pallas_call(
        functools.partial(outer_kernel, z),
        out_shape=(
            z.tiles(3, kind),
            z.tiles(2, kind),
            z.tiles(3, kind),
            jax.ShapeDtypeStruct(squares.shape, jnp.float32),
        ),
        in_specs=[SMEM] + [VMEM] * (7 + len(held)),
        out_specs=(VMEM,) * 4,
        scratch_shapes=[pltpu.VMEM((3, z.tile, z.tile), kind)],
        compiler_params=PARAMS,
        cost_estimate=z.cost(9, 4),
        name="outer",
    )(pattern, far, cross, z_cols, turned, p_part, d_part, squares, *held)


def middle_kernel(
    z, squares, z_cols, z_far, d_far, d_near, base_near, e_near, mask_near, refined, base, e_part, spread,
    square, tiles, cells, sem,
):
    lanes = jnp.sum(squares[...], axis=0, keepdims=True)
    folded = lanes[:, : z.block]
    for t in range(1, z.half):
        folded = folded + lanes[:, t * z.block : (t + 1) * z.block]
    spread[...] = jnp.broadcast_to(folded[None], spread.shape)
    near_first, _ = half_starts(z)
    factor = (z_far, z_cols.at[0], z_cols.at[1], z_cols.at[2])
    defect = (None, d_far, d_near)
    for i in (1, 2, 3):
        value = e_near[i - 1]
        if i < 3:
            value = value + dot(d_far[i], d_near[0])
        square[i - 1] = (value * mask_near[i - 1].astype(jnp.float32)).astype(square.dtype)
    for i in (1, 2, 3):
        value = base_near[i - 1] + 0.375 * tile_product(factor, square, i, 2, 1, 3)
        tiles[i - 1] = value * mask_near[i - 1].astype(jnp.float32)
    store_half(z, tiles, cells)
    copy = pltpu.make_async_copy(cells, refined.at[pl.ds(near_first, z.half)], sem)
    copy.start()
    for i in (0, 1, 2):
        base[i] = z_cols[0, i].astype(jnp.float32) + 0.5 * tile_product(factor, d_far, i, 1, 0, 2)
        e_part[i] = tile_product(defect, d_far, i, 1, 1, 2)
    copy.wait()


def middle_step(z, squares, z_cols, z_far, d_far, d_near, base_near, e_near, mask_near):
    kind = z_far.dtype
    shape = (z.columns, z.offsets, z.block, z.block)
    return pl.pallas_call(
        functools.partial(middle_kernel, z),
        out_shape=(
            jax.ShapeDtypeStruct(shape, kind),
            z.tiles(3, jnp.float32),
            z.tiles(3, jnp.float32),
            jax.ShapeDtypeStruct((z.devices, 1, z.block), jnp.float32),
        ),
        in_specs=[VMEM] * 8,
        out_specs=(HBM, VMEM, VMEM, VMEM),
        scratch_shapes=[
            pltpu.VMEM((3, z.tile, z.tile), kind),
            pltpu.VMEM((3, z.tile, z.tile), jnp.float32),
            pltpu.VMEM((z.half,) + shape[1:], kind),
            pltpu.SemaphoreType.DMA(()),
        ],
        compiler_params=PARAMS,
        cost_estimate=z.cost(21, 6),
        name="middle",
    )(squares, z_cols, z_far, d_far, d_near, base_near, e_near, mask_near)


def last_kernel(
    z, z_cols, z_far, d_far, d_in, base, e_part, mask_far, gathered, _, refined, norm, square, tiles,
    cells, sem,
):
    _, far_first = half_starts(z)
    factor = (z_far, z_cols.at[0], z_cols.at[1])
    values = (
        e_part[0] + dot(d_in[1], d_far[0]),
        e_part[1] + dot(d_in[0], d_far[0]),
        e_part[2],
    )
    for i, value in enumerate(values):
        square[i] = (value * mask_far[i].astype(jnp.float32)).astype(square.dtype)
    for i in (0, 1, 2):
        value = base[i] + 0.375 * tile_product(factor, square, i, 1, 0, 2)
        tiles[i] = value * mask_far[i].astype(jnp.float32)
    store_half(z, tiles, cells)
    copy = pltpu.make_async_copy(cells, refined.at[pl.ds(far_first, z.half)], sem)
    copy.start()
    mean = jnp.sum(gathered[...]) * (1.0 / z.entries)
    norm[...] = jnp.sqrt(jnp.full(norm.shape, mean, jnp.float32))
    copy.wait()


def last_step(z, z_cols, z_far, d_far, d_in, base, e_part, mask_far, gathered, refined):
    kind = refined.dtype
    return pl.pallas_call(
        functools.partial(last_kernel, z),
        out_shape=(
            jax.ShapeDtypeStruct(refined.shape, kind),
            jax.ShapeDtypeStruct((1, z.block), jnp.float32),
        ),
        in_specs=[VMEM] * 8 + [HBM],
        out_specs=(HBM, VMEM),
        scratch_shapes=[
            pltpu.VMEM((3, z.tile, z.tile), kind),
            pltpu.VMEM((3, z.tile, z.tile), jnp.float32),
            pltpu.VMEM((z.half,) + refined.shape[1:], kind),
            pltpu.SemaphoreType.DMA(()),
        ],
        input_output_aliases={8: 0},
        compiler_params=PARAMS,
        cost_estimate=z.cost(9, 4),
        name="last",
    )(z_cols, z_far, d_far, d_in, base, e_part, mask_far, gathered, refined)


def swaps(pairs):
    return [pair for i, j in pairs for pair in ((i, j), (j, i))]


def per_device(margin, factor, pattern):
    slabs = lax.axis_size("slab")
    devices = lax.axis_size("grp") * slabs
    z = Sizes(margin.shape, margin.shape[0] * slabs, devices)
    if slabs % 2 or z.columns != 2 * z.half:
        raise ValueError("sizes")
    near_pairs = [(i, i + 1) for i in range(0, devices - 1, 2)]
    far_pairs = [(i, i + 1) for i in range(1, devices - 1, 2)]
    inner_pairs = [(i, j) for i, j in far_pairs if j % slabs]
    cross_pairs = [(i, j) for i, j in far_pairs if not j % slabs]
    mask_near, mask_far = masks(z, pattern, margin.dtype)
    near, far, cross = pack(z, margin, factor, pattern, mask_near, mask_far)
    beyond = lax.ppermute(far, AXES, swaps(inner_pairs))
    across = lax.ppermute(cross, AXES, swaps(cross_pairs))
    beside = lax.ppermute(near, AXES, swaps(near_pairs))
    z_cols, turned, p_part, d_part, d_near, squares, base_near, e_near = inner_step(
        z, pattern, near, far, beside
    )
    held = (d_near, base_near, e_near, mask_near, mask_far)
    d_far, d_out, z_far, squares = outer_step(
        z, pattern, beyond, across, z_cols, turned, p_part, d_part, squares, held
    )
    d_in = lax.ppermute(d_out, AXES, swaps(far_pairs))
    refined, base, e_part, spread = middle_step(
        z, squares, z_cols, z_far, d_far, d_near, base_near, e_near, mask_near
    )
    gathered = lax.all_to_all(spread, AXES, 0, 0, tiled=True)
    refined, norm = last_step(
        z, z_cols, z_far, d_far, d_in, base, e_part, mask_far, gathered, refined
    )
    return refined, norm[0, 0]


def solution(mesh):
    return jax.shard_map(
        per_device,
        mesh=mesh,
        in_specs=(
            P(AXES, None, None, None),
            P(AXES, None, None, None),
            P(AXES, None),
        ),
        out_specs=(P(AXES, None, None, None), P()),
        check_vma=False,
    )
```

```python
import functools

import jax
import jax.numpy as jnp
from jax import lax
from jax.experimental import pallas as pl
from jax.experimental.pallas import tpu as pltpu
from jax.sharding import PartitionSpec as P


AXES = ("grp", "slab")
HBM = pl.BlockSpec(memory_space=pltpu.HBM)
VMEM = pl.BlockSpec(memory_space=pltpu.VMEM)
SMEM = pl.BlockSpec(memory_space=pltpu.SMEM)
PARAMS = pltpu.CompilerParams(vmem_limit_bytes=32 * 1024 * 1024)
FLAG_ROWS = 16


class Sizes:
    def __init__(self, shape, quarter_len, devices):
        self.columns, self.offsets, self.block, _ = shape
        self.half = (self.offsets - 1) // 2
        self.tile = self.half * self.block
        self.cells = self.half * self.offsets
        self.flag_blocks = -(-self.half * self.half * FLAG_ROWS // self.block)
        self.quarter_len = quarter_len
        self.devices = devices
        self.entries = self.columns * devices * self.block

    def cost(self, products, moved):
        return pl.CostEstimate(
            flops=products * 2 * self.tile**3, bytes_accessed=moved * 2**20, transcendentals=0
        )

    def tiles(self, count, dtype):
        return jax.ShapeDtypeStruct((count, self.tile, self.tile), dtype)


def odd_device():
    return lax.rem(lax.axis_index("slab"), 2)


def half_starts(z):
    near = jnp.where(odd_device() == 1, 0, z.columns - z.half)
    return near, z.columns - z.half - near


def keep(flag, value):
    return jnp.where(flag, value, jnp.zeros_like(value))


def dot(left, right):
    return jnp.dot(left, right, preferred_element_type=jnp.float32)


def chain_tile(true_tile):
    return jnp.where(odd_device() == 1, 2 - true_tile, true_tile)


def expand(z, out, read):
    block = z.block
    for t in range(z.half):
        for a in range(3 * z.half):
            o = a - t
            u = a % z.half
            if 0 <= o < z.offsets:
                value = read(t, o)
            else:
                value = jnp.zeros((block, block), out.dtype)
            out[
                chain_tile(a // z.half),
                u * block : (u + 1) * block,
                t * block : (t + 1) * block,
            ] = value


def offset_of(z, e, t, u):
    return jnp.where(odd_device() == 1, 1 - e, e - 1) * z.half + u - t + z.half


def flag_of(z, pattern, first, e, t, u):
    o = offset_of(z, e, t, u)
    inside = jnp.logical_and(o >= 0, o < z.offsets)
    return jnp.logical_and(inside, pattern[first + t, jnp.clip(o, 0, z.offsets - 1)] != 0)


def masked(z, value, flag):
    block = z.block
    rows = []
    for u in range(z.half):
        rows.append(
            jnp.concatenate(
                [
                    keep(
                        flag(t, u),
                        value[u * block : (u + 1) * block, t * block : (t + 1) * block],
                    )
                    for t in range(z.half)
                ],
                axis=1,
            )
        )
    return jnp.concatenate(rows, axis=0)


def own_masked(z, pattern, first, e, value):
    return masked(z, value, lambda t, u: flag_of(z, pattern, first, e, t, u))


def identity(z):
    shape = (z.tile, z.tile)
    rows = lax.broadcasted_iota(jnp.int32, shape, 0)
    return (rows == lax.broadcasted_iota(jnp.int32, shape, 1)).astype(jnp.float32)


def tile_product(left, right, i, c, low, high):
    total = None
    for k in range(max(low, i - 1, c - 1), min(high, i + 1, c + 1) + 1):
        term = dot(left[k][i - k + 1], right[k - c + 1])
        total = term if total is None else total + term
    return total


def sum_squares(z, value):
    wide = value.astype(jnp.float32)
    return jnp.sum((wide * wide).reshape(-1, 8, z.tile), axis=0)


def store_half(z, tiles, cells):
    block = z.block
    for t in range(z.half):
        for o in range(z.offsets):
            a = t + o
            u = a % z.half
            value = tiles[
                chain_tile(a // z.half),
                u * block : (u + 1) * block,
                t * block : (t + 1) * block,
            ]
            cells[t, o] = value.astype(cells.dtype)


def mask_kernel(z, pattern, mask_near, mask_far):
    ones = jnp.ones((z.tile, z.tile), jnp.float32)
    for out, first in zip((mask_near, mask_far), half_starts(z)):
        for e in range(3):
            out[e] = own_masked(z, pattern, first, e, ones).astype(out.dtype)


def masks(z, pattern, kind):
    return pl.pallas_call(
        functools.partial(mask_kernel, z),
        out_shape=(z.tiles(3, kind), z.tiles(3, kind)),
        in_specs=[SMEM],
        out_specs=(VMEM, VMEM),
        compiler_params=PARAMS,
        cost_estimate=z.cost(20, 1),
        name="masks",
    )(pattern)


def pack_kernel(z, margin, factor, pattern, _near, _far, near, far, cross):
    near_first, far_first = half_starts(z)
    first_row = lax.axis_index("slab") * z.columns
    plan = ((margin, far_first), (factor, far_first), (margin, near_first), (factor, near_first))
    for k, (source, first) in enumerate(plan):
        for t in range(z.half):
            for o in range(z.offsets):
                flag = pattern[first + t, o] != 0
                if k % 2:
                    row = first_row + first + t + o - z.half
                    inside = jnp.logical_and(row >= 0, row < z.quarter_len)
                    flag = jnp.logical_and(flag, inside)
                value = keep(flag, source[first + t, o])
                cell = t * z.offsets + o
                u = o + t - z.half
                if k == 0:
                    far[cell] = value
                    near[2 * z.cells + cell] = value
                elif k == 1:
                    far[z.cells + cell] = value
                    if 0 <= u < z.half:
                        cross[t, u] = value
                else:
                    near[(k - 2) * z.cells + cell] = value
    per_block = z.block // FLAG_ROWS
    for f in range(z.flag_blocks * per_block):
        t, u = f // z.half, f % z.half
        value = jnp.zeros((FLAG_ROWS, z.block), near.dtype)
        if t < z.half:
            value = keep(pattern[near_first + t, u - t + z.half] != 0, jnp.ones_like(value))
        low = f % per_block * FLAG_ROWS
        near[3 * z.cells + f // per_block, low : low + FLAG_ROWS] = value


def pack(z, margin, factor, pattern, mask_near, mask_far):
    kind = margin.dtype
    return pl.pallas_call(
        functools.partial(pack_kernel, z),
        out_shape=(
            jax.ShapeDtypeStruct((3 * z.cells + z.flag_blocks, z.block, z.block), kind),
            jax.ShapeDtypeStruct((2 * z.cells, z.block, z.block), kind),
            jax.ShapeDtypeStruct((z.half, z.half, z.block, z.block), kind),
        ),
        in_specs=[VMEM, VMEM, SMEM, VMEM, VMEM],
        out_specs=(VMEM, VMEM, VMEM),
        compiler_params=PARAMS,
        name="pack",
    )(margin, factor, pattern, mask_near, mask_far)


def inner_kernel(
    z, pattern, near, far, beside, z_cols, turned, p_part, d_part, d_near, squares, base_near, e_near,
    s_cols, z_turned, image, d_beside,
):
    near_first, _ = half_starts(z)
    kind = near.dtype

    def cells_of(ref, base):
        return lambda t, o: ref[base + t * z.offsets + o]

    expand(z, s_cols.at[0], cells_of(far, 0))
    expand(z, s_cols.at[1], cells_of(near, 0))
    expand(z, s_cols.at[2], cells_of(beside, 0))
    expand(z, s_cols.at[3], cells_of(beside, 2 * z.cells))
    expand(z, z_cols.at[0], cells_of(far, z.cells))
    expand(z, z_cols.at[1], cells_of(near, z.cells))
    expand(z, z_cols.at[2], cells_of(beside, z.cells))
    for x in range(3):
        for e in range(3):
            z_turned[x, e] = z_cols[x, e].T
    turned[0] = z_turned[0, 0]
    turned[1] = z_turned[0, 1]
    turned[2] = z_turned[1, 0]

    def image_tile(y, c):
        total = None
        for inner in range(max(c - 1, y - 1, 1), min(c + 1, y + 1) + 1):
            term = dot(s_cols[inner - 1, y - inner + 1], z_cols[c - 1, inner - c + 1])
            total = term if total is None else total + term
        return total

    def turned_sum(i, c, rows):
        total = None
        for m in rows:
            term = dot(z_turned[i - 1, m - i + 1], image[c - 1, m])
            total = term if total is None else total + term
        return total

    p_part[0] = image_tile(0, 1)
    p_part[1] = image_tile(1, 1)
    for c, rows in ((1, (2, 3)), (2, (0, 1, 2, 3, 4)), (3, (1, 2, 3, 4))):
        for y in rows:
            image[c - 1, y] = image_tile(y, c).astype(kind)
    d_part[0] = turned_sum(1, 1, (2,))
    d_part[1] = turned_sum(2, 1, (2, 3))
    eye = identity(z)
    total = jnp.zeros((8, z.tile), jnp.float32)
    for i in (1, 2, 3):
        value = -turned_sum(i, 2, (i - 1, i, i + 1))
        if i == 2:
            value = eye + value
        value = own_masked(z, pattern, near_first, i - 1, value).astype(kind)
        d_near[i - 1] = value
        total = total + sum_squares(z, value)
    squares[...] = total

    def side_flag(t, u):
        o = offset_of(z, 0, t, u)
        inside = jnp.logical_and(o >= 0, o < z.offsets)
        back = jnp.clip(z.offsets - 1 - o, 0, z.offsets - 1)
        return jnp.logical_and(inside, pattern[near_first + u, back] != 0)

    d_beside[0] = masked(z, -turned_sum(2, 3, (1, 2, 3)), side_flag).astype(kind)
    value = eye - turned_sum(3, 3, (2, 3, 4))
    block = z.block
    per_block = block // FLAG_ROWS
    for t in range(z.half):
        for u in range(z.half):
            f = t * z.half + u
            low = f % per_block * FLAG_ROWS
            flags = beside[3 * z.cells + f // per_block, low : low + FLAG_ROWS]
            flag = flags.astype(jnp.float32)[:1]
            part = (slice(u * block, (u + 1) * block), slice(t * block, (t + 1) * block))
            d_beside[1, part[0], part[1]] = (value[part] * flag).astype(kind)

    factor = (None, z_cols.at[0], z_cols.at[1], z_cols.at[2])
    defect = (None, None, d_near, d_beside)
    for i in (1, 2, 3):
        base_near[i - 1] = z_cols[1, i - 1].astype(jnp.float32) + 0.5 * tile_product(
            factor, d_near, i, 2, 1, 3
        )
        e_near[i - 1] = tile_product(defect, d_near, i, 2, 2, 3)


def inner_step(z, pattern, near, far, beside):
    kind = near.dtype
    tile = z.tile
    return pl.pallas_call(
        functools.partial(inner_kernel, z),
        out_shape=(
            jax.ShapeDtypeStruct((3, 3, tile, tile), kind),
            z.tiles(3, kind),
            z.tiles(2, jnp.float32),
            z.tiles(2, jnp.float32),
            z.tiles(3, kind),
            jax.ShapeDtypeStruct((8, tile), jnp.float32),
            z.tiles(3, jnp.float32),
            z.tiles(3, jnp.float32),
        ),
        in_specs=[SMEM, VMEM, VMEM, VMEM],
        out_specs=(VMEM,) * 8,
        scratch_shapes=[
            pltpu.VMEM((4, 3, tile, tile), kind),
            pltpu.VMEM((3, 3, tile, tile), kind),
            pltpu.VMEM((3, 5, tile, tile), kind),
            pltpu.VMEM((2, tile, tile), kind),
        ],
        compiler_params=PARAMS,
        cost_estimate=z.cost(54, 8),
        name="inner",
    )(pattern, near, far, beside)


def outer_kernel(
    z, pattern, far, cross, z_cols, turned, p_part, d_part, squares, *refs
):
    d_far, d_out, z_far, all_squares, s_far = refs[-5:]
    _, far_first = half_starts(z)
    kind = far.dtype

    def factor_cell(t, o):
        value = far[z.cells + t * z.offsets + o]
        u = o + t - z.half
        if 0 <= u < z.half:
            value = value + cross[t, u]
        return value

    expand(z, s_far, lambda t, o: far[t * z.offsets + o])
    expand(z, z_far, factor_cell)
    link = z_cols[0, 0]
    image = (
        dot(s_far[0], link).astype(kind),
        (dot(s_far[1], link) + p_part[0]).astype(kind),
        (dot(s_far[2], link) + p_part[1]).astype(kind),
    )
    values = (
        -(dot(z_far[0].T, image[0]) + dot(z_far[1].T, image[1]) + dot(z_far[2].T, image[2])),
        identity(z) - (dot(turned[0], image[1]) + dot(turned[1], image[2]) + d_part[0]),
        -(dot(turned[2], image[2]) + d_part[1]),
    )
    total = squares[...]
    for e, value in enumerate(values):
        value = own_masked(z, pattern, far_first, e, value).astype(kind)
        d_far[e] = value
        if e < 2:
            d_out[e] = value
        total = total + sum_squares(z, value)
    all_squares[...] = total


def outer_step(z, pattern, far, cross, z_cols, turned, p_part, d_part, squares, held):
    kind = far.dtype
    return pl.pallas_call(
        functools.partial(outer_kernel, z),
        out_shape=(
            z.tiles(3, kind),
            z.tiles(2, kind),
            z.tiles(3, kind),
            jax.ShapeDtypeStruct(squares.shape, jnp.float32),
        ),
        in_specs=[SMEM] + [VMEM] * (7 + len(held)),
        out_specs=(VMEM,) * 4,
        scratch_shapes=[pltpu.VMEM((3, z.tile, z.tile), kind)],
        compiler_params=PARAMS,
        cost_estimate=z.cost(9, 4),
        name="outer",
    )(pattern, far, cross, z_cols, turned, p_part, d_part, squares, *held)


def middle_kernel(
    z, squares, z_cols, z_far, d_far, d_near, base_near, e_near, mask_near, mask_far, refined, narrow, wide,
    spread, square, done, parts, tiles, cells, sems,
):
    near_first, _ = half_starts(z)
    moves = [
        (z_far.at[pl.ds(1, 2)], narrow.at[pl.ds(0, 2)]),
        (z_cols.at[0], narrow.at[pl.ds(2, 3)]),
        (z_cols.at[1, pl.ds(0, 2)], narrow.at[pl.ds(5, 2)]),
        (d_far.at[pl.ds(0, 1)], narrow.at[pl.ds(7, 1)]),
    ]
    copies = [
        pltpu.make_async_copy(source, target, sems.at[k]) for k, (source, target) in enumerate(moves)
    ]
    for copy in copies:
        copy.start()

    def send(source, target):
        copies.append(pltpu.make_async_copy(source, target, sems.at[len(copies)]))
        copies[-1].start()

    lanes = jnp.sum(squares[...], axis=0, keepdims=True)
    folded = lanes[:, : z.block]
    for t in range(1, z.half):
        folded = folded + lanes[:, t * z.block : (t + 1) * z.block]
    spread[...] = jnp.broadcast_to(folded[None], spread.shape)
    factor = (z_far, z_cols.at[0], z_cols.at[1], z_cols.at[2])
    defect = (None, d_far, d_near)
    value = tile_product(defect, d_far, 2, 1, 1, 2) * mask_far[2].astype(jnp.float32)
    done[0] = value.astype(done.dtype)
    send(done, narrow.at[pl.ds(8, 1)])
    for i in (0, 1):
        parts[i] = tile_product(defect, d_far, i, 1, 1, 2)
    for i in (0, 1, 2):
        parts[2 + i] = z_cols[0, i].astype(jnp.float32) + 0.5 * tile_product(
            factor, d_far, i, 1, 0, 2
        )
    send(parts, wide)
    for i in (1, 2, 3):
        value = e_near[i - 1]
        if i < 3:
            value = value + dot(d_far[i], d_near[0])
        square[i - 1] = (value * mask_near[i - 1].astype(jnp.float32)).astype(square.dtype)
    for i in (1, 2, 3):
        value = base_near[i - 1] + 0.375 * tile_product(factor, square, i, 2, 1, 3)
        tiles[i - 1] = value * mask_near[i - 1].astype(jnp.float32)
    store_half(z, tiles, cells)
    send(cells, refined.at[pl.ds(near_first, z.half)])
    for copy in copies:
        copy.wait()


def middle_step(z, squares, z_cols, z_far, d_far, d_near, base_near, e_near, mask_near, mask_far):
    kind = z_far.dtype
    shape = (z.columns, z.offsets, z.block, z.block)
    return pl.pallas_call(
        functools.partial(middle_kernel, z),
        out_shape=(
            jax.ShapeDtypeStruct(shape, kind),
            z.tiles(9, kind),
            z.tiles(5, jnp.float32),
            jax.ShapeDtypeStruct((z.devices, 1, z.block), jnp.float32),
        ),
        in_specs=[VMEM] * 9,
        out_specs=(HBM, HBM, HBM, VMEM),
        scratch_shapes=[
            pltpu.VMEM((3, z.tile, z.tile), kind),
            pltpu.VMEM((1, z.tile, z.tile), kind),
            pltpu.VMEM((5, z.tile, z.tile), jnp.float32),
            pltpu.VMEM((3, z.tile, z.tile), jnp.float32),
            pltpu.VMEM((z.half,) + shape[1:], kind),
            pltpu.SemaphoreType.DMA((7,)),
        ],
        compiler_params=PARAMS,
        cost_estimate=z.cost(21, 6),
        name="middle",
    )(squares, z_cols, z_far, d_far, d_near, base_near, e_near, mask_near, mask_far)


def last_kernel(
    z, pattern_in, narrow_in, wide_in, d_in, _, refined, _narrow, _wide, _d, pattern, narrow, wide, d_far,
    square, tiles, cells, sems,
):
    _, first = half_starts(z)
    link = pl.ds(7, 2)
    factor = pl.ds(0, 7)
    moves = (
        (pattern_in, pattern),
        (d_in, d_far),
        (narrow_in.at[link], narrow.at[link]),
        (wide_in.at[pl.ds(0, 2)], wide.at[pl.ds(0, 2)]),
        (narrow_in.at[factor], narrow.at[factor]),
        (wide_in.at[pl.ds(2, 3)], wide.at[pl.ds(2, 3)]),
    )
    copies = [
        pltpu.make_async_copy(source, target, sems.at[k]) for k, (source, target) in enumerate(moves)
    ]
    for copy in copies:
        copy.start()
    for copy in copies[:4]:
        copy.wait()
    for i in (0, 1):
        value = wide[i] + dot(d_far[1 - i], narrow[7])
        square[i] = own_masked(z, pattern, first, i, value).astype(square.dtype)
    square[2] = narrow[8]
    for copy in copies[4:]:
        copy.wait()
    base = (-1, 2, 5)
    for i in (0, 1, 2):
        total = None
        for k in range(max(0, i - 1), min(2, i + 1) + 1):
            term = dot(narrow[base[k] + i - k + 1], square[k])
            total = term if total is None else total + term
        tiles[i] = own_masked(z, pattern, first, i, wide[2 + i] + 0.375 * total)
    store_half(z, tiles, cells)
    copy = pltpu.make_async_copy(cells, refined.at[pl.ds(first, z.half)], sems.at[6])
    copy.start()
    copy.wait()


def last_step(z, pattern, narrow, wide, d_in, refined):
    kind = refined.dtype
    return pl.pallas_call(
        functools.partial(last_kernel, z),
        out_shape=tuple(
            jax.ShapeDtypeStruct(held.shape, held.dtype) for held in (refined, narrow, wide, d_in)
        ),
        in_specs=[HBM] * 5,
        out_specs=(HBM,) * 4,
        scratch_shapes=[
            pltpu.SMEM(pattern.shape, pattern.dtype),
            pltpu.VMEM(narrow.shape, kind),
            pltpu.VMEM(wide.shape, jnp.float32),
            pltpu.VMEM(d_in.shape, kind),
            pltpu.VMEM((3, z.tile, z.tile), kind),
            pltpu.VMEM((3, z.tile, z.tile), jnp.float32),
            pltpu.VMEM((z.half,) + refined.shape[1:], kind),
            pltpu.SemaphoreType.DMA((7,)),
        ],
        input_output_aliases={4: 0, 1: 1, 2: 2, 3: 3},
        compiler_params=PARAMS,
        cost_estimate=z.cost(9, 4),
        name="last",
    )(pattern, narrow, wide, d_in, refined)[0]


def norm_kernel(z, gathered, norm):
    mean = jnp.sum(gathered[...]) * (1.0 / z.entries)
    norm[...] = jnp.sqrt(jnp.full(norm.shape, mean, jnp.float32))


def norm_step(z, gathered):
    return pl.pallas_call(
        functools.partial(norm_kernel, z),
        out_shape=jax.ShapeDtypeStruct((1, z.block), jnp.float32),
        in_specs=[VMEM],
        out_specs=VMEM,
        compiler_params=PARAMS,
        name="norm",
    )(gathered)


def swaps(pairs):
    return [pair for i, j in pairs for pair in ((i, j), (j, i))]


def per_device(margin, factor, pattern):
    slabs = lax.axis_size("slab")
    devices = lax.axis_size("grp") * slabs
    z = Sizes(margin.shape, margin.shape[0] * slabs, devices)
    if slabs % 2 or z.columns != 2 * z.half:
        raise ValueError("sizes")
    near_pairs = [(i, i + 1) for i in range(0, devices - 1, 2)]
    far_pairs = [(i, i + 1) for i in range(1, devices - 1, 2)]
    inner_pairs = [(i, j) for i, j in far_pairs if j % slabs]
    cross_pairs = [(i, j) for i, j in far_pairs if not j % slabs]
    mask_near, mask_far = masks(z, pattern, margin.dtype)
    near, far, cross = pack(z, margin, factor, pattern, mask_near, mask_far)
    beyond = lax.ppermute(far, AXES, swaps(inner_pairs))
    across = lax.ppermute(cross, AXES, swaps(cross_pairs))
    beside = lax.ppermute(near, AXES, swaps(near_pairs))
    z_cols, turned, p_part, d_part, d_near, squares, base_near, e_near = inner_step(
        z, pattern, near, far, beside
    )
    held = (d_near, base_near, e_near, mask_near, mask_far)
    d_far, d_out, z_far, squares = outer_step(
        z, pattern, beyond, across, z_cols, turned, p_part, d_part, squares, held
    )
    d_in = lax.ppermute(d_out, AXES, swaps(far_pairs))
    refined, narrow, wide, spread = middle_step(
        z, squares, z_cols, z_far, d_far, d_near, base_near, e_near, mask_near, mask_far
    )
    gathered = lax.all_to_all(spread, AXES, 0, 0, tiled=True)
    refined = last_step(z, pattern, narrow, wide, d_in, refined)
    norm = norm_step(z, gathered)
    return refined, norm[0, 0]


def solution(mesh):
    return jax.shard_map(
        per_device,
        mesh=mesh,
        in_specs=(
            P(AXES, None, None, None),
            P(AXES, None, None, None),
            P(AXES, None),
        ),
        out_specs=(P(AXES, None, None, None), P()),
        check_vma=False,
    )
```

```python
import functools

import jax
import jax.numpy as jnp
from jax import lax
from jax.experimental import pallas as pl
from jax.experimental.pallas import tpu as pltpu
from jax.sharding import PartitionSpec as P


AXES = ("grp", "slab")
HBM = pl.BlockSpec(memory_space=pltpu.HBM)
VMEM = pl.BlockSpec(memory_space=pltpu.VMEM)
SMEM = pl.BlockSpec(memory_space=pltpu.SMEM)
PARAMS = pltpu.CompilerParams(vmem_limit_bytes=32 * 1024 * 1024)
FLAG_ROWS = 16


class Sizes:
    def __init__(self, shape, quarter_len, devices):
        self.columns, self.offsets, self.block, _ = shape
        self.half = (self.offsets - 1) // 2
        self.tile = self.half * self.block
        self.cells = self.half * self.offsets
        self.flag_blocks = -(-self.half * self.half * FLAG_ROWS // self.block)
        self.quarter_len = quarter_len
        self.devices = devices
        self.entries = self.columns * devices * self.block

    def cost(self, products, moved):
        return pl.CostEstimate(
            flops=products * 2 * self.tile**3, bytes_accessed=moved * 2**20, transcendentals=0
        )

    def tiles(self, count, dtype):
        return jax.ShapeDtypeStruct((count, self.tile, self.tile), dtype)


def odd_device():
    return lax.rem(lax.axis_index("slab"), 2)


def half_starts(z):
    near = jnp.where(odd_device() == 1, 0, z.columns - z.half)
    return near, z.columns - z.half - near


def keep(flag, value):
    return jnp.where(flag, value, jnp.zeros_like(value))


def dot(left, right):
    return jnp.dot(left, right, preferred_element_type=jnp.float32)


def chain_tile(true_tile):
    return jnp.where(odd_device() == 1, 2 - true_tile, true_tile)


def expand(z, out, read):
    block = z.block
    for t in range(z.half):
        for a in range(3 * z.half):
            o = a - t
            u = a % z.half
            if 0 <= o < z.offsets:
                value = read(t, o)
            else:
                value = jnp.zeros((block, block), out.dtype)
            out[
                chain_tile(a // z.half),
                u * block : (u + 1) * block,
                t * block : (t + 1) * block,
            ] = value


def offset_of(z, e, t, u):
    return jnp.where(odd_device() == 1, 1 - e, e - 1) * z.half + u - t + z.half


def flag_of(z, pattern, first, e, t, u):
    o = offset_of(z, e, t, u)
    inside = jnp.logical_and(o >= 0, o < z.offsets)
    return jnp.logical_and(inside, pattern[first + t, jnp.clip(o, 0, z.offsets - 1)] != 0)


def masked(z, value, flag):
    block = z.block
    rows = []
    for u in range(z.half):
        rows.append(
            jnp.concatenate(
                [
                    keep(
                        flag(t, u),
                        value[u * block : (u + 1) * block, t * block : (t + 1) * block],
                    )
                    for t in range(z.half)
                ],
                axis=1,
            )
        )
    return jnp.concatenate(rows, axis=0)


def own_masked(z, pattern, first, e, value):
    return masked(z, value, lambda t, u: flag_of(z, pattern, first, e, t, u))


def identity(z):
    shape = (z.tile, z.tile)
    rows = lax.broadcasted_iota(jnp.int32, shape, 0)
    return (rows == lax.broadcasted_iota(jnp.int32, shape, 1)).astype(jnp.float32)


def tile_product(left, right, i, c, low, high):
    total = None
    for k in range(max(low, i - 1, c - 1), min(high, i + 1, c + 1) + 1):
        term = dot(left[k][i - k + 1], right[k - c + 1])
        total = term if total is None else total + term
    return total


def sum_squares(z, value):
    wide = value.astype(jnp.float32)
    return jnp.sum((wide * wide).reshape(-1, 8, z.tile), axis=0)


def store_half(z, tiles, cells):
    block = z.block
    for t in range(z.half):
        for o in range(z.offsets):
            a = t + o
            u = a % z.half
            value = tiles[
                chain_tile(a // z.half),
                u * block : (u + 1) * block,
                t * block : (t + 1) * block,
            ]
            cells[t, o] = value.astype(cells.dtype)


def mask_kernel(z, pattern, mask_near):
    first, _ = half_starts(z)
    ones = jnp.ones((z.tile, z.tile), jnp.float32)
    for e in range(3):
        mask_near[e] = own_masked(z, pattern, first, e, ones).astype(mask_near.dtype)


def masks(z, pattern, kind):
    return pl.pallas_call(
        functools.partial(mask_kernel, z),
        out_shape=z.tiles(3, kind),
        in_specs=[SMEM],
        out_specs=VMEM,
        compiler_params=PARAMS,
        cost_estimate=z.cost(20, 1),
        name="masks",
    )(pattern)


def pack_kernel(z, margin, factor, pattern, _, near, far, cross):
    near_first, far_first = half_starts(z)
    first_row = lax.axis_index("slab") * z.columns
    plan = ((margin, far_first), (factor, far_first), (margin, near_first), (factor, near_first))
    for k, (source, first) in enumerate(plan):
        for t in range(z.half):
            for o in range(z.offsets):
                flag = pattern[first + t, o] != 0
                if k % 2:
                    row = first_row + first + t + o - z.half
                    inside = jnp.logical_and(row >= 0, row < z.quarter_len)
                    flag = jnp.logical_and(flag, inside)
                value = keep(flag, source[first + t, o])
                cell = t * z.offsets + o
                u = o + t - z.half
                if k == 0:
                    far[cell] = value
                    near[2 * z.cells + cell] = value
                elif k == 1:
                    far[z.cells + cell] = value
                    if 0 <= u < z.half:
                        cross[t, u] = value
                else:
                    near[(k - 2) * z.cells + cell] = value
    per_block = z.block // FLAG_ROWS
    for f in range(z.flag_blocks * per_block):
        t, u = f // z.half, f % z.half
        value = jnp.zeros((FLAG_ROWS, z.block), near.dtype)
        if t < z.half:
            value = keep(pattern[near_first + t, u - t + z.half] != 0, jnp.ones_like(value))
        low = f % per_block * FLAG_ROWS
        near[3 * z.cells + f // per_block, low : low + FLAG_ROWS] = value


def pack(z, margin, factor, pattern, mask_near):
    kind = margin.dtype
    return pl.pallas_call(
        functools.partial(pack_kernel, z),
        out_shape=(
            jax.ShapeDtypeStruct((3 * z.cells + z.flag_blocks, z.block, z.block), kind),
            jax.ShapeDtypeStruct((2 * z.cells, z.block, z.block), kind),
            jax.ShapeDtypeStruct((z.half, z.half, z.block, z.block), kind),
        ),
        in_specs=[VMEM, VMEM, SMEM, VMEM],
        out_specs=(VMEM, VMEM, VMEM),
        compiler_params=PARAMS,
        name="pack",
    )(margin, factor, pattern, mask_near)


def inner_kernel(
    z, pattern, near, far, beside, z_cols, turned, p_part, d_part, d_near, squares, base_near, e_near,
    s_cols, z_turned, image, d_beside,
):
    near_first, _ = half_starts(z)
    kind = near.dtype

    def cells_of(ref, base):
        return lambda t, o: ref[base + t * z.offsets + o]

    expand(z, s_cols.at[0], cells_of(far, 0))
    expand(z, s_cols.at[1], cells_of(near, 0))
    expand(z, s_cols.at[2], cells_of(beside, 0))
    expand(z, s_cols.at[3], cells_of(beside, 2 * z.cells))
    expand(z, z_cols.at[0], cells_of(far, z.cells))
    expand(z, z_cols.at[1], cells_of(near, z.cells))
    expand(z, z_cols.at[2], cells_of(beside, z.cells))
    for x in range(3):
        for e in range(3):
            z_turned[x, e] = z_cols[x, e].T
    turned[0] = z_turned[0, 0]
    turned[1] = z_turned[0, 1]
    turned[2] = z_turned[1, 0]

    def image_tile(y, c):
        total = None
        for inner in range(max(c - 1, y - 1, 1), min(c + 1, y + 1) + 1):
            term = dot(s_cols[inner - 1, y - inner + 1], z_cols[c - 1, inner - c + 1])
            total = term if total is None else total + term
        return total

    def turned_sum(i, c, rows):
        total = None
        for m in rows:
            term = dot(z_turned[i - 1, m - i + 1], image[c - 1, m])
            total = term if total is None else total + term
        return total

    p_part[0] = image_tile(0, 1)
    p_part[1] = image_tile(1, 1)
    for c, rows in ((1, (2, 3)), (2, (0, 1, 2, 3, 4)), (3, (1, 2, 3, 4))):
        for y in rows:
            image[c - 1, y] = image_tile(y, c).astype(kind)
    d_part[0] = turned_sum(1, 1, (2,))
    d_part[1] = turned_sum(2, 1, (2, 3))
    eye = identity(z)
    total = jnp.zeros((8, z.tile), jnp.float32)
    for i in (1, 2, 3):
        value = -turned_sum(i, 2, (i - 1, i, i + 1))
        if i == 2:
            value = eye + value
        value = own_masked(z, pattern, near_first, i - 1, value).astype(kind)
        d_near[i - 1] = value
        total = total + sum_squares(z, value)
    squares[...] = total

    def side_flag(t, u):
        o = offset_of(z, 0, t, u)
        inside = jnp.logical_and(o >= 0, o < z.offsets)
        back = jnp.clip(z.offsets - 1 - o, 0, z.offsets - 1)
        return jnp.logical_and(inside, pattern[near_first + u, back] != 0)

    d_beside[0] = masked(z, -turned_sum(2, 3, (1, 2, 3)), side_flag).astype(kind)
    value = eye - turned_sum(3, 3, (2, 3, 4))
    block = z.block
    per_block = block // FLAG_ROWS
    for t in range(z.half):
        for u in range(z.half):
            f = t * z.half + u
            low = f % per_block * FLAG_ROWS
            flags = beside[3 * z.cells + f // per_block, low : low + FLAG_ROWS]
            flag = flags.astype(jnp.float32)[:1]
            part = (slice(u * block, (u + 1) * block), slice(t * block, (t + 1) * block))
            d_beside[1, part[0], part[1]] = (value[part] * flag).astype(kind)

    factor = (None, z_cols.at[0], z_cols.at[1], z_cols.at[2])
    defect = (None, None, d_near, d_beside)
    for i in (1, 2, 3):
        base_near[i - 1] = z_cols[1, i - 1].astype(jnp.float32) + 0.5 * tile_product(
            factor, d_near, i, 2, 1, 3
        )
        e_near[i - 1] = tile_product(defect, d_near, i, 2, 2, 3)


def inner_step(z, pattern, near, far, beside):
    kind = near.dtype
    tile = z.tile
    return pl.pallas_call(
        functools.partial(inner_kernel, z),
        out_shape=(
            jax.ShapeDtypeStruct((3, 3, tile, tile), kind),
            z.tiles(3, kind),
            z.tiles(2, jnp.float32),
            z.tiles(2, jnp.float32),
            z.tiles(3, kind),
            jax.ShapeDtypeStruct((8, tile), jnp.float32),
            z.tiles(3, jnp.float32),
            z.tiles(3, jnp.float32),
        ),
        in_specs=[SMEM, VMEM, VMEM, VMEM],
        out_specs=(VMEM,) * 8,
        scratch_shapes=[
            pltpu.VMEM((4, 3, tile, tile), kind),
            pltpu.VMEM((3, 3, tile, tile), kind),
            pltpu.VMEM((3, 5, tile, tile), kind),
            pltpu.VMEM((2, tile, tile), kind),
        ],
        compiler_params=PARAMS,
        cost_estimate=z.cost(54, 8),
        name="inner",
    )(pattern, near, far, beside)


def outer_kernel(
    z, pattern, far, cross, z_cols, turned, p_part, d_part, squares, *refs
):
    d_far, d_out, z_far, all_squares, s_far = refs[-5:]
    _, far_first = half_starts(z)
    kind = far.dtype

    def factor_cell(t, o):
        value = far[z.cells + t * z.offsets + o]
        u = o + t - z.half
        if 0 <= u < z.half:
            value = value + cross[t, u]
        return value

    expand(z, s_far, lambda t, o: far[t * z.offsets + o])
    expand(z, z_far, factor_cell)
    link = z_cols[0, 0]
    image = (
        dot(s_far[0], link).astype(kind),
        (dot(s_far[1], link) + p_part[0]).astype(kind),
        (dot(s_far[2], link) + p_part[1]).astype(kind),
    )
    values = (
        -(dot(z_far[0].T, image[0]) + dot(z_far[1].T, image[1]) + dot(z_far[2].T, image[2])),
        identity(z) - (dot(turned[0], image[1]) + dot(turned[1], image[2]) + d_part[0]),
        -(dot(turned[2], image[2]) + d_part[1]),
    )
    total = squares[...]
    for e, value in enumerate(values):
        value = own_masked(z, pattern, far_first, e, value).astype(kind)
        d_far[e] = value
        if e < 2:
            d_out[e] = value
        total = total + sum_squares(z, value)
    all_squares[...] = total


def outer_step(z, pattern, far, cross, z_cols, turned, p_part, d_part, squares, held):
    kind = far.dtype
    return pl.pallas_call(
        functools.partial(outer_kernel, z),
        out_shape=(
            z.tiles(3, kind),
            z.tiles(2, kind),
            z.tiles(3, kind),
            jax.ShapeDtypeStruct(squares.shape, jnp.float32),
        ),
        in_specs=[SMEM] + [VMEM] * (7 + len(held)),
        out_specs=(VMEM,) * 4,
        scratch_shapes=[pltpu.VMEM((3, z.tile, z.tile), kind)],
        compiler_params=PARAMS,
        cost_estimate=z.cost(9, 4),
        name="outer",
    )(pattern, far, cross, z_cols, turned, p_part, d_part, squares, *held)


def middle_kernel(
    z, squares, z_cols, z_far, d_far, d_near, base_near, e_near, mask_near, refined, narrow, spread,
    square, tiles, cells, sems,
):
    near_first, _ = half_starts(z)
    moves = [
        (d_far, narrow.at[pl.ds(0, 3)]),
        (d_near.at[pl.ds(0, 2)], narrow.at[pl.ds(3, 2)]),
        (z_far.at[pl.ds(1, 2)], narrow.at[pl.ds(5, 2)]),
        (z_cols.at[0], narrow.at[pl.ds(7, 3)]),
        (z_cols.at[1, pl.ds(0, 2)], narrow.at[pl.ds(10, 2)]),
    ]
    copies = [
        pltpu.make_async_copy(source, target, sems.at[k]) for k, (source, target) in enumerate(moves)
    ]
    for copy in copies:
        copy.start()
    lanes = jnp.sum(squares[...], axis=0, keepdims=True)
    folded = lanes[:, : z.block]
    for t in range(1, z.half):
        folded = folded + lanes[:, t * z.block : (t + 1) * z.block]
    spread[...] = jnp.broadcast_to(folded[None], spread.shape)
    factor = (None, z_cols.at[0], z_cols.at[1], z_cols.at[2])
    for i in (1, 2, 3):
        value = e_near[i - 1]
        if i < 3:
            value = value + dot(d_far[i], d_near[0])
        square[i - 1] = (value * mask_near[i - 1].astype(jnp.float32)).astype(square.dtype)
    for i in (1, 2, 3):
        value = base_near[i - 1] + 0.375 * tile_product(factor, square, i, 2, 1, 3)
        tiles[i - 1] = value * mask_near[i - 1].astype(jnp.float32)
    store_half(z, tiles, cells)
    copies.append(
        pltpu.make_async_copy(cells, refined.at[pl.ds(near_first, z.half)], sems.at[len(moves)])
    )
    copies[-1].start()
    for copy in copies:
        copy.wait()


def middle_step(z, squares, z_cols, z_far, d_far, d_near, base_near, e_near, mask_near):
    kind = z_far.dtype
    shape = (z.columns, z.offsets, z.block, z.block)
    return pl.pallas_call(
        functools.partial(middle_kernel, z),
        out_shape=(
            jax.ShapeDtypeStruct(shape, kind),
            z.tiles(12, kind),
            jax.ShapeDtypeStruct((z.devices, 1, z.block), jnp.float32),
        ),
        in_specs=[VMEM] * 8,
        out_specs=(HBM, HBM, VMEM),
        scratch_shapes=[
            pltpu.VMEM((3, z.tile, z.tile), kind),
            pltpu.VMEM((3, z.tile, z.tile), jnp.float32),
            pltpu.VMEM((z.half,) + shape[1:], kind),
            pltpu.SemaphoreType.DMA((6,)),
        ],
        compiler_params=PARAMS,
        cost_estimate=z.cost(9, 6),
        name="middle",
    )(squares, z_cols, z_far, d_far, d_near, base_near, e_near, mask_near)


def last_kernel(
    z, pattern_in, narrow_in, d_in, _, refined, _narrow, _d, pattern, narrow, d_beyond, square, tiles,
    cells, sems,
):
    _, first = half_starts(z)
    moves = (
        (pattern_in, pattern),
        (d_in, d_beyond),
        (narrow_in.at[pl.ds(0, 5)], narrow.at[pl.ds(0, 5)]),
        (narrow_in.at[pl.ds(5, 7)], narrow.at[pl.ds(5, 7)]),
    )
    copies = [
        pltpu.make_async_copy(source, target, sems.at[k]) for k, (source, target) in enumerate(moves)
    ]
    for copy in copies:
        copy.start()
    for copy in copies[:3]:
        copy.wait()
    values = (
        dot(d_beyond[1], narrow[0]) + dot(narrow[0], narrow[1]),
        dot(d_beyond[0], narrow[0]) + dot(narrow[1], narrow[1]) + dot(narrow[3], narrow[2]),
        dot(narrow[2], narrow[1]) + dot(narrow[4], narrow[2]),
    )
    for i, value in enumerate(values):
        square[i] = own_masked(z, pattern, first, i, value).astype(square.dtype)
    copies[3].wait()
    base = (4, 7, 10)
    for i in (0, 1, 2):
        half = None
        rest = None
        for k in range(max(0, i - 1), min(2, i + 1) + 1):
            left = narrow[base[k] + i - k + 1]
            term = dot(left, narrow[k])
            half = term if half is None else half + term
            term = dot(left, square[k])
            rest = term if rest is None else rest + term
        value = narrow[7 + i].astype(jnp.float32) + 0.5 * half + 0.375 * rest
        tiles[i] = own_masked(z, pattern, first, i, value)
    store_half(z, tiles, cells)
    copy = pltpu.make_async_copy(cells, refined.at[pl.ds(first, z.half)], sems.at[4])
    copy.start()
    copy.wait()


def last_step(z, pattern, narrow, d_in, refined):
    kind = refined.dtype
    return pl.pallas_call(
        functools.partial(last_kernel, z),
        out_shape=tuple(
            jax.ShapeDtypeStruct(held.shape, held.dtype) for held in (refined, narrow, d_in)
        ),
        in_specs=[HBM] * 4,
        out_specs=(HBM,) * 3,
        scratch_shapes=[
            pltpu.SMEM(pattern.shape, pattern.dtype),
            pltpu.VMEM(narrow.shape, kind),
            pltpu.VMEM(d_in.shape, kind),
            pltpu.VMEM((3, z.tile, z.tile), kind),
            pltpu.VMEM((3, z.tile, z.tile), jnp.float32),
            pltpu.VMEM((z.half,) + refined.shape[1:], kind),
            pltpu.SemaphoreType.DMA((5,)),
        ],
        input_output_aliases={3: 0, 1: 1, 2: 2},
        compiler_params=PARAMS,
        cost_estimate=z.cost(21, 4),
        name="last",
    )(pattern, narrow, d_in, refined)


def norm_kernel(z, gathered, _, norm):
    mean = jnp.sum(gathered[...]) * (1.0 / z.entries)
    norm[...] = jnp.sqrt(jnp.full(norm.shape, mean, jnp.float32))


def norm_step(z, gathered, after):
    return pl.pallas_call(
        functools.partial(norm_kernel, z),
        out_shape=jax.ShapeDtypeStruct((1, z.block), jnp.float32),
        in_specs=[VMEM, HBM],
        out_specs=VMEM,
        compiler_params=PARAMS,
        name="norm",
    )(gathered, after)


def swaps(pairs):
    return [pair for i, j in pairs for pair in ((i, j), (j, i))]


def per_device(margin, factor, pattern):
    slabs = lax.axis_size("slab")
    devices = lax.axis_size("grp") * slabs
    z = Sizes(margin.shape, margin.shape[0] * slabs, devices)
    if slabs % 2 or z.columns != 2 * z.half:
        raise ValueError("sizes")
    near_pairs = [(i, i + 1) for i in range(0, devices - 1, 2)]
    far_pairs = [(i, i + 1) for i in range(1, devices - 1, 2)]
    inner_pairs = [(i, j) for i, j in far_pairs if j % slabs]
    cross_pairs = [(i, j) for i, j in far_pairs if not j % slabs]
    mask_near = masks(z, pattern, margin.dtype)
    near, far, cross = pack(z, margin, factor, pattern, mask_near)
    beyond = lax.ppermute(far, AXES, swaps(inner_pairs))
    across = lax.ppermute(cross, AXES, swaps(cross_pairs))
    beside = lax.ppermute(near, AXES, swaps(near_pairs))
    z_cols, turned, p_part, d_part, d_near, squares, base_near, e_near = inner_step(
        z, pattern, near, far, beside
    )
    held = (d_near, base_near, e_near, mask_near)
    d_far, d_out, z_far, squares = outer_step(
        z, pattern, beyond, across, z_cols, turned, p_part, d_part, squares, held
    )
    d_in = lax.ppermute(d_out, AXES, swaps(far_pairs))
    refined, narrow, spread = middle_step(
        z, squares, z_cols, z_far, d_far, d_near, base_near, e_near, mask_near
    )
    gathered = lax.all_to_all(spread, AXES, 0, 0, tiled=True)
    refined, narrow, _ = last_step(z, pattern, narrow, d_in, refined)
    norm = norm_step(z, gathered, narrow)
    return refined, norm[0, 0]


def solution(mesh):
    return jax.shard_map(
        per_device,
        mesh=mesh,
        in_specs=(
            P(AXES, None, None, None),
            P(AXES, None, None, None),
            P(AXES, None),
        ),
        out_specs=(P(AXES, None, None, None), P()),
        check_vma=False,
    )
```

```python
import functools

import jax
import jax.numpy as jnp
from jax import lax
from jax.experimental import pallas as pl
from jax.experimental.pallas import tpu as pltpu
from jax.sharding import PartitionSpec as P


AXES = ("grp", "slab")
HBM = pl.BlockSpec(memory_space=pltpu.HBM)
VMEM = pl.BlockSpec(memory_space=pltpu.VMEM)
SMEM = pl.BlockSpec(memory_space=pltpu.SMEM)
PARAMS = pltpu.CompilerParams(vmem_limit_bytes=32 * 1024 * 1024)
FLAG_ROWS = 16


class Sizes:
    def __init__(self, shape, quarter_len, devices):
        self.columns, self.offsets, self.block, _ = shape
        self.half = (self.offsets - 1) // 2
        self.tile = self.half * self.block
        self.cells = self.half * self.offsets
        self.flag_blocks = -(-self.half * self.half * FLAG_ROWS // self.block)
        self.quarter_len = quarter_len
        self.devices = devices
        self.entries = self.columns * devices * self.block

    def cost(self, products, moved):
        return pl.CostEstimate(
            flops=products * 2 * self.tile**3, bytes_accessed=moved * 2**20, transcendentals=0
        )

    def tiles(self, count, dtype):
        return jax.ShapeDtypeStruct((count, self.tile, self.tile), dtype)


def odd_device():
    return lax.rem(lax.axis_index("slab"), 2)


def half_starts(z):
    near = jnp.where(odd_device() == 1, 0, z.columns - z.half)
    return near, z.columns - z.half - near


def keep(flag, value):
    return jnp.where(flag, value, jnp.zeros_like(value))


def dot(left, right):
    return jnp.dot(left, right, preferred_element_type=jnp.float32)


def chain_tile(true_tile):
    return jnp.where(odd_device() == 1, 2 - true_tile, true_tile)


def expand(z, out, read):
    block = z.block
    for t in range(z.half):
        for a in range(3 * z.half):
            o = a - t
            u = a % z.half
            if 0 <= o < z.offsets:
                value = read(t, o)
            else:
                value = jnp.zeros((block, block), out.dtype)
            out[
                chain_tile(a // z.half),
                u * block : (u + 1) * block,
                t * block : (t + 1) * block,
            ] = value


def offset_of(z, e, t, u):
    return jnp.where(odd_device() == 1, 1 - e, e - 1) * z.half + u - t + z.half


def flag_of(z, pattern, first, e, t, u):
    o = offset_of(z, e, t, u)
    inside = jnp.logical_and(o >= 0, o < z.offsets)
    return jnp.logical_and(inside, pattern[first + t, jnp.clip(o, 0, z.offsets - 1)] != 0)


def masked(z, value, flag):
    block = z.block
    rows = []
    for u in range(z.half):
        rows.append(
            jnp.concatenate(
                [
                    keep(
                        flag(t, u),
                        value[u * block : (u + 1) * block, t * block : (t + 1) * block],
                    )
                    for t in range(z.half)
                ],
                axis=1,
            )
        )
    return jnp.concatenate(rows, axis=0)


def own_masked(z, pattern, first, e, value):
    return masked(z, value, lambda t, u: flag_of(z, pattern, first, e, t, u))


def identity(z):
    shape = (z.tile, z.tile)
    rows = lax.broadcasted_iota(jnp.int32, shape, 0)
    return (rows == lax.broadcasted_iota(jnp.int32, shape, 1)).astype(jnp.float32)


def tile_product(left, right, i, c, low, high):
    total = None
    for k in range(max(low, i - 1, c - 1), min(high, i + 1, c + 1) + 1):
        term = dot(left[k][i - k + 1], right[k - c + 1])
        total = term if total is None else total + term
    return total


def sum_squares(z, value):
    wide = value.astype(jnp.float32)
    return jnp.sum((wide * wide).reshape(-1, 8, z.tile), axis=0)


def store_half(z, tiles, cells):
    block = z.block
    for t in range(z.half):
        for o in range(z.offsets):
            a = t + o
            u = a % z.half
            value = tiles[
                chain_tile(a // z.half),
                u * block : (u + 1) * block,
                t * block : (t + 1) * block,
            ]
            cells[t, o] = value.astype(cells.dtype)


def mask_kernel(z, pattern, mask_near, mask_far):
    ones = jnp.ones((z.tile, z.tile), jnp.float32)
    for out, first in zip((mask_near, mask_far), half_starts(z)):
        for e in range(3):
            out[e] = own_masked(z, pattern, first, e, ones).astype(out.dtype)


def masks(z, pattern, kind):
    return pl.pallas_call(
        functools.partial(mask_kernel, z),
        out_shape=(z.tiles(3, kind), z.tiles(3, kind)),
        in_specs=[SMEM],
        out_specs=(VMEM, VMEM),
        compiler_params=PARAMS,
        cost_estimate=z.cost(20, 1),
        name="masks",
    )(pattern)


def pack_kernel(z, margin, factor, pattern, _near, _far, near, far, cross):
    near_first, far_first = half_starts(z)
    first_row = lax.axis_index("slab") * z.columns
    plan = ((margin, far_first), (factor, far_first), (margin, near_first), (factor, near_first))
    for k, (source, first) in enumerate(plan):
        for t in range(z.half):
            for o in range(z.offsets):
                flag = pattern[first + t, o] != 0
                if k % 2:
                    row = first_row + first + t + o - z.half
                    inside = jnp.logical_and(row >= 0, row < z.quarter_len)
                    flag = jnp.logical_and(flag, inside)
                value = keep(flag, source[first + t, o])
                cell = t * z.offsets + o
                u = o + t - z.half
                if k == 0:
                    far[cell] = value
                    near[2 * z.cells + cell] = value
                elif k == 1:
                    far[z.cells + cell] = value
                    if 0 <= u < z.half:
                        cross[t, u] = value
                else:
                    near[(k - 2) * z.cells + cell] = value
    per_block = z.block // FLAG_ROWS
    for f in range(z.flag_blocks * per_block):
        t, u = f // z.half, f % z.half
        value = jnp.zeros((FLAG_ROWS, z.block), near.dtype)
        if t < z.half:
            value = keep(pattern[near_first + t, u - t + z.half] != 0, jnp.ones_like(value))
        low = f % per_block * FLAG_ROWS
        near[3 * z.cells + f // per_block, low : low + FLAG_ROWS] = value


def pack(z, margin, factor, pattern, mask_near, mask_far):
    kind = margin.dtype
    return pl.pallas_call(
        functools.partial(pack_kernel, z),
        out_shape=(
            jax.ShapeDtypeStruct((3 * z.cells + z.flag_blocks, z.block, z.block), kind),
            jax.ShapeDtypeStruct((2 * z.cells, z.block, z.block), kind),
            jax.ShapeDtypeStruct((z.half, z.half, z.block, z.block), kind),
        ),
        in_specs=[VMEM, VMEM, SMEM, VMEM, VMEM],
        out_specs=(VMEM, VMEM, VMEM),
        compiler_params=PARAMS,
        name="pack",
    )(margin, factor, pattern, mask_near, mask_far)


def inner_kernel(
    z, pattern, near, far, beside, z_cols, turned, p_part, d_part, d_near, squares, base_near, e_near,
    s_cols, z_turned, image, d_beside,
):
    near_first, _ = half_starts(z)
    kind = near.dtype

    def cells_of(ref, base):
        return lambda t, o: ref[base + t * z.offsets + o]

    expand(z, s_cols.at[0], cells_of(far, 0))
    expand(z, s_cols.at[1], cells_of(near, 0))
    expand(z, s_cols.at[2], cells_of(beside, 0))
    expand(z, s_cols.at[3], cells_of(beside, 2 * z.cells))
    expand(z, z_cols.at[0], cells_of(far, z.cells))
    expand(z, z_cols.at[1], cells_of(near, z.cells))
    expand(z, z_cols.at[2], cells_of(beside, z.cells))
    for x in range(3):
        for e in range(3):
            z_turned[x, e] = z_cols[x, e].T
    turned[0] = z_turned[0, 0]
    turned[1] = z_turned[0, 1]
    turned[2] = z_turned[1, 0]

    def image_tile(y, c):
        total = None
        for inner in range(max(c - 1, y - 1, 1), min(c + 1, y + 1) + 1):
            term = dot(s_cols[inner - 1, y - inner + 1], z_cols[c - 1, inner - c + 1])
            total = term if total is None else total + term
        return total

    def turned_sum(i, c, rows):
        total = None
        for m in rows:
            term = dot(z_turned[i - 1, m - i + 1], image[c - 1, m])
            total = term if total is None else total + term
        return total

    p_part[0] = image_tile(0, 1)
    p_part[1] = image_tile(1, 1)
    for c, rows in ((1, (2, 3)), (2, (0, 1, 2, 3, 4)), (3, (1, 2, 3, 4))):
        for y in rows:
            image[c - 1, y] = image_tile(y, c).astype(kind)
    d_part[0] = turned_sum(1, 1, (2,))
    d_part[1] = turned_sum(2, 1, (2, 3))
    eye = identity(z)
    total = jnp.zeros((8, z.tile), jnp.float32)
    for i in (1, 2, 3):
        value = -turned_sum(i, 2, (i - 1, i, i + 1))
        if i == 2:
            value = eye + value
        value = own_masked(z, pattern, near_first, i - 1, value).astype(kind)
        d_near[i - 1] = value
        total = total + sum_squares(z, value)
    squares[...] = total

    def side_flag(t, u):
        o = offset_of(z, 0, t, u)
        inside = jnp.logical_and(o >= 0, o < z.offsets)
        back = jnp.clip(z.offsets - 1 - o, 0, z.offsets - 1)
        return jnp.logical_and(inside, pattern[near_first + u, back] != 0)

    d_beside[0] = masked(z, -turned_sum(2, 3, (1, 2, 3)), side_flag).astype(kind)
    value = eye - turned_sum(3, 3, (2, 3, 4))
    block = z.block
    per_block = block // FLAG_ROWS
    for t in range(z.half):
        for u in range(z.half):
            f = t * z.half + u
            low = f % per_block * FLAG_ROWS
            flags = beside[3 * z.cells + f // per_block, low : low + FLAG_ROWS]
            flag = flags.astype(jnp.float32)[:1]
            part = (slice(u * block, (u + 1) * block), slice(t * block, (t + 1) * block))
            d_beside[1, part[0], part[1]] = (value[part] * flag).astype(kind)

    factor = (None, z_cols.at[0], z_cols.at[1], z_cols.at[2])
    defect = (None, None, d_near, d_beside)
    for i in (1, 2, 3):
        base_near[i - 1] = z_cols[1, i - 1].astype(jnp.float32) + 0.5 * tile_product(
            factor, d_near, i, 2, 1, 3
        )
        e_near[i - 1] = tile_product(defect, d_near, i, 2, 2, 3)


def inner_step(z, pattern, near, far, beside):
    kind = near.dtype
    tile = z.tile
    return pl.pallas_call(
        functools.partial(inner_kernel, z),
        out_shape=(
            jax.ShapeDtypeStruct((3, 3, tile, tile), kind),
            z.tiles(3, kind),
            z.tiles(2, jnp.float32),
            z.tiles(2, jnp.float32),
            z.tiles(3, kind),
            jax.ShapeDtypeStruct((8, tile), jnp.float32),
            z.tiles(3, jnp.float32),
            z.tiles(3, jnp.float32),
        ),
        in_specs=[SMEM, VMEM, VMEM, VMEM],
        out_specs=(VMEM,) * 8,
        scratch_shapes=[
            pltpu.VMEM((4, 3, tile, tile), kind),
            pltpu.VMEM((3, 3, tile, tile), kind),
            pltpu.VMEM((3, 5, tile, tile), kind),
            pltpu.VMEM((2, tile, tile), kind),
        ],
        compiler_params=PARAMS,
        cost_estimate=z.cost(54, 8),
        name="inner",
    )(pattern, near, far, beside)


def outer_kernel(
    z, pattern, far, cross, z_cols, turned, p_part, d_part, squares, *refs
):
    d_far, d_out, z_far, all_squares, s_far = refs[-5:]
    _, far_first = half_starts(z)
    kind = far.dtype

    def factor_cell(t, o):
        value = far[z.cells + t * z.offsets + o]
        u = o + t - z.half
        if 0 <= u < z.half:
            value = value + cross[t, u]
        return value

    expand(z, s_far, lambda t, o: far[t * z.offsets + o])
    expand(z, z_far, factor_cell)
    link = z_cols[0, 0]
    image = (
        dot(s_far[0], link).astype(kind),
        (dot(s_far[1], link) + p_part[0]).astype(kind),
        (dot(s_far[2], link) + p_part[1]).astype(kind),
    )
    values = (
        -(dot(z_far[0].T, image[0]) + dot(z_far[1].T, image[1]) + dot(z_far[2].T, image[2])),
        identity(z) - (dot(turned[0], image[1]) + dot(turned[1], image[2]) + d_part[0]),
        -(dot(turned[2], image[2]) + d_part[1]),
    )
    total = squares[...]
    for e, value in enumerate(values):
        value = own_masked(z, pattern, far_first, e, value).astype(kind)
        d_far[e] = value
        if e < 2:
            d_out[e] = value
        total = total + sum_squares(z, value)
    lanes = jnp.sum(total, axis=0, keepdims=True)
    folded = lanes[:, : z.block]
    for t in range(1, z.half):
        folded = folded + lanes[:, t * z.block : (t + 1) * z.block]
    all_squares[...] = folded


def outer_step(z, pattern, far, cross, z_cols, turned, p_part, d_part, squares, held):
    kind = far.dtype
    return pl.pallas_call(
        functools.partial(outer_kernel, z),
        out_shape=(
            z.tiles(3, kind),
            z.tiles(2, kind),
            z.tiles(3, kind),
            jax.ShapeDtypeStruct((1, z.block), jnp.float32),
        ),
        in_specs=[SMEM] + [VMEM] * (7 + len(held)),
        out_specs=(VMEM,) * 4,
        scratch_shapes=[pltpu.VMEM((3, z.tile, z.tile), kind)],
        compiler_params=PARAMS,
        cost_estimate=z.cost(9, 4),
        name="outer",
    )(pattern, far, cross, z_cols, turned, p_part, d_part, squares, *held)


def middle_kernel(
    z, z_cols, z_far, d_far, d_near, base_near, e_near, mask_near, refined, base, e_part, square, tiles,
    cells, sem,
):
    near_first, _ = half_starts(z)
    factor = (z_far, z_cols.at[0], z_cols.at[1], z_cols.at[2])
    defect = (None, d_far, d_near)
    for i in (1, 2, 3):
        value = e_near[i - 1]
        if i < 3:
            value = value + dot(d_far[i], d_near[0])
        square[i - 1] = (value * mask_near[i - 1].astype(jnp.float32)).astype(square.dtype)
    for i in (1, 2, 3):
        value = base_near[i - 1] + 0.375 * tile_product(factor, square, i, 2, 1, 3)
        tiles[i - 1] = value * mask_near[i - 1].astype(jnp.float32)
    store_half(z, tiles, cells)
    copy = pltpu.make_async_copy(cells, refined.at[pl.ds(near_first, z.half)], sem)
    copy.start()
    for i in (0, 1, 2):
        base[i] = z_cols[0, i].astype(jnp.float32) + 0.5 * tile_product(factor, d_far, i, 1, 0, 2)
        e_part[i] = tile_product(defect, d_far, i, 1, 1, 2)
    copy.wait()


def middle_step(z, z_cols, z_far, d_far, d_near, base_near, e_near, mask_near):
    kind = z_far.dtype
    shape = (z.columns, z.offsets, z.block, z.block)
    return pl.pallas_call(
        functools.partial(middle_kernel, z),
        out_shape=(
            jax.ShapeDtypeStruct(shape, kind),
            z.tiles(3, jnp.float32),
            z.tiles(3, jnp.float32),
        ),
        in_specs=[VMEM] * 7,
        out_specs=(HBM, VMEM, VMEM),
        scratch_shapes=[
            pltpu.VMEM((3, z.tile, z.tile), kind),
            pltpu.VMEM((3, z.tile, z.tile), jnp.float32),
            pltpu.VMEM((z.half,) + shape[1:], kind),
            pltpu.SemaphoreType.DMA(()),
        ],
        compiler_params=PARAMS,
        cost_estimate=z.cost(21, 6),
        name="middle",
    )(z_cols, z_far, d_far, d_near, base_near, e_near, mask_near)


def last_kernel(
    z, z_cols, z_far, d_far, d_in, base, e_part, mask_far, _, refined, square, tiles, cells, sem
):
    _, far_first = half_starts(z)
    factor = (z_far, z_cols.at[0], z_cols.at[1])
    values = (
        e_part[0] + dot(d_in[1], d_far[0]),
        e_part[1] + dot(d_in[0], d_far[0]),
        e_part[2],
    )
    for i, value in enumerate(values):
        square[i] = (value * mask_far[i].astype(jnp.float32)).astype(square.dtype)
    for i in (0, 1, 2):
        value = base[i] + 0.375 * tile_product(factor, square, i, 1, 0, 2)
        tiles[i] = value * mask_far[i].astype(jnp.float32)
    store_half(z, tiles, cells)
    copy = pltpu.make_async_copy(cells, refined.at[pl.ds(far_first, z.half)], sem)
    copy.start()
    copy.wait()


def last_step(z, z_cols, z_far, d_far, d_in, base, e_part, mask_far, refined):
    kind = refined.dtype
    return pl.pallas_call(
        functools.partial(last_kernel, z),
        out_shape=jax.ShapeDtypeStruct(refined.shape, kind),
        in_specs=[VMEM] * 7 + [HBM],
        out_specs=HBM,
        scratch_shapes=[
            pltpu.VMEM((3, z.tile, z.tile), kind),
            pltpu.VMEM((3, z.tile, z.tile), jnp.float32),
            pltpu.VMEM((z.half,) + refined.shape[1:], kind),
            pltpu.SemaphoreType.DMA(()),
        ],
        input_output_aliases={7: 0},
        compiler_params=PARAMS,
        cost_estimate=z.cost(9, 4),
        name="last",
    )(z_cols, z_far, d_far, d_in, base, e_part, mask_far, refined)


def norm_kernel(z, gathered, _, norm, _held, cells, sem):
    copy = pltpu.make_async_copy(gathered, cells, sem)
    copy.start()
    copy.wait()
    mean = jnp.sum(cells[...]) * (1.0 / z.entries)
    norm[...] = jnp.sqrt(jnp.full(norm.shape, mean, jnp.float32))


def norm_step(z, gathered, after):
    return pl.pallas_call(
        functools.partial(norm_kernel, z),
        out_shape=(
            jax.ShapeDtypeStruct((1, z.block), jnp.float32),
            jax.ShapeDtypeStruct(gathered.shape, gathered.dtype),
        ),
        in_specs=[HBM, HBM],
        out_specs=(VMEM, HBM),
        scratch_shapes=[
            pltpu.VMEM(gathered.shape, gathered.dtype),
            pltpu.SemaphoreType.DMA(()),
        ],
        input_output_aliases={0: 1},
        compiler_params=PARAMS,
        name="norm",
    )(gathered, after)[0]


def swaps(pairs):
    return [pair for i, j in pairs for pair in ((i, j), (j, i))]


def per_device(margin, factor, pattern):
    slabs = lax.axis_size("slab")
    devices = lax.axis_size("grp") * slabs
    z = Sizes(margin.shape, margin.shape[0] * slabs, devices)
    if slabs % 2 or z.columns != 2 * z.half:
        raise ValueError("sizes")
    near_pairs = [(i, i + 1) for i in range(0, devices - 1, 2)]
    far_pairs = [(i, i + 1) for i in range(1, devices - 1, 2)]
    inner_pairs = [(i, j) for i, j in far_pairs if j % slabs]
    cross_pairs = [(i, j) for i, j in far_pairs if not j % slabs]
    mask_near, mask_far = masks(z, pattern, margin.dtype)
    near, far, cross = pack(z, margin, factor, pattern, mask_near, mask_far)
    beyond = lax.ppermute(far, AXES, swaps(inner_pairs))
    across = lax.ppermute(cross, AXES, swaps(cross_pairs))
    beside = lax.ppermute(near, AXES, swaps(near_pairs))
    z_cols, turned, p_part, d_part, d_near, squares, base_near, e_near = inner_step(
        z, pattern, near, far, beside
    )
    held = (d_near, base_near, e_near, mask_near, mask_far)
    d_far, d_out, z_far, squares = outer_step(
        z, pattern, beyond, across, z_cols, turned, p_part, d_part, squares, held
    )
    gathered = lax.all_gather(squares, AXES, axis=0, tiled=True)
    d_in = lax.ppermute(d_out, AXES, swaps(far_pairs))
    refined, base, e_part = middle_step(
        z, z_cols, z_far, d_far, d_near, base_near, e_near, mask_near
    )
    refined = last_step(z, z_cols, z_far, d_far, d_in, base, e_part, mask_far, refined)
    norm = norm_step(z, gathered, refined)
    return refined, norm[0, 0]


def solution(mesh):
    return jax.shard_map(
        per_device,
        mesh=mesh,
        in_specs=(
            P(AXES, None, None, None),
            P(AXES, None, None, None),
            P(AXES, None),
        ),
        out_specs=(P(AXES, None, None, None), P()),
        check_vma=False,
    )
```

```python
import functools

import jax
import jax.numpy as jnp
from jax import lax
from jax.experimental import pallas as pl
from jax.experimental.pallas import tpu as pltpu
from jax.sharding import PartitionSpec as P


AXES = ("grp", "slab")
HBM = pl.BlockSpec(memory_space=pltpu.HBM)
VMEM = pl.BlockSpec(memory_space=pltpu.VMEM)
SMEM = pl.BlockSpec(memory_space=pltpu.SMEM)
PARAMS = pltpu.CompilerParams(vmem_limit_bytes=32 * 1024 * 1024)
FLAG_ROWS = 16


class Sizes:
    def __init__(self, shape, quarter_len, devices):
        self.columns, self.offsets, self.block, _ = shape
        self.half = (self.offsets - 1) // 2
        self.tile = self.half * self.block
        self.cells = self.half * self.offsets
        self.flag_blocks = -(-self.half * self.half * FLAG_ROWS // self.block)
        self.quarter_len = quarter_len
        self.devices = devices
        self.entries = self.columns * devices * self.block

    def cost(self, products, moved):
        return pl.CostEstimate(
            flops=products * 2 * self.tile**3, bytes_accessed=moved * 2**20, transcendentals=0
        )

    def tiles(self, count, dtype):
        return jax.ShapeDtypeStruct((count, self.tile, self.tile), dtype)


def odd_device():
    return lax.rem(lax.axis_index("slab"), 2)


def half_starts(z):
    near = jnp.where(odd_device() == 1, 0, z.columns - z.half)
    return near, z.columns - z.half - near


def keep(flag, value):
    return jnp.where(flag, value, jnp.zeros_like(value))


def dot(left, right):
    return jnp.dot(left, right, preferred_element_type=jnp.float32)


def chain_tile(true_tile):
    return jnp.where(odd_device() == 1, 2 - true_tile, true_tile)


def expand(z, out, read):
    block = z.block
    for t in range(z.half):
        for a in range(3 * z.half):
            o = a - t
            u = a % z.half
            if 0 <= o < z.offsets:
                value = read(t, o)
            else:
                value = jnp.zeros((block, block), out.dtype)
            out[
                chain_tile(a // z.half),
                u * block : (u + 1) * block,
                t * block : (t + 1) * block,
            ] = value


def offset_of(z, e, t, u):
    return jnp.where(odd_device() == 1, 1 - e, e - 1) * z.half + u - t + z.half


def flag_of(z, pattern, first, e, t, u):
    o = offset_of(z, e, t, u)
    inside = jnp.logical_and(o >= 0, o < z.offsets)
    return jnp.logical_and(inside, pattern[first + t, jnp.clip(o, 0, z.offsets - 1)] != 0)


def masked(z, value, flag):
    block = z.block
    rows = []
    for u in range(z.half):
        rows.append(
            jnp.concatenate(
                [
                    keep(
                        flag(t, u),
                        value[u * block : (u + 1) * block, t * block : (t + 1) * block],
                    )
                    for t in range(z.half)
                ],
                axis=1,
            )
        )
    return jnp.concatenate(rows, axis=0)


def own_masked(z, pattern, first, e, value):
    return masked(z, value, lambda t, u: flag_of(z, pattern, first, e, t, u))


def identity(z):
    shape = (z.tile, z.tile)
    rows = lax.broadcasted_iota(jnp.int32, shape, 0)
    return (rows == lax.broadcasted_iota(jnp.int32, shape, 1)).astype(jnp.float32)


def tile_product(left, right, i, c, low, high):
    total = None
    for k in range(max(low, i - 1, c - 1), min(high, i + 1, c + 1) + 1):
        term = dot(left[k][i - k + 1], right[k - c + 1])
        total = term if total is None else total + term
    return total


def sum_squares(z, value):
    wide = value.astype(jnp.float32)
    return jnp.sum((wide * wide).reshape(-1, 8, z.tile), axis=0)


def store_half(z, tiles, cells):
    block = z.block
    for t in range(z.half):
        for o in range(z.offsets):
            a = t + o
            u = a % z.half
            value = tiles[
                chain_tile(a // z.half),
                u * block : (u + 1) * block,
                t * block : (t + 1) * block,
            ]
            cells[t, o] = value.astype(cells.dtype)


def mask_kernel(z, pattern, mask_near):
    first, _ = half_starts(z)
    ones = jnp.ones((z.tile, z.tile), jnp.float32)
    for e in range(3):
        mask_near[e] = own_masked(z, pattern, first, e, ones).astype(mask_near.dtype)


def masks(z, pattern, kind):
    return pl.pallas_call(
        functools.partial(mask_kernel, z),
        out_shape=z.tiles(3, kind),
        in_specs=[SMEM],
        out_specs=VMEM,
        compiler_params=PARAMS,
        cost_estimate=z.cost(20, 1),
        name="masks",
    )(pattern)


def pack_kernel(z, margin, factor, pattern, _, near, far, cross):
    near_first, far_first = half_starts(z)
    first_row = lax.axis_index("slab") * z.columns
    plan = ((margin, far_first), (factor, far_first), (margin, near_first), (factor, near_first))
    for k, (source, first) in enumerate(plan):
        for t in range(z.half):
            for o in range(z.offsets):
                flag = pattern[first + t, o] != 0
                if k % 2:
                    row = first_row + first + t + o - z.half
                    inside = jnp.logical_and(row >= 0, row < z.quarter_len)
                    flag = jnp.logical_and(flag, inside)
                value = keep(flag, source[first + t, o])
                cell = t * z.offsets + o
                u = o + t - z.half
                if k == 0:
                    far[cell] = value
                    near[2 * z.cells + cell] = value
                elif k == 1:
                    far[z.cells + cell] = value
                    if 0 <= u < z.half:
                        cross[t, u] = value
                else:
                    near[(k - 2) * z.cells + cell] = value
    per_block = z.block // FLAG_ROWS
    for f in range(z.flag_blocks * per_block):
        t, u = f // z.half, f % z.half
        value = jnp.zeros((FLAG_ROWS, z.block), near.dtype)
        if t < z.half:
            value = keep(pattern[near_first + t, u - t + z.half] != 0, jnp.ones_like(value))
        low = f % per_block * FLAG_ROWS
        near[3 * z.cells + f // per_block, low : low + FLAG_ROWS] = value


def pack(z, margin, factor, pattern, mask_near):
    kind = margin.dtype
    return pl.pallas_call(
        functools.partial(pack_kernel, z),
        out_shape=(
            jax.ShapeDtypeStruct((3 * z.cells + z.flag_blocks, z.block, z.block), kind),
            jax.ShapeDtypeStruct((2 * z.cells, z.block, z.block), kind),
            jax.ShapeDtypeStruct((z.half, z.half, z.block, z.block), kind),
        ),
        in_specs=[VMEM, VMEM, SMEM, VMEM],
        out_specs=(VMEM, VMEM, VMEM),
        compiler_params=PARAMS,
        name="pack",
    )(margin, factor, pattern, mask_near)


def inner_kernel(
    z, pattern, near, far, beside, z_cols, turned, p_part, d_part, d_near, squares, base_near, e_near,
    s_cols, z_turned, image, d_beside,
):
    near_first, _ = half_starts(z)
    kind = near.dtype

    def cells_of(ref, base):
        return lambda t, o: ref[base + t * z.offsets + o]

    expand(z, s_cols.at[0], cells_of(far, 0))
    expand(z, s_cols.at[1], cells_of(near, 0))
    expand(z, s_cols.at[2], cells_of(beside, 0))
    expand(z, s_cols.at[3], cells_of(beside, 2 * z.cells))
    expand(z, z_cols.at[0], cells_of(far, z.cells))
    expand(z, z_cols.at[1], cells_of(near, z.cells))
    expand(z, z_cols.at[2], cells_of(beside, z.cells))
    for x in range(3):
        for e in range(3):
            z_turned[x, e] = z_cols[x, e].T
    turned[0] = z_turned[0, 0]
    turned[1] = z_turned[0, 1]
    turned[2] = z_turned[1, 0]

    def image_tile(y, c):
        total = None
        for inner in range(max(c - 1, y - 1, 1), min(c + 1, y + 1) + 1):
            term = dot(s_cols[inner - 1, y - inner + 1], z_cols[c - 1, inner - c + 1])
            total = term if total is None else total + term
        return total

    def turned_sum(i, c, rows):
        total = None
        for m in rows:
            term = dot(z_turned[i - 1, m - i + 1], image[c - 1, m])
            total = term if total is None else total + term
        return total

    p_part[0] = image_tile(0, 1)
    p_part[1] = image_tile(1, 1)
    for c, rows in ((1, (2, 3)), (2, (0, 1, 2, 3, 4)), (3, (1, 2, 3, 4))):
        for y in rows:
            image[c - 1, y] = image_tile(y, c).astype(kind)
    d_part[0] = turned_sum(1, 1, (2,))
    d_part[1] = turned_sum(2, 1, (2, 3))
    eye = identity(z)
    total = jnp.zeros((8, z.tile), jnp.float32)
    for i in (1, 2, 3):
        value = -turned_sum(i, 2, (i - 1, i, i + 1))
        if i == 2:
            value = eye + value
        value = own_masked(z, pattern, near_first, i - 1, value).astype(kind)
        d_near[i - 1] = value
        total = total + sum_squares(z, value)
    squares[...] = total

    def side_flag(t, u):
        o = offset_of(z, 0, t, u)
        inside = jnp.logical_and(o >= 0, o < z.offsets)
        back = jnp.clip(z.offsets - 1 - o, 0, z.offsets - 1)
        return jnp.logical_and(inside, pattern[near_first + u, back] != 0)

    d_beside[0] = masked(z, -turned_sum(2, 3, (1, 2, 3)), side_flag).astype(kind)
    value = eye - turned_sum(3, 3, (2, 3, 4))
    block = z.block
    per_block = block // FLAG_ROWS
    for t in range(z.half):
        for u in range(z.half):
            f = t * z.half + u
            low = f % per_block * FLAG_ROWS
            flags = beside[3 * z.cells + f // per_block, low : low + FLAG_ROWS]
            flag = flags.astype(jnp.float32)[:1]
            part = (slice(u * block, (u + 1) * block), slice(t * block, (t + 1) * block))
            d_beside[1, part[0], part[1]] = (value[part] * flag).astype(kind)

    factor = (None, z_cols.at[0], z_cols.at[1], z_cols.at[2])
    defect = (None, None, d_near, d_beside)
    for i in (1, 2, 3):
        base_near[i - 1] = z_cols[1, i - 1].astype(jnp.float32) + 0.5 * tile_product(
            factor, d_near, i, 2, 1, 3
        )
        e_near[i - 1] = tile_product(defect, d_near, i, 2, 2, 3)


def inner_step(z, pattern, near, far, beside):
    kind = near.dtype
    tile = z.tile
    return pl.pallas_call(
        functools.partial(inner_kernel, z),
        out_shape=(
            jax.ShapeDtypeStruct((3, 3, tile, tile), kind),
            z.tiles(3, kind),
            z.tiles(2, jnp.float32),
            z.tiles(2, jnp.float32),
            z.tiles(3, kind),
            jax.ShapeDtypeStruct((8, tile), jnp.float32),
            z.tiles(3, jnp.float32),
            z.tiles(3, jnp.float32),
        ),
        in_specs=[SMEM, VMEM, VMEM, VMEM],
        out_specs=(VMEM,) * 8,
        scratch_shapes=[
            pltpu.VMEM((4, 3, tile, tile), kind),
            pltpu.VMEM((3, 3, tile, tile), kind),
            pltpu.VMEM((3, 5, tile, tile), kind),
            pltpu.VMEM((2, tile, tile), kind),
        ],
        compiler_params=PARAMS,
        cost_estimate=z.cost(54, 8),
        name="inner",
    )(pattern, near, far, beside)


def outer_kernel(
    z, pattern, far, cross, z_cols, turned, p_part, d_part, squares, *refs
):
    d_far, d_out, z_far, all_squares, s_far = refs[-5:]
    _, far_first = half_starts(z)
    kind = far.dtype

    def factor_cell(t, o):
        value = far[z.cells + t * z.offsets + o]
        u = o + t - z.half
        if 0 <= u < z.half:
            value = value + cross[t, u]
        return value

    expand(z, s_far, lambda t, o: far[t * z.offsets + o])
    expand(z, z_far, factor_cell)
    link = z_cols[0, 0]
    image = (
        dot(s_far[0], link).astype(kind),
        (dot(s_far[1], link) + p_part[0]).astype(kind),
        (dot(s_far[2], link) + p_part[1]).astype(kind),
    )
    values = (
        -(dot(z_far[0].T, image[0]) + dot(z_far[1].T, image[1]) + dot(z_far[2].T, image[2])),
        identity(z) - (dot(turned[0], image[1]) + dot(turned[1], image[2]) + d_part[0]),
        -(dot(turned[2], image[2]) + d_part[1]),
    )
    total = squares[...]
    for e, value in enumerate(values):
        value = own_masked(z, pattern, far_first, e, value).astype(kind)
        d_far[e] = value
        if e < 2:
            d_out[e] = value
        total = total + sum_squares(z, value)
    lanes = jnp.sum(total, axis=0, keepdims=True)
    folded = lanes[:, : z.block]
    for t in range(1, z.half):
        folded = folded + lanes[:, t * z.block : (t + 1) * z.block]
    all_squares[...] = folded


def outer_step(z, pattern, far, cross, z_cols, turned, p_part, d_part, squares, held):
    kind = far.dtype
    return pl.pallas_call(
        functools.partial(outer_kernel, z),
        out_shape=(
            z.tiles(3, kind),
            z.tiles(2, kind),
            z.tiles(3, kind),
            jax.ShapeDtypeStruct((1, z.block), jnp.float32),
        ),
        in_specs=[SMEM] + [VMEM] * (7 + len(held)),
        out_specs=(VMEM,) * 4,
        scratch_shapes=[pltpu.VMEM((3, z.tile, z.tile), kind)],
        compiler_params=PARAMS,
        cost_estimate=z.cost(9, 4),
        name="outer",
    )(pattern, far, cross, z_cols, turned, p_part, d_part, squares, *held)


def middle_kernel(
    z, squares, squares_beside, z_cols, z_far, d_far, d_near, base_near, e_near, mask_near, refined,
    narrow, spread, square, tiles, cells, sems,
):
    near_first, _ = half_starts(z)
    moves = [
        (d_far, narrow.at[pl.ds(0, 3)]),
        (d_near.at[pl.ds(0, 2)], narrow.at[pl.ds(3, 2)]),
        (z_far.at[pl.ds(1, 2)], narrow.at[pl.ds(5, 2)]),
        (z_cols.at[0], narrow.at[pl.ds(7, 3)]),
        (z_cols.at[1, pl.ds(0, 2)], narrow.at[pl.ds(10, 2)]),
    ]
    copies = [
        pltpu.make_async_copy(source, target, sems.at[k]) for k, (source, target) in enumerate(moves)
    ]
    for copy in copies:
        copy.start()
    both = squares[...] + squares_beside[...]
    spread[...] = jnp.broadcast_to(both[None], spread.shape)
    factor = (None, z_cols.at[0], z_cols.at[1], z_cols.at[2])
    for i in (1, 2, 3):
        value = e_near[i - 1]
        if i < 3:
            value = value + dot(d_far[i], d_near[0])
        square[i - 1] = (value * mask_near[i - 1].astype(jnp.float32)).astype(square.dtype)
    for i in (1, 2, 3):
        value = base_near[i - 1] + 0.375 * tile_product(factor, square, i, 2, 1, 3)
        tiles[i - 1] = value * mask_near[i - 1].astype(jnp.float32)
    store_half(z, tiles, cells)
    copies.append(
        pltpu.make_async_copy(cells, refined.at[pl.ds(near_first, z.half)], sems.at[len(moves)])
    )
    copies[-1].start()
    for copy in copies:
        copy.wait()


def middle_step(
    z, squares, squares_beside, z_cols, z_far, d_far, d_near, base_near, e_near, mask_near
):
    kind = z_far.dtype
    shape = (z.columns, z.offsets, z.block, z.block)
    return pl.pallas_call(
        functools.partial(middle_kernel, z),
        out_shape=(
            jax.ShapeDtypeStruct(shape, kind),
            z.tiles(12, kind),
            jax.ShapeDtypeStruct((z.devices // 2, 1, z.block), jnp.float32),
        ),
        in_specs=[VMEM] * 9,
        out_specs=(HBM, HBM, VMEM),
        scratch_shapes=[
            pltpu.VMEM((3, z.tile, z.tile), kind),
            pltpu.VMEM((3, z.tile, z.tile), jnp.float32),
            pltpu.VMEM((z.half,) + shape[1:], kind),
            pltpu.SemaphoreType.DMA((6,)),
        ],
        compiler_params=PARAMS,
        cost_estimate=z.cost(9, 6),
        name="middle",
    )(squares, squares_beside, z_cols, z_far, d_far, d_near, base_near, e_near, mask_near)


def last_kernel(
    z, pattern_in, narrow_in, d_in, _, refined, _narrow, _d, pattern, narrow, d_beyond, square, tiles,
    cells, sems,
):
    _, first = half_starts(z)
    moves = (
        (pattern_in, pattern),
        (d_in, d_beyond),
        (narrow_in.at[pl.ds(0, 5)], narrow.at[pl.ds(0, 5)]),
        (narrow_in.at[pl.ds(5, 7)], narrow.at[pl.ds(5, 7)]),
    )
    copies = [
        pltpu.make_async_copy(source, target, sems.at[k]) for k, (source, target) in enumerate(moves)
    ]
    for copy in copies:
        copy.start()
    for copy in copies[:3]:
        copy.wait()
    values = (
        dot(d_beyond[1], narrow[0]) + dot(narrow[0], narrow[1]),
        dot(d_beyond[0], narrow[0]) + dot(narrow[1], narrow[1]) + dot(narrow[3], narrow[2]),
        dot(narrow[2], narrow[1]) + dot(narrow[4], narrow[2]),
    )
    for i, value in enumerate(values):
        square[i] = own_masked(z, pattern, first, i, value).astype(square.dtype)
    copies[3].wait()
    base = (4, 7, 10)
    for i in (0, 1, 2):
        half = None
        rest = None
        for k in range(max(0, i - 1), min(2, i + 1) + 1):
            left = narrow[base[k] + i - k + 1]
            term = dot(left, narrow[k])
            half = term if half is None else half + term
            term = dot(left, square[k])
            rest = term if rest is None else rest + term
        value = narrow[7 + i].astype(jnp.float32) + 0.5 * half + 0.375 * rest
        tiles[i] = own_masked(z, pattern, first, i, value)
    store_half(z, tiles, cells)
    copy = pltpu.make_async_copy(cells, refined.at[pl.ds(first, z.half)], sems.at[4])
    copy.start()
    copy.wait()


def last_step(z, pattern, narrow, d_in, refined):
    kind = refined.dtype
    return pl.pallas_call(
        functools.partial(last_kernel, z),
        out_shape=tuple(
            jax.ShapeDtypeStruct(held.shape, held.dtype) for held in (refined, narrow, d_in)
        ),
        in_specs=[HBM] * 4,
        out_specs=(HBM,) * 3,
        scratch_shapes=[
            pltpu.SMEM(pattern.shape, pattern.dtype),
            pltpu.VMEM(narrow.shape, kind),
            pltpu.VMEM(d_in.shape, kind),
            pltpu.VMEM((3, z.tile, z.tile), kind),
            pltpu.VMEM((3, z.tile, z.tile), jnp.float32),
            pltpu.VMEM((z.half,) + refined.shape[1:], kind),
            pltpu.SemaphoreType.DMA((5,)),
        ],
        input_output_aliases={3: 0, 1: 1, 2: 2},
        compiler_params=PARAMS,
        cost_estimate=z.cost(21, 4),
        name="last",
    )(pattern, narrow, d_in, refined)


def norm_kernel(z, gathered, _, norm):
    mean = jnp.sum(gathered[...]) * (1.0 / z.entries)
    norm[...] = jnp.sqrt(jnp.full(norm.shape, mean, jnp.float32))


def norm_step(z, gathered, after):
    return pl.pallas_call(
        functools.partial(norm_kernel, z),
        out_shape=jax.ShapeDtypeStruct((1, z.block), jnp.float32),
        in_specs=[VMEM, HBM],
        out_specs=VMEM,
        compiler_params=PARAMS,
        name="norm",
    )(gathered, after)


def swaps(pairs):
    return [pair for i, j in pairs for pair in ((i, j), (j, i))]


def per_device(margin, factor, pattern):
    slabs = lax.axis_size("slab")
    devices = lax.axis_size("grp") * slabs
    z = Sizes(margin.shape, margin.shape[0] * slabs, devices)
    if slabs % 2 or z.columns != 2 * z.half:
        raise ValueError("sizes")
    near_pairs = [(i, i + 1) for i in range(0, devices - 1, 2)]
    far_pairs = [(i, i + 1) for i in range(1, devices - 1, 2)]
    inner_pairs = [(i, j) for i, j in far_pairs if j % slabs]
    cross_pairs = [(i, j) for i, j in far_pairs if not j % slabs]
    mask_near = masks(z, pattern, margin.dtype)
    near, far, cross = pack(z, margin, factor, pattern, mask_near)
    beyond = lax.ppermute(far, AXES, swaps(inner_pairs))
    across = lax.ppermute(cross, AXES, swaps(cross_pairs))
    beside = lax.ppermute(near, AXES, swaps(near_pairs))
    z_cols, turned, p_part, d_part, d_near, squares, base_near, e_near = inner_step(
        z, pattern, near, far, beside
    )
    held = (d_near, base_near, e_near, mask_near)
    d_far, d_out, z_far, squares = outer_step(
        z, pattern, beyond, across, z_cols, turned, p_part, d_part, squares, held
    )
    squares_beside = lax.ppermute(squares, AXES, swaps(near_pairs))
    d_in = lax.ppermute(d_out, AXES, swaps(far_pairs))
    refined, narrow, spread = middle_step(
        z, squares, squares_beside, z_cols, z_far, d_far, d_near, base_near, e_near, mask_near
    )
    groups = [list(range(core, devices, 2)) for core in range(2)]
    gathered = lax.all_to_all(spread, AXES, 0, 0, tiled=True, axis_index_groups=groups)
    refined, narrow, _ = last_step(z, pattern, narrow, d_in, refined)
    norm = norm_step(z, gathered, narrow)
    return refined, norm[0, 0]


def solution(mesh):
    return jax.shard_map(
        per_device,
        mesh=mesh,
        in_specs=(
            P(AXES, None, None, None),
            P(AXES, None, None, None),
            P(AXES, None),
        ),
        out_specs=(P(AXES, None, None, None), P()),
        check_vma=False,
    )
```

```python
import functools

import jax
import jax.numpy as jnp
from jax import lax
from jax.experimental import pallas as pl
from jax.experimental.pallas import tpu as pltpu
from jax.sharding import PartitionSpec as P


AXES = ("grp", "slab")
HBM = pl.BlockSpec(memory_space=pltpu.HBM)
VMEM = pl.BlockSpec(memory_space=pltpu.VMEM)
SMEM = pl.BlockSpec(memory_space=pltpu.SMEM)
PARAMS = pltpu.CompilerParams(vmem_limit_bytes=32 * 1024 * 1024)
FLAG_ROWS = 16


class Sizes:
    def __init__(self, shape, quarter_len, devices):
        self.columns, self.offsets, self.block, _ = shape
        self.half = (self.offsets - 1) // 2
        self.tile = self.half * self.block
        self.cells = self.half * self.offsets
        self.flag_blocks = -(-self.half * self.half * FLAG_ROWS // self.block)
        self.quarter_len = quarter_len
        self.devices = devices
        self.entries = self.columns * devices * self.block

    def cost(self, products, moved):
        return pl.CostEstimate(
            flops=products * 2 * self.tile**3, bytes_accessed=moved * 2**20, transcendentals=0
        )

    def tiles(self, count, dtype):
        return jax.ShapeDtypeStruct((count, self.tile, self.tile), dtype)


def odd_device():
    return lax.rem(lax.axis_index("slab"), 2)


def half_starts(z):
    near = jnp.where(odd_device() == 1, 0, z.columns - z.half)
    return near, z.columns - z.half - near


def keep(flag, value):
    return jnp.where(flag, value, jnp.zeros_like(value))


def dot(left, right):
    return jnp.dot(left, right, preferred_element_type=jnp.float32)


def chain_tile(true_tile):
    return jnp.where(odd_device() == 1, 2 - true_tile, true_tile)


def expand(z, out, read):
    block = z.block
    for t in range(z.half):
        for a in range(3 * z.half):
            o = a - t
            u = a % z.half
            if 0 <= o < z.offsets:
                value = read(t, o)
            else:
                value = jnp.zeros((block, block), out.dtype)
            out[
                chain_tile(a // z.half),
                u * block : (u + 1) * block,
                t * block : (t + 1) * block,
            ] = value


def offset_of(z, e, t, u):
    return jnp.where(odd_device() == 1, 1 - e, e - 1) * z.half + u - t + z.half


def flag_of(z, pattern, first, e, t, u):
    o = offset_of(z, e, t, u)
    inside = jnp.logical_and(o >= 0, o < z.offsets)
    return jnp.logical_and(inside, pattern[first + t, jnp.clip(o, 0, z.offsets - 1)] != 0)


def masked(z, value, flag):
    block = z.block
    rows = []
    for u in range(z.half):
        rows.append(
            jnp.concatenate(
                [
                    keep(
                        flag(t, u),
                        value[u * block : (u + 1) * block, t * block : (t + 1) * block],
                    )
                    for t in range(z.half)
                ],
                axis=1,
            )
        )
    return jnp.concatenate(rows, axis=0)


def own_masked(z, pattern, first, e, value):
    return masked(z, value, lambda t, u: flag_of(z, pattern, first, e, t, u))


def identity(z):
    shape = (z.tile, z.tile)
    rows = lax.broadcasted_iota(jnp.int32, shape, 0)
    return (rows == lax.broadcasted_iota(jnp.int32, shape, 1)).astype(jnp.float32)


def tile_product(left, right, i, c, low, high):
    total = None
    for k in range(max(low, i - 1, c - 1), min(high, i + 1, c + 1) + 1):
        term = dot(left[k][i - k + 1], right[k - c + 1])
        total = term if total is None else total + term
    return total


def sum_squares(z, value):
    wide = value.astype(jnp.float32)
    return jnp.sum((wide * wide).reshape(-1, 8, z.tile), axis=0)


def store_half(z, tiles, cells):
    block = z.block
    for t in range(z.half):
        for o in range(z.offsets):
            a = t + o
            u = a % z.half
            value = tiles[
                chain_tile(a // z.half),
                u * block : (u + 1) * block,
                t * block : (t + 1) * block,
            ]
            cells[t, o] = value.astype(cells.dtype)


def mask_kernel(z, pattern, mask_near):
    first, _ = half_starts(z)
    ones = jnp.ones((z.tile, z.tile), jnp.float32)
    for e in range(3):
        mask_near[e] = own_masked(z, pattern, first, e, ones).astype(mask_near.dtype)


def masks(z, pattern, kind):
    return pl.pallas_call(
        functools.partial(mask_kernel, z),
        out_shape=z.tiles(3, kind),
        in_specs=[SMEM],
        out_specs=VMEM,
        compiler_params=PARAMS,
        cost_estimate=z.cost(20, 1),
        name="masks",
    )(pattern)


def pack_kernel(z, margin, factor, pattern, _, near, far, cross):
    near_first, far_first = half_starts(z)
    first_row = lax.axis_index("slab") * z.columns
    plan = ((margin, far_first), (factor, far_first), (margin, near_first), (factor, near_first))
    for k, (source, first) in enumerate(plan):
        for t in range(z.half):
            for o in range(z.offsets):
                flag = pattern[first + t, o] != 0
                if k % 2:
                    row = first_row + first + t + o - z.half
                    inside = jnp.logical_and(row >= 0, row < z.quarter_len)
                    flag = jnp.logical_and(flag, inside)
                value = keep(flag, source[first + t, o])
                cell = t * z.offsets + o
                u = o + t - z.half
                if k == 0:
                    far[cell] = value
                    near[2 * z.cells + cell] = value
                elif k == 1:
                    far[z.cells + cell] = value
                    if 0 <= u < z.half:
                        cross[t, u] = value
                else:
                    near[(k - 2) * z.cells + cell] = value
    per_block = z.block // FLAG_ROWS
    for f in range(z.flag_blocks * per_block):
        t, u = f // z.half, f % z.half
        value = jnp.zeros((FLAG_ROWS, z.block), near.dtype)
        if t < z.half:
            value = keep(pattern[near_first + t, u - t + z.half] != 0, jnp.ones_like(value))
        low = f % per_block * FLAG_ROWS
        near[3 * z.cells + f // per_block, low : low + FLAG_ROWS] = value


def pack(z, margin, factor, pattern, mask_near):
    kind = margin.dtype
    return pl.pallas_call(
        functools.partial(pack_kernel, z),
        out_shape=(
            jax.ShapeDtypeStruct((3 * z.cells + z.flag_blocks, z.block, z.block), kind),
            jax.ShapeDtypeStruct((2 * z.cells, z.block, z.block), kind),
            jax.ShapeDtypeStruct((z.half, z.half, z.block, z.block), kind),
        ),
        in_specs=[VMEM, VMEM, SMEM, VMEM],
        out_specs=(VMEM, VMEM, VMEM),
        compiler_params=PARAMS,
        name="pack",
    )(margin, factor, pattern, mask_near)


def inner_kernel(
    z, pattern, mask_near, near, far, beside, z_cols, turned, p_part, d_part, squares, held16, held32,
    s_cols, z_turned, image, d_near, d_beside, sums, sems,
):
    near_first, _ = half_starts(z)
    kind = near.dtype

    def cells_of(ref, base):
        return lambda t, o: ref[base + t * z.offsets + o]

    expand(z, s_cols.at[0], cells_of(far, 0))
    expand(z, s_cols.at[1], cells_of(near, 0))
    expand(z, s_cols.at[2], cells_of(beside, 0))
    expand(z, s_cols.at[3], cells_of(beside, 2 * z.cells))
    expand(z, z_cols.at[0], cells_of(far, z.cells))
    expand(z, z_cols.at[1], cells_of(near, z.cells))
    expand(z, z_cols.at[2], cells_of(beside, z.cells))
    moves = [
        (z_cols.at[0], held16.at[pl.ds(2, 3)]),
        (z_cols.at[1], held16.at[pl.ds(5, 3)]),
        (z_cols.at[2, pl.ds(0, 2)], held16.at[pl.ds(8, 2)]),
        (d_near.at[pl.ds(0, 2)], held16.at[pl.ds(0, 2)]),
        (sums, held32),
    ]
    copies = [
        pltpu.make_async_copy(source, target, sems.at[k]) for k, (source, target) in enumerate(moves)
    ]
    for copy in copies[:3]:
        copy.start()
    for x in range(3):
        for e in range(3):
            z_turned[x, e] = z_cols[x, e].T
    turned[0] = z_turned[0, 0]
    turned[1] = z_turned[0, 1]
    turned[2] = z_turned[1, 0]

    def image_tile(y, c):
        total = None
        for inner in range(max(c - 1, y - 1, 1), min(c + 1, y + 1) + 1):
            term = dot(s_cols[inner - 1, y - inner + 1], z_cols[c - 1, inner - c + 1])
            total = term if total is None else total + term
        return total

    def turned_sum(i, c, rows):
        total = None
        for m in rows:
            term = dot(z_turned[i - 1, m - i + 1], image[c - 1, m])
            total = term if total is None else total + term
        return total

    p_part[0] = image_tile(0, 1)
    p_part[1] = image_tile(1, 1)
    for c, rows in ((1, (2, 3)), (2, (0, 1, 2, 3, 4)), (3, (1, 2, 3, 4))):
        for y in rows:
            image[c - 1, y] = image_tile(y, c).astype(kind)
    d_part[0] = turned_sum(1, 1, (2,))
    d_part[1] = turned_sum(2, 1, (2, 3))
    eye = identity(z)
    total = jnp.zeros((8, z.tile), jnp.float32)
    for i in (1, 2, 3):
        value = -turned_sum(i, 2, (i - 1, i, i + 1))
        if i == 2:
            value = eye + value
        value = (value * mask_near[i - 1].astype(jnp.float32)).astype(kind)
        d_near[i - 1] = value
        total = total + sum_squares(z, value)
    squares[...] = total
    copies[3].start()

    def side_flag(t, u):
        o = offset_of(z, 0, t, u)
        inside = jnp.logical_and(o >= 0, o < z.offsets)
        back = jnp.clip(z.offsets - 1 - o, 0, z.offsets - 1)
        return jnp.logical_and(inside, pattern[near_first + u, back] != 0)

    d_beside[0] = masked(z, -turned_sum(2, 3, (1, 2, 3)), side_flag).astype(kind)
    value = eye - turned_sum(3, 3, (2, 3, 4))
    block = z.block
    per_block = block // FLAG_ROWS
    for t in range(z.half):
        for u in range(z.half):
            f = t * z.half + u
            low = f % per_block * FLAG_ROWS
            flags = beside[3 * z.cells + f // per_block, low : low + FLAG_ROWS]
            flag = flags.astype(jnp.float32)[:1]
            part = (slice(u * block, (u + 1) * block), slice(t * block, (t + 1) * block))
            d_beside[1, part[0], part[1]] = (value[part] * flag).astype(kind)

    factor = (None, z_cols.at[0], z_cols.at[1], z_cols.at[2])
    defect = (None, None, d_near, d_beside)
    for i in (1, 2, 3):
        sums[i - 1] = z_cols[1, i - 1].astype(jnp.float32) + 0.5 * tile_product(
            factor, d_near, i, 2, 1, 3
        )
        sums[2 + i] = tile_product(defect, d_near, i, 2, 2, 3)
    copies[4].start()
    for copy in copies:
        copy.wait()


def inner_step(z, pattern, mask_near, near, far, beside):
    kind = near.dtype
    tile = z.tile
    return pl.pallas_call(
        functools.partial(inner_kernel, z),
        out_shape=(
            jax.ShapeDtypeStruct((3, 3, tile, tile), kind),
            z.tiles(3, kind),
            z.tiles(2, jnp.float32),
            z.tiles(2, jnp.float32),
            jax.ShapeDtypeStruct((8, tile), jnp.float32),
            z.tiles(10, kind),
            z.tiles(6, jnp.float32),
        ),
        in_specs=[SMEM, VMEM, VMEM, VMEM, VMEM],
        out_specs=(VMEM,) * 5 + (HBM,) * 2,
        scratch_shapes=[
            pltpu.VMEM((4, 3, tile, tile), kind),
            pltpu.VMEM((3, 3, tile, tile), kind),
            pltpu.VMEM((3, 5, tile, tile), kind),
            pltpu.VMEM((3, tile, tile), kind),
            pltpu.VMEM((2, tile, tile), kind),
            pltpu.VMEM((6, tile, tile), jnp.float32),
            pltpu.SemaphoreType.DMA((5,)),
        ],
        compiler_params=PARAMS,
        cost_estimate=z.cost(54, 8),
        name="inner",
    )(pattern, mask_near, near, far, beside)


def outer_kernel(
    z, pattern, far, cross, z_cols, turned, p_part, d_part, squares, d_out, carry, spread, s_far, z_far,
    d_far, sems,
):
    _, far_first = half_starts(z)
    kind = far.dtype

    def factor_cell(t, o):
        value = far[z.cells + t * z.offsets + o]
        u = o + t - z.half
        if 0 <= u < z.half:
            value = value + cross[t, u]
        return value

    expand(z, s_far, lambda t, o: far[t * z.offsets + o])
    expand(z, z_far, factor_cell)
    copies = [pltpu.make_async_copy(z_far.at[pl.ds(1, 2)], carry.at[pl.ds(0, 2)], sems.at[0])]
    copies[0].start()
    link = z_cols[0, 0]
    image = (
        dot(s_far[0], link).astype(kind),
        (dot(s_far[1], link) + p_part[0]).astype(kind),
        (dot(s_far[2], link) + p_part[1]).astype(kind),
    )
    values = (
        -(dot(z_far[0].T, image[0]) + dot(z_far[1].T, image[1]) + dot(z_far[2].T, image[2])),
        identity(z) - (dot(turned[0], image[1]) + dot(turned[1], image[2]) + d_part[0]),
        -(dot(turned[2], image[2]) + d_part[1]),
    )
    total = squares[...]
    for e, value in enumerate(values):
        value = own_masked(z, pattern, far_first, e, value).astype(kind)
        d_far[e] = value
        copies.append(
            pltpu.make_async_copy(d_far.at[pl.ds(e, 1)], carry.at[pl.ds(2 + e, 1)], sems.at[1 + e])
        )
        copies[-1].start()
        if e < 2:
            d_out[e] = value
        total = total + sum_squares(z, value)
    lanes = jnp.sum(total, axis=0, keepdims=True)
    folded = lanes[:, : z.block]
    for t in range(1, z.half):
        folded = folded + lanes[:, t * z.block : (t + 1) * z.block]
    spread[...] = jnp.broadcast_to(folded[None], spread.shape)
    for copy in copies:
        copy.wait()


def outer_step(z, pattern, far, cross, z_cols, turned, p_part, d_part, squares):
    kind = far.dtype
    return pl.pallas_call(
        functools.partial(outer_kernel, z),
        out_shape=(
            z.tiles(2, kind),
            z.tiles(5, kind),
            jax.ShapeDtypeStruct((z.devices, 1, z.block), jnp.float32),
        ),
        in_specs=[SMEM] + [VMEM] * 7,
        out_specs=(VMEM, HBM, VMEM),
        scratch_shapes=[
            pltpu.VMEM((3, z.tile, z.tile), kind),
            pltpu.VMEM((3, z.tile, z.tile), kind),
            pltpu.VMEM((3, z.tile, z.tile), kind),
            pltpu.SemaphoreType.DMA((4,)),
        ],
        compiler_params=PARAMS,
        cost_estimate=z.cost(9, 4),
        name="outer",
    )(pattern, far, cross, z_cols, turned, p_part, d_part, squares)


def middle_kernel(
    z, pattern_in, held16_in, held32_in, carry_in, refined, _a, _b, _c, pattern, held16, held32, d_far,
    square, tiles, cells, sems,
):
    first, _ = half_starts(z)
    moves = (
        (pattern_in, pattern),
        (carry_in.at[pl.ds(3, 2)], d_far),
        (held16_in.at[pl.ds(0, 1)], held16.at[pl.ds(0, 1)]),
        (held32_in.at[pl.ds(3, 3)], held32.at[pl.ds(3, 3)]),
        (held16_in.at[pl.ds(3, 7)], held16.at[pl.ds(3, 7)]),
        (held32_in.at[pl.ds(0, 3)], held32.at[pl.ds(0, 3)]),
    )
    copies = [
        pltpu.make_async_copy(source, target, sems.at[k]) for k, (source, target) in enumerate(moves)
    ]
    for copy in copies:
        copy.start()
    for copy in copies[:4]:
        copy.wait()
    for i in (1, 2, 3):
        value = held32[2 + i]
        if i < 3:
            value = value + dot(d_far[i - 1], held16[0])
        square[i - 1] = own_masked(z, pattern, first, i - 1, value).astype(square.dtype)
    for copy in copies[4:]:
        copy.wait()
    for i in (1, 2, 3):
        total = None
        for k in range(max(1, i - 1), min(3, i + 1) + 1):
            term = dot(held16[3 * k - 1 + i - k + 1], square[k - 1])
            total = term if total is None else total + term
        tiles[i - 1] = own_masked(z, pattern, first, i - 1, held32[i - 1] + 0.375 * total)
    store_half(z, tiles, cells)
    copy = pltpu.make_async_copy(cells, refined.at[pl.ds(first, z.half)], sems.at[6])
    copy.start()
    copy.wait()


def middle_step(z, pattern, held16, held32, carry):
    kind = held16.dtype
    shape = (z.columns, z.offsets, z.block, z.block)
    return pl.pallas_call(
        functools.partial(middle_kernel, z),
        out_shape=(
            jax.ShapeDtypeStruct(shape, kind),
            jax.ShapeDtypeStruct(held16.shape, kind),
            jax.ShapeDtypeStruct(held32.shape, jnp.float32),
            jax.ShapeDtypeStruct(carry.shape, kind),
        ),
        in_specs=[HBM] * 4,
        out_specs=(HBM,) * 4,
        scratch_shapes=[
            pltpu.SMEM(pattern.shape, pattern.dtype),
            pltpu.VMEM(held16.shape, kind),
            pltpu.VMEM(held32.shape, jnp.float32),
            pltpu.VMEM((2, z.tile, z.tile), kind),
            pltpu.VMEM((3, z.tile, z.tile), kind),
            pltpu.VMEM((3, z.tile, z.tile), jnp.float32),
            pltpu.VMEM((z.half,) + shape[1:], kind),
            pltpu.SemaphoreType.DMA((7,)),
        ],
        input_output_aliases={1: 1, 2: 2, 3: 3},
        compiler_params=PARAMS,
        cost_estimate=z.cost(9, 6),
        name="middle",
    )(pattern, held16, held32, carry)


def last_kernel(
    z, pattern_in, held16, carry, d_in, _, refined, _a, _b, _c, pattern, narrow, d_beyond, square, tiles,
    cells, sems,
):
    _, first = half_starts(z)
    moves = (
        (pattern_in, pattern),
        (d_in, d_beyond),
        (carry.at[pl.ds(2, 3)], narrow.at[pl.ds(0, 3)]),
        (held16.at[pl.ds(0, 2)], narrow.at[pl.ds(3, 2)]),
        (carry.at[pl.ds(0, 2)], narrow.at[pl.ds(5, 2)]),
        (held16.at[pl.ds(2, 5)], narrow.at[pl.ds(7, 5)]),
    )
    copies = [
        pltpu.make_async_copy(source, target, sems.at[k]) for k, (source, target) in enumerate(moves)
    ]
    for copy in copies:
        copy.start()
    for copy in copies[:4]:
        copy.wait()
    values = (
        dot(d_beyond[1], narrow[0]) + dot(narrow[0], narrow[1]),
        dot(d_beyond[0], narrow[0]) + dot(narrow[1], narrow[1]) + dot(narrow[3], narrow[2]),
        dot(narrow[2], narrow[1]) + dot(narrow[4], narrow[2]),
    )
    for i, value in enumerate(values):
        square[i] = own_masked(z, pattern, first, i, value).astype(square.dtype)
    for copy in copies[4:]:
        copy.wait()
    base = (4, 7, 10)
    for i in (0, 1, 2):
        half = None
        rest = None
        for k in range(max(0, i - 1), min(2, i + 1) + 1):
            left = narrow[base[k] + i - k + 1]
            term = dot(left, narrow[k])
            half = term if half is None else half + term
            term = dot(left, square[k])
            rest = term if rest is None else rest + term
        value = narrow[7 + i].astype(jnp.float32) + 0.5 * half + 0.375 * rest
        tiles[i] = own_masked(z, pattern, first, i, value)
    store_half(z, tiles, cells)
    copy = pltpu.make_async_copy(cells, refined.at[pl.ds(first, z.half)], sems.at[6])
    copy.start()
    copy.wait()


def last_step(z, pattern, held16, carry, d_in, refined):
    kind = refined.dtype
    return pl.pallas_call(
        functools.partial(last_kernel, z),
        out_shape=tuple(
            jax.ShapeDtypeStruct(held.shape, held.dtype) for held in (refined, held16, carry, d_in)
        ),
        in_specs=[HBM] * 5,
        out_specs=(HBM,) * 4,
        scratch_shapes=[
            pltpu.SMEM(pattern.shape, pattern.dtype),
            pltpu.VMEM((12, z.tile, z.tile), kind),
            pltpu.VMEM(d_in.shape, kind),
            pltpu.VMEM((3, z.tile, z.tile), kind),
            pltpu.VMEM((3, z.tile, z.tile), jnp.float32),
            pltpu.VMEM((z.half,) + refined.shape[1:], kind),
            pltpu.SemaphoreType.DMA((7,)),
        ],
        input_output_aliases={4: 0, 1: 1, 2: 2, 3: 3},
        compiler_params=PARAMS,
        cost_estimate=z.cost(21, 4),
        name="last",
    )(pattern, held16, carry, d_in, refined)


def norm_kernel(z, gathered, _, norm):
    mean = jnp.sum(gathered[...]) * (1.0 / z.entries)
    norm[...] = jnp.sqrt(jnp.full(norm.shape, mean, jnp.float32))


def norm_step(z, gathered, after):
    return pl.pallas_call(
        functools.partial(norm_kernel, z),
        out_shape=jax.ShapeDtypeStruct((1, z.block), jnp.float32),
        in_specs=[VMEM, HBM],
        out_specs=VMEM,
        compiler_params=PARAMS,
        name="norm",
    )(gathered, after)


def swaps(pairs):
    return [pair for i, j in pairs for pair in ((i, j), (j, i))]


def per_device(margin, factor, pattern):
    slabs = lax.axis_size("slab")
    devices = lax.axis_size("grp") * slabs
    z = Sizes(margin.shape, margin.shape[0] * slabs, devices)
    if slabs % 2 or z.columns != 2 * z.half:
        raise ValueError("sizes")
    near_pairs = [(i, i + 1) for i in range(0, devices - 1, 2)]
    far_pairs = [(i, i + 1) for i in range(1, devices - 1, 2)]
    inner_pairs = [(i, j) for i, j in far_pairs if j % slabs]
    cross_pairs = [(i, j) for i, j in far_pairs if not j % slabs]
    mask_near = masks(z, pattern, margin.dtype)
    near, far, cross = pack(z, margin, factor, pattern, mask_near)
    beyond = lax.ppermute(far, AXES, swaps(inner_pairs))
    across = lax.ppermute(cross, AXES, swaps(cross_pairs))
    beside = lax.ppermute(near, AXES, swaps(near_pairs))
    z_cols, turned, p_part, d_part, squares, held16, held32 = inner_step(
        z, pattern, mask_near, near, far, beside
    )
    d_out, carry, spread = outer_step(
        z, pattern, beyond, across, z_cols, turned, p_part, d_part, squares
    )
    gathered = lax.all_to_all(spread, AXES, 0, 0, tiled=True)
    d_in = lax.ppermute(d_out, AXES, swaps(far_pairs))
    refined, held16, _, carry = middle_step(z, pattern, held16, held32, carry)
    refined, held16, _, _ = last_step(z, pattern, held16, carry, d_in, refined)
    norm = norm_step(z, gathered, held16)
    return refined, norm[0, 0]


def solution(mesh):
    return jax.shard_map(
        per_device,
        mesh=mesh,
        in_specs=(
            P(AXES, None, None, None),
            P(AXES, None, None, None),
            P(AXES, None),
        ),
        out_specs=(P(AXES, None, None, None), P()),
        check_vma=False,
    )
```

```python
import functools

import jax
import jax.numpy as jnp
from jax import lax
from jax.experimental import pallas as pl
from jax.experimental.pallas import tpu as pltpu
from jax.sharding import PartitionSpec as P


AXES = ("grp", "slab")
HBM = pl.BlockSpec(memory_space=pltpu.HBM)
VMEM = pl.BlockSpec(memory_space=pltpu.VMEM)
SMEM = pl.BlockSpec(memory_space=pltpu.SMEM)
PARAMS = pltpu.CompilerParams(vmem_limit_bytes=32 * 1024 * 1024)
FLAG_ROWS = 16


class Sizes:
    def __init__(self, shape, quarter_len, devices):
        self.columns, self.offsets, self.block, _ = shape
        self.half = (self.offsets - 1) // 2
        self.tile = self.half * self.block
        self.cells = self.half * self.offsets
        self.flag_blocks = -(-self.half * self.half * FLAG_ROWS // self.block)
        self.quarter_len = quarter_len
        self.devices = devices
        self.entries = self.columns * devices * self.block

    def cost(self, products, moved):
        return pl.CostEstimate(
            flops=products * 2 * self.tile**3, bytes_accessed=moved * 2**20, transcendentals=0
        )

    def tiles(self, count, dtype):
        return jax.ShapeDtypeStruct((count, self.tile, self.tile), dtype)


def odd_device():
    return lax.rem(lax.axis_index("slab"), 2)


def half_starts(z):
    near = jnp.where(odd_device() == 1, 0, z.columns - z.half)
    return near, z.columns - z.half - near


def keep(flag, value):
    return jnp.where(flag, value, jnp.zeros_like(value))


def dot(left, right):
    return jnp.dot(left, right, preferred_element_type=jnp.float32)


def chain_tile(true_tile):
    return jnp.where(odd_device() == 1, 2 - true_tile, true_tile)


def expand(z, out, read):
    block = z.block
    for t in range(z.half):
        for a in range(3 * z.half):
            o = a - t
            u = a % z.half
            if 0 <= o < z.offsets:
                value = read(t, o)
            else:
                value = jnp.zeros((block, block), out.dtype)
            out[
                chain_tile(a // z.half),
                u * block : (u + 1) * block,
                t * block : (t + 1) * block,
            ] = value


def offset_of(z, e, t, u):
    return jnp.where(odd_device() == 1, 1 - e, e - 1) * z.half + u - t + z.half


def flag_of(z, pattern, first, e, t, u):
    o = offset_of(z, e, t, u)
    inside = jnp.logical_and(o >= 0, o < z.offsets)
    return jnp.logical_and(inside, pattern[first + t, jnp.clip(o, 0, z.offsets - 1)] != 0)


def masked(z, value, flag):
    block = z.block
    rows = []
    for u in range(z.half):
        rows.append(
            jnp.concatenate(
                [
                    keep(
                        flag(t, u),
                        value[u * block : (u + 1) * block, t * block : (t + 1) * block],
                    )
                    for t in range(z.half)
                ],
                axis=1,
            )
        )
    return jnp.concatenate(rows, axis=0)


def own_masked(z, pattern, first, e, value):
    return masked(z, value, lambda t, u: flag_of(z, pattern, first, e, t, u))


def identity(z):
    shape = (z.tile, z.tile)
    rows = lax.broadcasted_iota(jnp.int32, shape, 0)
    return (rows == lax.broadcasted_iota(jnp.int32, shape, 1)).astype(jnp.float32)


def tile_product(left, right, i, c, low, high):
    total = None
    for k in range(max(low, i - 1, c - 1), min(high, i + 1, c + 1) + 1):
        term = dot(left[k][i - k + 1], right[k - c + 1])
        total = term if total is None else total + term
    return total


def sum_squares(z, value):
    wide = value.astype(jnp.float32)
    return jnp.sum((wide * wide).reshape(-1, 8, z.tile), axis=0)


def store_half(z, tiles, cells):
    block = z.block
    for t in range(z.half):
        for o in range(z.offsets):
            a = t + o
            u = a % z.half
            value = tiles[
                chain_tile(a // z.half),
                u * block : (u + 1) * block,
                t * block : (t + 1) * block,
            ]
            cells[t, o] = value.astype(cells.dtype)


def mask_kernel(z, pattern, mask_near):
    first, _ = half_starts(z)
    ones = jnp.ones((z.tile, z.tile), jnp.float32)
    for e in range(3):
        mask_near[e] = own_masked(z, pattern, first, e, ones).astype(mask_near.dtype)


def masks(z, pattern, kind):
    return pl.pallas_call(
        functools.partial(mask_kernel, z),
        out_shape=z.tiles(3, kind),
        in_specs=[SMEM],
        out_specs=VMEM,
        compiler_params=PARAMS,
        cost_estimate=z.cost(20, 1),
        name="masks",
    )(pattern)


def pack_kernel(z, margin, factor, pattern, _, near, far, cross):
    near_first, far_first = half_starts(z)
    first_row = lax.axis_index("slab") * z.columns
    plan = ((margin, far_first), (factor, far_first), (margin, near_first), (factor, near_first))
    for k, (source, first) in enumerate(plan):
        for t in range(z.half):
            for o in range(z.offsets):
                flag = pattern[first + t, o] != 0
                if k % 2:
                    row = first_row + first + t + o - z.half
                    inside = jnp.logical_and(row >= 0, row < z.quarter_len)
                    flag = jnp.logical_and(flag, inside)
                value = keep(flag, source[first + t, o])
                cell = t * z.offsets + o
                u = o + t - z.half
                if k == 0:
                    far[cell] = value
                    near[2 * z.cells + cell] = value
                elif k == 1:
                    far[z.cells + cell] = value
                    if 0 <= u < z.half:
                        cross[t, u] = value
                else:
                    near[(k - 2) * z.cells + cell] = value
    per_block = z.block // FLAG_ROWS
    for f in range(z.flag_blocks * per_block):
        t, u = f // z.half, f % z.half
        value = jnp.zeros((FLAG_ROWS, z.block), near.dtype)
        if t < z.half:
            value = keep(pattern[near_first + t, u - t + z.half] != 0, jnp.ones_like(value))
        low = f % per_block * FLAG_ROWS
        near[3 * z.cells + f // per_block, low : low + FLAG_ROWS] = value


def pack(z, margin, factor, pattern, mask_near):
    kind = margin.dtype
    return pl.pallas_call(
        functools.partial(pack_kernel, z),
        out_shape=(
            jax.ShapeDtypeStruct((3 * z.cells + z.flag_blocks, z.block, z.block), kind),
            jax.ShapeDtypeStruct((2 * z.cells, z.block, z.block), kind),
            jax.ShapeDtypeStruct((z.half, z.half, z.block, z.block), kind),
        ),
        in_specs=[VMEM, VMEM, SMEM, VMEM],
        out_specs=(VMEM, VMEM, VMEM),
        compiler_params=PARAMS,
        name="pack",
    )(margin, factor, pattern, mask_near)


def inner_kernel(
    z, pattern, mask_near, near, far, beside, z_cols, turned, p_part, d_part, squares, held16, held32,
    flags, s_cols, z_turned, image, d_near, d_beside, sums, sems,
):
    near_first, _ = half_starts(z)
    kind = near.dtype

    def cells_of(ref, base):
        return lambda t, o: ref[base + t * z.offsets + o]

    expand(z, s_cols.at[0], cells_of(far, 0))
    expand(z, s_cols.at[1], cells_of(near, 0))
    expand(z, s_cols.at[2], cells_of(beside, 0))
    expand(z, s_cols.at[3], cells_of(beside, 2 * z.cells))
    expand(z, z_cols.at[0], cells_of(far, z.cells))
    expand(z, z_cols.at[1], cells_of(near, z.cells))
    expand(z, z_cols.at[2], cells_of(beside, z.cells))
    moves = [
        (z_cols.at[0], held16.at[pl.ds(2, 3)]),
        (z_cols.at[1], held16.at[pl.ds(5, 3)]),
        (z_cols.at[2, pl.ds(0, 2)], held16.at[pl.ds(8, 2)]),
        (pattern, flags),
        (d_near.at[pl.ds(0, 2)], held16.at[pl.ds(0, 2)]),
        (sums, held32),
    ]
    copies = [
        pltpu.make_async_copy(source, target, sems.at[k]) for k, (source, target) in enumerate(moves)
    ]
    for copy in copies[:4]:
        copy.start()
    for x in range(3):
        for e in range(3):
            z_turned[x, e] = z_cols[x, e].T
    turned[0] = z_turned[0, 0]
    turned[1] = z_turned[0, 1]
    turned[2] = z_turned[1, 0]

    def image_tile(y, c):
        total = None
        for inner in range(max(c - 1, y - 1, 1), min(c + 1, y + 1) + 1):
            term = dot(s_cols[inner - 1, y - inner + 1], z_cols[c - 1, inner - c + 1])
            total = term if total is None else total + term
        return total

    def turned_sum(i, c, rows):
        total = None
        for m in rows:
            term = dot(z_turned[i - 1, m - i + 1], image[c - 1, m])
            total = term if total is None else total + term
        return total

    p_part[0] = image_tile(0, 1)
    p_part[1] = image_tile(1, 1)
    for c, rows in ((1, (2, 3)), (2, (0, 1, 2, 3, 4)), (3, (1, 2, 3, 4))):
        for y in rows:
            image[c - 1, y] = image_tile(y, c).astype(kind)
    d_part[0] = turned_sum(1, 1, (2,))
    d_part[1] = turned_sum(2, 1, (2, 3))
    eye = identity(z)
    total = jnp.zeros((8, z.tile), jnp.float32)
    for i in (1, 2, 3):
        value = -turned_sum(i, 2, (i - 1, i, i + 1))
        if i == 2:
            value = eye + value
        value = (value * mask_near[i - 1].astype(jnp.float32)).astype(kind)
        d_near[i - 1] = value
        total = total + sum_squares(z, value)
    squares[...] = total
    copies[4].start()

    def side_flag(t, u):
        o = offset_of(z, 0, t, u)
        inside = jnp.logical_and(o >= 0, o < z.offsets)
        back = jnp.clip(z.offsets - 1 - o, 0, z.offsets - 1)
        return jnp.logical_and(inside, pattern[near_first + u, back] != 0)

    d_beside[0] = masked(z, -turned_sum(2, 3, (1, 2, 3)), side_flag).astype(kind)
    value = eye - turned_sum(3, 3, (2, 3, 4))
    block = z.block
    per_block = block // FLAG_ROWS
    for t in range(z.half):
        for u in range(z.half):
            f = t * z.half + u
            low = f % per_block * FLAG_ROWS
            flags = beside[3 * z.cells + f // per_block, low : low + FLAG_ROWS]
            flag = flags.astype(jnp.float32)[:1]
            part = (slice(u * block, (u + 1) * block), slice(t * block, (t + 1) * block))
            d_beside[1, part[0], part[1]] = (value[part] * flag).astype(kind)

    factor = (None, z_cols.at[0], z_cols.at[1], z_cols.at[2])
    defect = (None, None, d_near, d_beside)
    for i in (1, 2, 3):
        sums[i - 1] = z_cols[1, i - 1].astype(jnp.float32) + 0.5 * tile_product(
            factor, d_near, i, 2, 1, 3
        )
        sums[2 + i] = tile_product(defect, d_near, i, 2, 2, 3)
    copies[5].start()
    for copy in copies:
        copy.wait()


def inner_step(z, pattern, mask_near, near, far, beside):
    kind = near.dtype
    tile = z.tile
    return pl.pallas_call(
        functools.partial(inner_kernel, z),
        out_shape=(
            jax.ShapeDtypeStruct((3, 3, tile, tile), kind),
            z.tiles(3, kind),
            z.tiles(2, jnp.float32),
            z.tiles(2, jnp.float32),
            jax.ShapeDtypeStruct((8, tile), jnp.float32),
            z.tiles(10, kind),
            z.tiles(6, jnp.float32),
            jax.ShapeDtypeStruct(pattern.shape, pattern.dtype),
        ),
        in_specs=[SMEM, VMEM, VMEM, VMEM, VMEM],
        out_specs=(VMEM,) * 5 + (HBM,) * 3,
        scratch_shapes=[
            pltpu.VMEM((4, 3, tile, tile), kind),
            pltpu.VMEM((3, 3, tile, tile), kind),
            pltpu.VMEM((3, 5, tile, tile), kind),
            pltpu.VMEM((3, tile, tile), kind),
            pltpu.VMEM((2, tile, tile), kind),
            pltpu.VMEM((6, tile, tile), jnp.float32),
            pltpu.SemaphoreType.DMA((6,)),
        ],
        compiler_params=PARAMS,
        cost_estimate=z.cost(54, 8),
        name="inner",
    )(pattern, mask_near, near, far, beside)


def outer_kernel(
    z, pattern, far, cross, z_cols, turned, p_part, d_part, squares, d_out, carry, spread_out, s_far,
    z_far, d_far, spread, sems,
):
    _, far_first = half_starts(z)
    kind = far.dtype

    def factor_cell(t, o):
        value = far[z.cells + t * z.offsets + o]
        u = o + t - z.half
        if 0 <= u < z.half:
            value = value + cross[t, u]
        return value

    expand(z, s_far, lambda t, o: far[t * z.offsets + o])
    expand(z, z_far, factor_cell)
    copies = []

    def send(source, target):
        copies.append(pltpu.make_async_copy(source, target, sems.at[len(copies)]))
        copies[-1].start()

    send(z_far.at[pl.ds(1, 2)], carry.at[pl.ds(0, 2)])
    link = z_cols[0, 0]
    image = (
        dot(s_far[0], link).astype(kind),
        (dot(s_far[1], link) + p_part[0]).astype(kind),
        (dot(s_far[2], link) + p_part[1]).astype(kind),
    )
    values = (
        -(dot(z_far[0].T, image[0]) + dot(z_far[1].T, image[1]) + dot(z_far[2].T, image[2])),
        identity(z) - (dot(turned[0], image[1]) + dot(turned[1], image[2]) + d_part[0]),
        -(dot(turned[2], image[2]) + d_part[1]),
    )
    total = squares[...]
    for e, value in enumerate(values):
        value = own_masked(z, pattern, far_first, e, value).astype(kind)
        d_far[e] = value
        total = total + sum_squares(z, value)
        if e == 1:
            send(d_far.at[pl.ds(0, 2)], d_out)
    send(d_far, carry.at[pl.ds(2, 3)])
    lanes = jnp.sum(total, axis=0, keepdims=True)
    folded = lanes[:, : z.block]
    for t in range(1, z.half):
        folded = folded + lanes[:, t * z.block : (t + 1) * z.block]
    spread[...] = jnp.broadcast_to(folded[None], spread.shape)
    send(spread, spread_out)
    for copy in copies:
        copy.wait()


def outer_step(z, pattern, far, cross, z_cols, turned, p_part, d_part, squares):
    kind = far.dtype
    return pl.pallas_call(
        functools.partial(outer_kernel, z),
        out_shape=(
            z.tiles(2, kind),
            z.tiles(5, kind),
            jax.ShapeDtypeStruct((z.devices, 1, z.block), jnp.float32),
        ),
        in_specs=[SMEM] + [VMEM] * 7,
        out_specs=(HBM, HBM, HBM),
        scratch_shapes=[
            pltpu.VMEM((3, z.tile, z.tile), kind),
            pltpu.VMEM((3, z.tile, z.tile), kind),
            pltpu.VMEM((3, z.tile, z.tile), kind),
            pltpu.VMEM((z.devices, 1, z.block), jnp.float32),
            pltpu.SemaphoreType.DMA((4,)),
        ],
        compiler_params=PARAMS,
        cost_estimate=z.cost(9, 4),
        name="outer",
    )(pattern, far, cross, z_cols, turned, p_part, d_part, squares)


def middle_kernel(
    z, pattern_in, held16_in, held32_in, carry_in, refined, _a, _b, _c, _d, pattern, held16, held32, d_far,
    square, tiles, cells, sems,
):
    first, _ = half_starts(z)
    moves = (
        (pattern_in, pattern),
        (carry_in.at[pl.ds(3, 2)], d_far),
        (held16_in.at[pl.ds(0, 1)], held16.at[pl.ds(0, 1)]),
        (held32_in.at[pl.ds(3, 3)], held32.at[pl.ds(3, 3)]),
        (held16_in.at[pl.ds(3, 7)], held16.at[pl.ds(3, 7)]),
        (held32_in.at[pl.ds(0, 3)], held32.at[pl.ds(0, 3)]),
    )
    copies = [
        pltpu.make_async_copy(source, target, sems.at[k]) for k, (source, target) in enumerate(moves)
    ]
    for copy in copies:
        copy.start()
    for copy in copies[:4]:
        copy.wait()
    for i in (1, 2, 3):
        value = held32[2 + i]
        if i < 3:
            value = value + dot(d_far[i - 1], held16[0])
        square[i - 1] = own_masked(z, pattern, first, i - 1, value).astype(square.dtype)
    for copy in copies[4:]:
        copy.wait()
    for i in (1, 2, 3):
        total = None
        for k in range(max(1, i - 1), min(3, i + 1) + 1):
            term = dot(held16[3 * k - 1 + i - k + 1], square[k - 1])
            total = term if total is None else total + term
        tiles[i - 1] = own_masked(z, pattern, first, i - 1, held32[i - 1] + 0.375 * total)
    store_half(z, tiles, cells)
    copy = pltpu.make_async_copy(cells, refined.at[pl.ds(first, z.half)], sems.at[6])
    copy.start()
    copy.wait()


def middle_step(z, pattern, held16, held32, carry):
    kind = held16.dtype
    shape = (z.columns, z.offsets, z.block, z.block)
    return pl.pallas_call(
        functools.partial(middle_kernel, z),
        out_shape=(
            jax.ShapeDtypeStruct(shape, kind),
            jax.ShapeDtypeStruct(held16.shape, kind),
            jax.ShapeDtypeStruct(held32.shape, jnp.float32),
            jax.ShapeDtypeStruct(carry.shape, kind),
            jax.ShapeDtypeStruct(pattern.shape, pattern.dtype),
        ),
        in_specs=[HBM] * 4,
        out_specs=(HBM,) * 5,
        scratch_shapes=[
            pltpu.SMEM(pattern.shape, pattern.dtype),
            pltpu.VMEM(held16.shape, kind),
            pltpu.VMEM(held32.shape, jnp.float32),
            pltpu.VMEM((2, z.tile, z.tile), kind),
            pltpu.VMEM((3, z.tile, z.tile), kind),
            pltpu.VMEM((3, z.tile, z.tile), jnp.float32),
            pltpu.VMEM((z.half,) + shape[1:], kind),
            pltpu.SemaphoreType.DMA((7,)),
        ],
        input_output_aliases={1: 1, 2: 2, 3: 3, 0: 4},
        compiler_params=PARAMS,
        cost_estimate=z.cost(9, 6),
        name="middle",
    )(pattern, held16, held32, carry)


def last_kernel(
    z, pattern_in, held16, carry, d_in, _, refined, _a, _b, _c, _d, pattern, narrow, d_beyond, square,
    tiles, cells, sems,
):
    _, first = half_starts(z)
    moves = (
        (pattern_in, pattern),
        (d_in, d_beyond),
        (carry.at[pl.ds(2, 3)], narrow.at[pl.ds(0, 3)]),
        (held16.at[pl.ds(0, 2)], narrow.at[pl.ds(3, 2)]),
        (carry.at[pl.ds(0, 2)], narrow.at[pl.ds(5, 2)]),
        (held16.at[pl.ds(2, 5)], narrow.at[pl.ds(7, 5)]),
    )
    copies = [
        pltpu.make_async_copy(source, target, sems.at[k]) for k, (source, target) in enumerate(moves)
    ]
    for copy in copies:
        copy.start()
    for copy in copies[:4]:
        copy.wait()
    values = (
        dot(d_beyond[1], narrow[0]) + dot(narrow[0], narrow[1]),
        dot(d_beyond[0], narrow[0]) + dot(narrow[1], narrow[1]) + dot(narrow[3], narrow[2]),
        dot(narrow[2], narrow[1]) + dot(narrow[4], narrow[2]),
    )
    for i, value in enumerate(values):
        square[i] = own_masked(z, pattern, first, i, value).astype(square.dtype)
    for copy in copies[4:]:
        copy.wait()
    base = (4, 7, 10)
    for i in (0, 1, 2):
        half = None
        rest = None
        for k in range(max(0, i - 1), min(2, i + 1) + 1):
            left = narrow[base[k] + i - k + 1]
            term = dot(left, narrow[k])
            half = term if half is None else half + term
            term = dot(left, square[k])
            rest = term if rest is None else rest + term
        value = narrow[7 + i].astype(jnp.float32) + 0.5 * half + 0.375 * rest
        tiles[i] = own_masked(z, pattern, first, i, value)
    store_half(z, tiles, cells)
    copy = pltpu.make_async_copy(cells, refined.at[pl.ds(first, z.half)], sems.at[6])
    copy.start()
    copy.wait()


def last_step(z, pattern, held16, carry, d_in, refined):
    kind = refined.dtype
    return pl.pallas_call(
        functools.partial(last_kernel, z),
        out_shape=tuple(
            jax.ShapeDtypeStruct(held.shape, held.dtype) for held in (refined, held16, carry, d_in, pattern)
        ),
        in_specs=[HBM] * 5,
        out_specs=(HBM,) * 5,
        scratch_shapes=[
            pltpu.SMEM(pattern.shape, pattern.dtype),
            pltpu.VMEM((12, z.tile, z.tile), kind),
            pltpu.VMEM(d_in.shape, kind),
            pltpu.VMEM((3, z.tile, z.tile), kind),
            pltpu.VMEM((3, z.tile, z.tile), jnp.float32),
            pltpu.VMEM((z.half,) + refined.shape[1:], kind),
            pltpu.SemaphoreType.DMA((7,)),
        ],
        input_output_aliases={4: 0, 1: 1, 2: 2, 3: 3, 0: 4},
        compiler_params=PARAMS,
        cost_estimate=z.cost(21, 4),
        name="last",
    )(pattern, held16, carry, d_in, refined)


def norm_kernel(z, gathered, _, norm):
    mean = jnp.sum(gathered[...]) * (1.0 / z.entries)
    norm[...] = jnp.sqrt(jnp.full(norm.shape, mean, jnp.float32))


def norm_step(z, gathered, after):
    return pl.pallas_call(
        functools.partial(norm_kernel, z),
        out_shape=jax.ShapeDtypeStruct((1, z.block), jnp.float32),
        in_specs=[VMEM, HBM],
        out_specs=VMEM,
        compiler_params=PARAMS,
        name="norm",
    )(gathered, after)


def swaps(pairs):
    return [pair for i, j in pairs for pair in ((i, j), (j, i))]


def per_device(margin, factor, pattern):
    slabs = lax.axis_size("slab")
    devices = lax.axis_size("grp") * slabs
    z = Sizes(margin.shape, margin.shape[0] * slabs, devices)
    if slabs % 2 or z.columns != 2 * z.half:
        raise ValueError("sizes")
    near_pairs = [(i, i + 1) for i in range(0, devices - 1, 2)]
    far_pairs = [(i, i + 1) for i in range(1, devices - 1, 2)]
    inner_pairs = [(i, j) for i, j in far_pairs if j % slabs]
    cross_pairs = [(i, j) for i, j in far_pairs if not j % slabs]
    mask_near = masks(z, pattern, margin.dtype)
    near, far, cross = pack(z, margin, factor, pattern, mask_near)
    beyond = lax.ppermute(far, AXES, swaps(inner_pairs))
    across = lax.ppermute(cross, AXES, swaps(cross_pairs))
    beside = lax.ppermute(near, AXES, swaps(near_pairs))
    z_cols, turned, p_part, d_part, squares, held16, held32, flags = inner_step(
        z, pattern, mask_near, near, far, beside
    )
    d_out, carry, spread = outer_step(
        z, pattern, beyond, across, z_cols, turned, p_part, d_part, squares
    )
    gathered = lax.all_to_all(spread, AXES, 0, 0, tiled=True)
    d_in = lax.ppermute(d_out, AXES, swaps(far_pairs))
    refined, held16, _, carry, flags = middle_step(z, flags, held16, held32, carry)
    refined, held16, _, _, _ = last_step(z, flags, held16, carry, d_in, refined)
    norm = norm_step(z, gathered, held16)
    return refined, norm[0, 0]


def solution(mesh):
    return jax.shard_map(
        per_device,
        mesh=mesh,
        in_specs=(
            P(AXES, None, None, None),
            P(AXES, None, None, None),
            P(AXES, None),
        ),
        out_specs=(P(AXES, None, None, None), P()),
        check_vma=False,
    )
```

```python
import functools

import jax
import jax.numpy as jnp
from jax import lax
from jax.experimental import pallas as pl
from jax.experimental.pallas import tpu as pltpu
from jax.sharding import PartitionSpec as P


AXES = ("grp", "slab")
HBM = pl.BlockSpec(memory_space=pltpu.HBM)
VMEM = pl.BlockSpec(memory_space=pltpu.VMEM)
SMEM = pl.BlockSpec(memory_space=pltpu.SMEM)
PARAMS = pltpu.CompilerParams(vmem_limit_bytes=32 * 1024 * 1024)
FLAG_ROWS = 16


class Sizes:
    def __init__(self, shape, quarter_len, devices):
        self.columns, self.offsets, self.block, _ = shape
        self.half = (self.offsets - 1) // 2
        self.tile = self.half * self.block
        self.cells = self.half * self.offsets
        self.flag_blocks = -(-self.half * self.half * FLAG_ROWS // self.block)
        self.quarter_len = quarter_len
        self.devices = devices
        self.entries = self.columns * devices * self.block

    def cost(self, products, moved):
        return pl.CostEstimate(
            flops=products * 2 * self.tile**3, bytes_accessed=moved * 2**20, transcendentals=0
        )

    def tiles(self, count, dtype):
        return jax.ShapeDtypeStruct((count, self.tile, self.tile), dtype)


def odd_device():
    return lax.rem(lax.axis_index("slab"), 2)


def half_starts(z):
    near = jnp.where(odd_device() == 1, 0, z.columns - z.half)
    return near, z.columns - z.half - near


def keep(flag, value):
    return jnp.where(flag, value, jnp.zeros_like(value))


def dot(left, right):
    return jnp.dot(left, right, preferred_element_type=jnp.float32)


def chain_tile(true_tile):
    return jnp.where(odd_device() == 1, 2 - true_tile, true_tile)


def expand(z, out, read):
    block = z.block
    for t in range(z.half):
        for a in range(3 * z.half):
            o = a - t
            u = a % z.half
            if 0 <= o < z.offsets:
                value = read(t, o)
            else:
                value = jnp.zeros((block, block), out.dtype)
            out[
                chain_tile(a // z.half),
                u * block : (u + 1) * block,
                t * block : (t + 1) * block,
            ] = value


def offset_of(z, e, t, u):
    return jnp.where(odd_device() == 1, 1 - e, e - 1) * z.half + u - t + z.half


def flag_of(z, pattern, first, e, t, u):
    o = offset_of(z, e, t, u)
    inside = jnp.logical_and(o >= 0, o < z.offsets)
    return jnp.logical_and(inside, pattern[first + t, jnp.clip(o, 0, z.offsets - 1)] != 0)


def masked(z, value, flag):
    block = z.block
    rows = []
    for u in range(z.half):
        rows.append(
            jnp.concatenate(
                [
                    keep(
                        flag(t, u),
                        value[u * block : (u + 1) * block, t * block : (t + 1) * block],
                    )
                    for t in range(z.half)
                ],
                axis=1,
            )
        )
    return jnp.concatenate(rows, axis=0)


def own_masked(z, pattern, first, e, value):
    return masked(z, value, lambda t, u: flag_of(z, pattern, first, e, t, u))


def identity(z):
    shape = (z.tile, z.tile)
    rows = lax.broadcasted_iota(jnp.int32, shape, 0)
    return (rows == lax.broadcasted_iota(jnp.int32, shape, 1)).astype(jnp.float32)


def tile_product(left, right, i, c, low, high):
    total = None
    for k in range(max(low, i - 1, c - 1), min(high, i + 1, c + 1) + 1):
        term = dot(left[k][i - k + 1], right[k - c + 1])
        total = term if total is None else total + term
    return total


def sum_squares(z, value):
    wide = value.astype(jnp.float32)
    return jnp.sum((wide * wide).reshape(-1, 8, z.tile), axis=0)


def store_half(z, tiles, cells):
    block = z.block
    for t in range(z.half):
        for o in range(z.offsets):
            a = t + o
            u = a % z.half
            value = tiles[
                chain_tile(a // z.half),
                u * block : (u + 1) * block,
                t * block : (t + 1) * block,
            ]
            cells[t, o] = value.astype(cells.dtype)


def unit_kernel(z, unit):
    unit[...] = identity(z)


def unit_tile(z):
    return pl.pallas_call(
        functools.partial(unit_kernel, z),
        out_shape=jax.ShapeDtypeStruct((z.tile, z.tile), jnp.float32),
        out_specs=VMEM,
        compiler_params=PARAMS,
        cost_estimate=z.cost(20, 1),
        name="unit",
    )()


def pack_kernel(z, margin, factor, pattern, _, near, far, cross):
    near_first, far_first = half_starts(z)
    first_row = lax.axis_index("slab") * z.columns
    plan = ((margin, far_first), (factor, far_first), (margin, near_first), (factor, near_first))
    for k, (source, first) in enumerate(plan):
        for t in range(z.half):
            for o in range(z.offsets):
                flag = pattern[first + t, o] != 0
                if k % 2:
                    row = first_row + first + t + o - z.half
                    inside = jnp.logical_and(row >= 0, row < z.quarter_len)
                    flag = jnp.logical_and(flag, inside)
                value = keep(flag, source[first + t, o])
                cell = t * z.offsets + o
                u = o + t - z.half
                if k == 0:
                    far[cell] = value
                    near[2 * z.cells + cell] = value
                elif k == 1:
                    far[z.cells + cell] = value
                    if 0 <= u < z.half:
                        cross[t, u] = value
                else:
                    near[(k - 2) * z.cells + cell] = value
    per_block = z.block // FLAG_ROWS
    for f in range(z.flag_blocks * per_block):
        t, u = f // z.half, f % z.half
        value = jnp.zeros((FLAG_ROWS, z.block), near.dtype)
        if t < z.half:
            value = keep(pattern[near_first + t, u - t + z.half] != 0, jnp.ones_like(value))
        low = f % per_block * FLAG_ROWS
        near[3 * z.cells + f // per_block, low : low + FLAG_ROWS] = value


def pack(z, margin, factor, pattern, unit):
    kind = margin.dtype
    return pl.pallas_call(
        functools.partial(pack_kernel, z),
        out_shape=(
            jax.ShapeDtypeStruct((3 * z.cells + z.flag_blocks, z.block, z.block), kind),
            jax.ShapeDtypeStruct((2 * z.cells, z.block, z.block), kind),
            jax.ShapeDtypeStruct((z.half, z.half, z.block, z.block), kind),
        ),
        in_specs=[VMEM, VMEM, SMEM, VMEM],
        out_specs=(VMEM, VMEM, VMEM),
        compiler_params=PARAMS,
        name="pack",
    )(margin, factor, pattern, unit)


def inner_kernel(
    z, pattern, unit, near, far, beside, z_cols, turned, p_part, d_part, squares, held16, held32,
    flags, s_cols, z_turned, image, d_near, d_beside, sums, sems,
):
    near_first, _ = half_starts(z)
    kind = near.dtype

    def cells_of(ref, base):
        return lambda t, o: ref[base + t * z.offsets + o]

    expand(z, s_cols.at[0], cells_of(far, 0))
    expand(z, s_cols.at[1], cells_of(near, 0))
    expand(z, s_cols.at[2], cells_of(beside, 0))
    expand(z, s_cols.at[3], cells_of(beside, 2 * z.cells))
    expand(z, z_cols.at[0], cells_of(far, z.cells))
    expand(z, z_cols.at[1], cells_of(near, z.cells))
    expand(z, z_cols.at[2], cells_of(beside, z.cells))
    moves = [
        (z_cols.at[0], held16.at[pl.ds(2, 3)]),
        (z_cols.at[1], held16.at[pl.ds(5, 3)]),
        (z_cols.at[2, pl.ds(0, 2)], held16.at[pl.ds(8, 2)]),
        (pattern, flags),
        (d_near.at[pl.ds(0, 2)], held16.at[pl.ds(0, 2)]),
        (sums, held32),
    ]
    copies = [
        pltpu.make_async_copy(source, target, sems.at[k]) for k, (source, target) in enumerate(moves)
    ]
    for copy in copies[:4]:
        copy.start()
    for x in range(3):
        for e in range(3):
            z_turned[x, e] = z_cols[x, e].T
    turned[0] = z_turned[0, 0]
    turned[1] = z_turned[0, 1]
    turned[2] = z_turned[1, 0]

    def image_tile(y, c):
        total = None
        for inner in range(max(c - 1, y - 1, 1), min(c + 1, y + 1) + 1):
            term = dot(s_cols[inner - 1, y - inner + 1], z_cols[c - 1, inner - c + 1])
            total = term if total is None else total + term
        return total

    def turned_sum(i, c, rows):
        total = None
        for m in rows:
            term = dot(z_turned[i - 1, m - i + 1], image[c - 1, m])
            total = term if total is None else total + term
        return total

    p_part[0] = image_tile(0, 1)
    p_part[1] = image_tile(1, 1)
    for c, rows in ((1, (2, 3)), (2, (0, 1, 2, 3, 4)), (3, (1, 2, 3, 4))):
        for y in rows:
            image[c - 1, y] = image_tile(y, c).astype(kind)
    d_part[0] = turned_sum(1, 1, (2,))
    d_part[1] = turned_sum(2, 1, (2, 3))
    eye = unit[...]
    total = jnp.zeros((8, z.tile), jnp.float32)
    for i in (1, 2, 3):
        value = -turned_sum(i, 2, (i - 1, i, i + 1))
        if i == 2:
            value = eye + value
        value = own_masked(z, pattern, near_first, i - 1, value).astype(kind)
        d_near[i - 1] = value
        total = total + sum_squares(z, value)
    squares[...] = total
    copies[4].start()

    def side_flag(t, u):
        o = offset_of(z, 0, t, u)
        inside = jnp.logical_and(o >= 0, o < z.offsets)
        back = jnp.clip(z.offsets - 1 - o, 0, z.offsets - 1)
        return jnp.logical_and(inside, pattern[near_first + u, back] != 0)

    d_beside[0] = masked(z, -turned_sum(2, 3, (1, 2, 3)), side_flag).astype(kind)
    value = eye - turned_sum(3, 3, (2, 3, 4))
    block = z.block
    per_block = block // FLAG_ROWS
    for t in range(z.half):
        for u in range(z.half):
            f = t * z.half + u
            low = f % per_block * FLAG_ROWS
            flags = beside[3 * z.cells + f // per_block, low : low + FLAG_ROWS]
            flag = flags.astype(jnp.float32)[:1]
            part = (slice(u * block, (u + 1) * block), slice(t * block, (t + 1) * block))
            d_beside[1, part[0], part[1]] = (value[part] * flag).astype(kind)

    factor = (None, z_cols.at[0], z_cols.at[1], z_cols.at[2])
    defect = (None, None, d_near, d_beside)
    for i in (1, 2, 3):
        sums[i - 1] = z_cols[1, i - 1].astype(jnp.float32) + 0.5 * tile_product(
            factor, d_near, i, 2, 1, 3
        )
        sums[2 + i] = tile_product(defect, d_near, i, 2, 2, 3)
    copies[5].start()
    for copy in copies:
        copy.wait()


def inner_step(z, pattern, unit, near, far, beside):
    kind = near.dtype
    tile = z.tile
    return pl.pallas_call(
        functools.partial(inner_kernel, z),
        out_shape=(
            jax.ShapeDtypeStruct((3, 3, tile, tile), kind),
            z.tiles(3, kind),
            z.tiles(2, jnp.float32),
            z.tiles(2, jnp.float32),
            jax.ShapeDtypeStruct((8, tile), jnp.float32),
            z.tiles(10, kind),
            z.tiles(6, jnp.float32),
            jax.ShapeDtypeStruct(pattern.shape, pattern.dtype),
        ),
        in_specs=[SMEM, VMEM, VMEM, VMEM, VMEM],
        out_specs=(VMEM,) * 5 + (HBM,) * 3,
        scratch_shapes=[
            pltpu.VMEM((4, 3, tile, tile), kind),
            pltpu.VMEM((3, 3, tile, tile), kind),
            pltpu.VMEM((3, 5, tile, tile), kind),
            pltpu.VMEM((3, tile, tile), kind),
            pltpu.VMEM((2, tile, tile), kind),
            pltpu.VMEM((6, tile, tile), jnp.float32),
            pltpu.SemaphoreType.DMA((6,)),
        ],
        compiler_params=PARAMS,
        cost_estimate=z.cost(54, 8),
        name="inner",
    )(pattern, unit, near, far, beside)


def outer_kernel(
    z, pattern, unit, far, cross, z_cols, turned, p_part, d_part, squares, d_out, carry, spread_out, s_far,
    z_far, d_far, spread, sems,
):
    _, far_first = half_starts(z)
    kind = far.dtype

    def factor_cell(t, o):
        value = far[z.cells + t * z.offsets + o]
        u = o + t - z.half
        if 0 <= u < z.half:
            value = value + cross[t, u]
        return value

    expand(z, s_far, lambda t, o: far[t * z.offsets + o])
    expand(z, z_far, factor_cell)
    copies = []

    def send(source, target):
        copies.append(pltpu.make_async_copy(source, target, sems.at[len(copies)]))
        copies[-1].start()

    send(z_far.at[pl.ds(1, 2)], carry.at[pl.ds(0, 2)])
    link = z_cols[0, 0]
    image = (
        dot(s_far[0], link).astype(kind),
        (dot(s_far[1], link) + p_part[0]).astype(kind),
        (dot(s_far[2], link) + p_part[1]).astype(kind),
    )
    values = (
        -(dot(z_far[0].T, image[0]) + dot(z_far[1].T, image[1]) + dot(z_far[2].T, image[2])),
        unit[...] - (dot(turned[0], image[1]) + dot(turned[1], image[2]) + d_part[0]),
        -(dot(turned[2], image[2]) + d_part[1]),
    )
    total = squares[...]
    for e, value in enumerate(values):
        value = own_masked(z, pattern, far_first, e, value).astype(kind)
        d_far[e] = value
        total = total + sum_squares(z, value)
        if e == 1:
            send(d_far.at[pl.ds(0, 2)], d_out)
    send(d_far, carry.at[pl.ds(2, 3)])
    lanes = jnp.sum(total, axis=0, keepdims=True)
    folded = lanes[:, : z.block]
    for t in range(1, z.half):
        folded = folded + lanes[:, t * z.block : (t + 1) * z.block]
    spread[...] = jnp.broadcast_to(folded[None], spread.shape)
    send(spread, spread_out)
    for copy in copies:
        copy.wait()


def outer_step(z, pattern, unit, far, cross, z_cols, turned, p_part, d_part, squares):
    kind = far.dtype
    return pl.pallas_call(
        functools.partial(outer_kernel, z),
        out_shape=(
            z.tiles(2, kind),
            z.tiles(5, kind),
            jax.ShapeDtypeStruct((z.devices, 1, z.block), jnp.float32),
        ),
        in_specs=[SMEM] + [VMEM] * 8,
        out_specs=(HBM, HBM, HBM),
        scratch_shapes=[
            pltpu.VMEM((3, z.tile, z.tile), kind),
            pltpu.VMEM((3, z.tile, z.tile), kind),
            pltpu.VMEM((3, z.tile, z.tile), kind),
            pltpu.VMEM((z.devices, 1, z.block), jnp.float32),
            pltpu.SemaphoreType.DMA((4,)),
        ],
        compiler_params=PARAMS,
        cost_estimate=z.cost(9, 4),
        name="outer",
    )(pattern, unit, far, cross, z_cols, turned, p_part, d_part, squares)


def middle_kernel(
    z, pattern_in, held16_in, held32_in, carry_in, refined, _a, _b, _c, _d, pattern, held16, held32, d_far,
    square, tiles, cells, sems,
):
    first, _ = half_starts(z)
    moves = (
        (pattern_in, pattern),
        (carry_in.at[pl.ds(3, 2)], d_far),
        (held16_in.at[pl.ds(0, 1)], held16.at[pl.ds(0, 1)]),
        (held32_in.at[pl.ds(3, 3)], held32.at[pl.ds(3, 3)]),
        (held16_in.at[pl.ds(3, 7)], held16.at[pl.ds(3, 7)]),
        (held32_in.at[pl.ds(0, 3)], held32.at[pl.ds(0, 3)]),
    )
    copies = [
        pltpu.make_async_copy(source, target, sems.at[k]) for k, (source, target) in enumerate(moves)
    ]
    for copy in copies:
        copy.start()
    for copy in copies[:4]:
        copy.wait()
    for i in (1, 2, 3):
        value = held32[2 + i]
        if i < 3:
            value = value + dot(d_far[i - 1], held16[0])
        square[i - 1] = own_masked(z, pattern, first, i - 1, value).astype(square.dtype)
    for copy in copies[4:]:
        copy.wait()
    for i in (1, 2, 3):
        total = None
        for k in range(max(1, i - 1), min(3, i + 1) + 1):
            term = dot(held16[3 * k - 1 + i - k + 1], square[k - 1])
            total = term if total is None else total + term
        tiles[i - 1] = own_masked(z, pattern, first, i - 1, held32[i - 1] + 0.375 * total)
    store_half(z, tiles, cells)
    copy = pltpu.make_async_copy(cells, refined.at[pl.ds(first, z.half)], sems.at[6])
    copy.start()
    copy.wait()


def middle_step(z, pattern, held16, held32, carry):
    kind = held16.dtype
    shape = (z.columns, z.offsets, z.block, z.block)
    return pl.pallas_call(
        functools.partial(middle_kernel, z),
        out_shape=(
            jax.ShapeDtypeStruct(shape, kind),
            jax.ShapeDtypeStruct(held16.shape, kind),
            jax.ShapeDtypeStruct(held32.shape, jnp.float32),
            jax.ShapeDtypeStruct(carry.shape, kind),
            jax.ShapeDtypeStruct(pattern.shape, pattern.dtype),
        ),
        in_specs=[HBM] * 4,
        out_specs=(HBM,) * 5,
        scratch_shapes=[
            pltpu.SMEM(pattern.shape, pattern.dtype),
            pltpu.VMEM(held16.shape, kind),
            pltpu.VMEM(held32.shape, jnp.float32),
            pltpu.VMEM((2, z.tile, z.tile), kind),
            pltpu.VMEM((3, z.tile, z.tile), kind),
            pltpu.VMEM((3, z.tile, z.tile), jnp.float32),
            pltpu.VMEM((z.half,) + shape[1:], kind),
            pltpu.SemaphoreType.DMA((7,)),
        ],
        input_output_aliases={1: 1, 2: 2, 3: 3, 0: 4},
        compiler_params=PARAMS,
        cost_estimate=z.cost(9, 6),
        name="middle",
    )(pattern, held16, held32, carry)


def last_kernel(
    z, pattern_in, held16, carry, d_in, _, refined, _a, _b, _c, _d, pattern, narrow, d_beyond, square,
    tiles, cells, sems,
):
    _, first = half_starts(z)
    moves = (
        (pattern_in, pattern),
        (d_in, d_beyond),
        (carry.at[pl.ds(2, 3)], narrow.at[pl.ds(0, 3)]),
        (held16.at[pl.ds(0, 2)], narrow.at[pl.ds(3, 2)]),
        (carry.at[pl.ds(0, 2)], narrow.at[pl.ds(5, 2)]),
        (held16.at[pl.ds(2, 5)], narrow.at[pl.ds(7, 5)]),
    )
    copies = [
        pltpu.make_async_copy(source, target, sems.at[k]) for k, (source, target) in enumerate(moves)
    ]
    for copy in copies:
        copy.start()
    for copy in copies[:4]:
        copy.wait()
    values = (
        dot(d_beyond[1], narrow[0]) + dot(narrow[0], narrow[1]),
        dot(d_beyond[0], narrow[0]) + dot(narrow[1], narrow[1]) + dot(narrow[3], narrow[2]),
        dot(narrow[2], narrow[1]) + dot(narrow[4], narrow[2]),
    )
    for i, value in enumerate(values):
        square[i] = own_masked(z, pattern, first, i, value).astype(square.dtype)
    for copy in copies[4:]:
        copy.wait()
    base = (4, 7, 10)
    for i in (0, 1, 2):
        half = None
        rest = None
        for k in range(max(0, i - 1), min(2, i + 1) + 1):
            left = narrow[base[k] + i - k + 1]
            term = dot(left, narrow[k])
            half = term if half is None else half + term
            term = dot(left, square[k])
            rest = term if rest is None else rest + term
        value = narrow[7 + i].astype(jnp.float32) + 0.5 * half + 0.375 * rest
        tiles[i] = own_masked(z, pattern, first, i, value)
    store_half(z, tiles, cells)
    copy = pltpu.make_async_copy(cells, refined.at[pl.ds(first, z.half)], sems.at[6])
    copy.start()
    copy.wait()


def last_step(z, pattern, held16, carry, d_in, refined):
    kind = refined.dtype
    return pl.pallas_call(
        functools.partial(last_kernel, z),
        out_shape=tuple(
            jax.ShapeDtypeStruct(held.shape, held.dtype) for held in (refined, held16, carry, d_in, pattern)
        ),
        in_specs=[HBM] * 5,
        out_specs=(HBM,) * 5,
        scratch_shapes=[
            pltpu.SMEM(pattern.shape, pattern.dtype),
            pltpu.VMEM((12, z.tile, z.tile), kind),
            pltpu.VMEM(d_in.shape, kind),
            pltpu.VMEM((3, z.tile, z.tile), kind),
            pltpu.VMEM((3, z.tile, z.tile), jnp.float32),
            pltpu.VMEM((z.half,) + refined.shape[1:], kind),
            pltpu.SemaphoreType.DMA((7,)),
        ],
        input_output_aliases={4: 0, 1: 1, 2: 2, 3: 3, 0: 4},
        compiler_params=PARAMS,
        cost_estimate=z.cost(21, 4),
        name="last",
    )(pattern, held16, carry, d_in, refined)


def norm_kernel(z, gathered, _, norm):
    mean = jnp.sum(gathered[...]) * (1.0 / z.entries)
    norm[...] = jnp.sqrt(jnp.full(norm.shape, mean, jnp.float32))


def norm_step(z, gathered, after):
    return pl.pallas_call(
        functools.partial(norm_kernel, z),
        out_shape=jax.ShapeDtypeStruct((1, z.block), jnp.float32),
        in_specs=[VMEM, HBM],
        out_specs=VMEM,
        compiler_params=PARAMS,
        name="norm",
    )(gathered, after)


def swaps(pairs):
    return [pair for i, j in pairs for pair in ((i, j), (j, i))]


def per_device(margin, factor, pattern):
    slabs = lax.axis_size("slab")
    devices = lax.axis_size("grp") * slabs
    z = Sizes(margin.shape, margin.shape[0] * slabs, devices)
    if slabs % 2 or z.columns != 2 * z.half:
        raise ValueError("sizes")
    near_pairs = [(i, i + 1) for i in range(0, devices - 1, 2)]
    far_pairs = [(i, i + 1) for i in range(1, devices - 1, 2)]
    inner_pairs = [(i, j) for i, j in far_pairs if j % slabs]
    cross_pairs = [(i, j) for i, j in far_pairs if not j % slabs]
    unit = unit_tile(z)
    near, far, cross = pack(z, margin, factor, pattern, unit)
    beyond = lax.ppermute(far, AXES, swaps(inner_pairs))
    across = lax.ppermute(cross, AXES, swaps(cross_pairs))
    beside = lax.ppermute(near, AXES, swaps(near_pairs))
    z_cols, turned, p_part, d_part, squares, held16, held32, flags = inner_step(
        z, pattern, unit, near, far, beside
    )
    d_out, carry, spread = outer_step(
        z, pattern, unit, beyond, across, z_cols, turned, p_part, d_part, squares
    )
    gathered = lax.all_to_all(spread, AXES, 0, 0, tiled=True)
    d_in = lax.ppermute(d_out, AXES, swaps(far_pairs))
    refined, held16, _, carry, flags = middle_step(z, flags, held16, held32, carry)
    refined, held16, _, _, _ = last_step(z, flags, held16, carry, d_in, refined)
    norm = norm_step(z, gathered, held16)
    return refined, norm[0, 0]


def solution(mesh):
    return jax.shard_map(
        per_device,
        mesh=mesh,
        in_specs=(
            P(AXES, None, None, None),
            P(AXES, None, None, None),
            P(AXES, None),
        ),
        out_specs=(P(AXES, None, None, None), P()),
        check_vma=False,
    )
```

```python
import functools

import jax
import jax.numpy as jnp
from jax import lax
from jax.experimental import pallas as pl
from jax.experimental.pallas import tpu as pltpu
from jax.sharding import PartitionSpec as P


AXES = ("grp", "slab")
HBM = pl.BlockSpec(memory_space=pltpu.HBM)
VMEM = pl.BlockSpec(memory_space=pltpu.VMEM)
SMEM = pl.BlockSpec(memory_space=pltpu.SMEM)
PARAMS = pltpu.CompilerParams(vmem_limit_bytes=32 * 1024 * 1024)
FLAG_ROWS = 16


class Sizes:
    def __init__(self, shape, quarter_len, devices):
        self.columns, self.offsets, self.block, _ = shape
        self.half = (self.offsets - 1) // 2
        self.tile = self.half * self.block
        self.cells = self.half * self.offsets
        self.flag_blocks = -(-self.half * self.half * FLAG_ROWS // self.block)
        self.quarter_len = quarter_len
        self.devices = devices
        self.entries = self.columns * devices * self.block

    def cost(self, products, moved):
        return pl.CostEstimate(
            flops=products * 2 * self.tile**3, bytes_accessed=moved * 2**20, transcendentals=0
        )

    def tiles(self, count, dtype):
        return jax.ShapeDtypeStruct((count, self.tile, self.tile), dtype)


def odd_device():
    return lax.rem(lax.axis_index("slab"), 2)


def half_starts(z):
    near = jnp.where(odd_device() == 1, 0, z.columns - z.half)
    return near, z.columns - z.half - near


def keep(flag, value):
    return jnp.where(flag, value, jnp.zeros_like(value))


def dot(left, right):
    return jnp.dot(left, right, preferred_element_type=jnp.float32)


def chain_tile(true_tile):
    return jnp.where(odd_device() == 1, 2 - true_tile, true_tile)


def expand(z, out, read):
    block = z.block
    for t in range(z.half):
        for a in range(3 * z.half):
            o = a - t
            u = a % z.half
            if 0 <= o < z.offsets:
                value = read(t, o)
            else:
                value = jnp.zeros((block, block), out.dtype)
            out[
                chain_tile(a // z.half),
                u * block : (u + 1) * block,
                t * block : (t + 1) * block,
            ] = value


def offset_of(z, e, t, u):
    return jnp.where(odd_device() == 1, 1 - e, e - 1) * z.half + u - t + z.half


def flag_of(z, pattern, first, e, t, u):
    o = offset_of(z, e, t, u)
    inside = jnp.logical_and(o >= 0, o < z.offsets)
    return jnp.logical_and(inside, pattern[first + t, jnp.clip(o, 0, z.offsets - 1)] != 0)


def masked(z, value, flag):
    block = z.block
    rows = []
    for u in range(z.half):
        rows.append(
            jnp.concatenate(
                [
                    keep(
                        flag(t, u),
                        value[u * block : (u + 1) * block, t * block : (t + 1) * block],
                    )
                    for t in range(z.half)
                ],
                axis=1,
            )
        )
    return jnp.concatenate(rows, axis=0)


def own_masked(z, pattern, first, e, value):
    return masked(z, value, lambda t, u: flag_of(z, pattern, first, e, t, u))


def identity(z):
    shape = (z.tile, z.tile)
    rows = lax.broadcasted_iota(jnp.int32, shape, 0)
    return (rows == lax.broadcasted_iota(jnp.int32, shape, 1)).astype(jnp.float32)


def tile_product(left, right, i, c, low, high):
    total = None
    for k in range(max(low, i - 1, c - 1), min(high, i + 1, c + 1) + 1):
        term = dot(left[k][i - k + 1], right[k - c + 1])
        total = term if total is None else total + term
    return total


def sum_squares(z, value):
    wide = value.astype(jnp.float32)
    return jnp.sum((wide * wide).reshape(-1, 8, z.tile), axis=0)


def store_half(z, tiles, cells):
    block = z.block
    for t in range(z.half):
        for o in range(z.offsets):
            a = t + o
            u = a % z.half
            value = tiles[
                chain_tile(a // z.half),
                u * block : (u + 1) * block,
                t * block : (t + 1) * block,
            ]
            cells[t, o] = value.astype(cells.dtype)


def unit_kernel(z, unit):
    unit[...] = identity(z)


def unit_tile(z):
    return pl.pallas_call(
        functools.partial(unit_kernel, z),
        out_shape=jax.ShapeDtypeStruct((z.tile, z.tile), jnp.float32),
        out_specs=VMEM,
        compiler_params=PARAMS,
        cost_estimate=z.cost(20, 1),
        name="unit",
    )()


def pack_kernel(z, margin, factor, pattern, _, near, far, cross):
    near_first, far_first = half_starts(z)
    first_row = lax.axis_index("slab") * z.columns
    plan = ((margin, far_first), (factor, far_first), (margin, near_first), (factor, near_first))
    for k, (source, first) in enumerate(plan):
        for t in range(z.half):
            for o in range(z.offsets):
                flag = pattern[first + t, o] != 0
                if k % 2:
                    row = first_row + first + t + o - z.half
                    inside = jnp.logical_and(row >= 0, row < z.quarter_len)
                    flag = jnp.logical_and(flag, inside)
                value = keep(flag, source[first + t, o])
                cell = t * z.offsets + o
                u = o + t - z.half
                if k == 0:
                    far[cell] = value
                    near[2 * z.cells + cell] = value
                elif k == 1:
                    far[z.cells + cell] = value
                    if 0 <= u < z.half:
                        cross[t, u] = value
                else:
                    near[(k - 2) * z.cells + cell] = value
    per_block = z.block // FLAG_ROWS
    for f in range(z.flag_blocks * per_block):
        t, u = f // z.half, f % z.half
        value = jnp.zeros((FLAG_ROWS, z.block), near.dtype)
        if t < z.half:
            value = keep(pattern[near_first + t, u - t + z.half] != 0, jnp.ones_like(value))
        low = f % per_block * FLAG_ROWS
        near[3 * z.cells + f // per_block, low : low + FLAG_ROWS] = value


def pack(z, margin, factor, pattern, unit):
    kind = margin.dtype
    return pl.pallas_call(
        functools.partial(pack_kernel, z),
        out_shape=(
            jax.ShapeDtypeStruct((3 * z.cells + z.flag_blocks, z.block, z.block), kind),
            jax.ShapeDtypeStruct((2 * z.cells, z.block, z.block), kind),
            jax.ShapeDtypeStruct((z.half, z.half, z.block, z.block), kind),
        ),
        in_specs=[VMEM, VMEM, SMEM, VMEM],
        out_specs=(VMEM, VMEM, VMEM),
        compiler_params=PARAMS,
        name="pack",
    )(margin, factor, pattern, unit)


def inner_kernel(
    z, pattern, unit, near, far, beside, z_cols, turned, p_part, d_part, squares, held16, held32,
    flags, s_cols, z_turned, image, d_near, d_beside, sums, sems,
):
    near_first, _ = half_starts(z)
    kind = near.dtype

    def cells_of(ref, base):
        return lambda t, o: ref[base + t * z.offsets + o]

    expand(z, s_cols.at[0], cells_of(far, 0))
    expand(z, s_cols.at[1], cells_of(near, 0))
    expand(z, s_cols.at[2], cells_of(beside, 0))
    expand(z, s_cols.at[3], cells_of(beside, 2 * z.cells))
    expand(z, z_cols.at[0], cells_of(far, z.cells))
    expand(z, z_cols.at[1], cells_of(near, z.cells))
    expand(z, z_cols.at[2], cells_of(beside, z.cells))
    moves = [
        (z_cols.at[0], held16.at[pl.ds(2, 3)]),
        (z_cols.at[1], held16.at[pl.ds(5, 3)]),
        (z_cols.at[2, pl.ds(0, 2)], held16.at[pl.ds(8, 2)]),
        (pattern, flags),
        (d_near.at[pl.ds(0, 2)], held16.at[pl.ds(0, 2)]),
        (sums, held32),
    ]
    copies = [
        pltpu.make_async_copy(source, target, sems.at[k]) for k, (source, target) in enumerate(moves)
    ]
    for copy in copies[:4]:
        copy.start()
    for x in range(3):
        for e in range(3):
            z_turned[x, e] = z_cols[x, e].T
    turned[0] = z_turned[0, 0]
    turned[1] = z_turned[0, 1]
    turned[2] = z_turned[1, 0]

    def image_tile(y, c):
        total = None
        for inner in range(max(c - 1, y - 1, 1), min(c + 1, y + 1) + 1):
            term = dot(s_cols[inner - 1, y - inner + 1], z_cols[c - 1, inner - c + 1])
            total = term if total is None else total + term
        return total

    def turned_sum(i, c, rows):
        total = None
        for m in rows:
            term = dot(z_turned[i - 1, m - i + 1], image[c - 1, m])
            total = term if total is None else total + term
        return total

    p_part[0] = image_tile(0, 1)
    p_part[1] = image_tile(1, 1)
    for c, rows in ((1, (2, 3)), (2, (0, 1, 2, 3, 4)), (3, (1, 2, 3, 4))):
        for y in rows:
            image[c - 1, y] = image_tile(y, c).astype(kind)
    d_part[0] = turned_sum(1, 1, (2,))
    d_part[1] = turned_sum(2, 1, (2, 3))
    eye = unit[...]
    total = jnp.zeros((8, z.tile), jnp.float32)
    for i in (1, 2, 3):
        value = -turned_sum(i, 2, (i - 1, i, i + 1))
        if i == 2:
            value = eye + value
        value = own_masked(z, pattern, near_first, i - 1, value).astype(kind)
        d_near[i - 1] = value
        total = total + sum_squares(z, value)
    squares[...] = total
    copies[4].start()

    def side_flag(t, u):
        o = offset_of(z, 0, t, u)
        inside = jnp.logical_and(o >= 0, o < z.offsets)
        back = jnp.clip(z.offsets - 1 - o, 0, z.offsets - 1)
        return jnp.logical_and(inside, pattern[near_first + u, back] != 0)

    d_beside[0] = masked(z, -turned_sum(2, 3, (1, 2, 3)), side_flag).astype(kind)
    value = eye - turned_sum(3, 3, (2, 3, 4))
    block = z.block
    per_block = block // FLAG_ROWS
    for t in range(z.half):
        for u in range(z.half):
            f = t * z.half + u
            low = f % per_block * FLAG_ROWS
            flags = beside[3 * z.cells + f // per_block, low : low + FLAG_ROWS]
            flag = flags.astype(jnp.float32)[:1]
            part = (slice(u * block, (u + 1) * block), slice(t * block, (t + 1) * block))
            d_beside[1, part[0], part[1]] = (value[part] * flag).astype(kind)

    factor = (None, z_cols.at[0], z_cols.at[1], z_cols.at[2])
    defect = (None, None, d_near, d_beside)
    for i in (1, 2, 3):
        sums[i - 1] = z_cols[1, i - 1].astype(jnp.float32) + 0.5 * tile_product(
            factor, d_near, i, 2, 1, 3
        )
        sums[2 + i] = tile_product(defect, d_near, i, 2, 2, 3)
    copies[5].start()
    for copy in copies:
        copy.wait()


def inner_step(z, pattern, unit, near, far, beside):
    kind = near.dtype
    tile = z.tile
    return pl.pallas_call(
        functools.partial(inner_kernel, z),
        out_shape=(
            jax.ShapeDtypeStruct((3, 3, tile, tile), kind),
            z.tiles(3, kind),
            z.tiles(2, jnp.float32),
            z.tiles(2, jnp.float32),
            jax.ShapeDtypeStruct((8, tile), jnp.float32),
            z.tiles(10, kind),
            z.tiles(6, jnp.float32),
            jax.ShapeDtypeStruct(pattern.shape, pattern.dtype),
        ),
        in_specs=[SMEM, VMEM, VMEM, VMEM, VMEM],
        out_specs=(VMEM,) * 5 + (HBM,) * 3,
        scratch_shapes=[
            pltpu.VMEM((4, 3, tile, tile), kind),
            pltpu.VMEM((3, 3, tile, tile), kind),
            pltpu.VMEM((3, 5, tile, tile), kind),
            pltpu.VMEM((3, tile, tile), kind),
            pltpu.VMEM((2, tile, tile), kind),
            pltpu.VMEM((6, tile, tile), jnp.float32),
            pltpu.SemaphoreType.DMA((6,)),
        ],
        compiler_params=PARAMS,
        cost_estimate=z.cost(54, 8),
        name="inner",
    )(pattern, unit, near, far, beside)


def outer_kernel(
    z, pattern, unit, far, cross, z_cols, turned, p_part, d_part, squares, d_out, carry, spread, s_far,
    z_far, d_pair, sem,
):
    _, far_first = half_starts(z)
    kind = far.dtype

    def factor_cell(t, o):
        value = far[z.cells + t * z.offsets + o]
        u = o + t - z.half
        if 0 <= u < z.half:
            value = value + cross[t, u]
        return value

    expand(z, s_far, lambda t, o: far[t * z.offsets + o])
    expand(z, z_far, factor_cell)
    carry[0] = z_far[1]
    carry[1] = z_far[2]
    copy = pltpu.make_async_copy(d_pair, d_out, sem)
    link = z_cols[0, 0]
    image = (
        dot(s_far[0], link).astype(kind),
        (dot(s_far[1], link) + p_part[0]).astype(kind),
        (dot(s_far[2], link) + p_part[1]).astype(kind),
    )
    values = (
        -(dot(z_far[0].T, image[0]) + dot(z_far[1].T, image[1]) + dot(z_far[2].T, image[2])),
        unit[...] - (dot(turned[0], image[1]) + dot(turned[1], image[2]) + d_part[0]),
        -(dot(turned[2], image[2]) + d_part[1]),
    )
    total = squares[...]
    for e, value in enumerate(values):
        value = own_masked(z, pattern, far_first, e, value).astype(kind)
        carry[2 + e] = value
        if e < 2:
            d_pair[e] = value
        if e == 1:
            copy.start()
        total = total + sum_squares(z, value)
    lanes = jnp.sum(total, axis=0, keepdims=True)
    folded = lanes[:, : z.block]
    for t in range(1, z.half):
        folded = folded + lanes[:, t * z.block : (t + 1) * z.block]
    spread[...] = jnp.broadcast_to(folded[None], spread.shape)
    copy.wait()


def outer_step(z, pattern, unit, far, cross, z_cols, turned, p_part, d_part, squares):
    kind = far.dtype
    return pl.pallas_call(
        functools.partial(outer_kernel, z),
        out_shape=(
            z.tiles(2, kind),
            z.tiles(5, kind),
            jax.ShapeDtypeStruct((z.devices, 1, z.block), jnp.float32),
        ),
        in_specs=[SMEM] + [VMEM] * 8,
        out_specs=(HBM, VMEM, VMEM),
        scratch_shapes=[
            pltpu.VMEM((3, z.tile, z.tile), kind),
            pltpu.VMEM((3, z.tile, z.tile), kind),
            pltpu.VMEM((2, z.tile, z.tile), kind),
            pltpu.SemaphoreType.DMA(()),
        ],
        compiler_params=PARAMS,
        cost_estimate=z.cost(9, 4),
        name="outer",
    )(pattern, unit, far, cross, z_cols, turned, p_part, d_part, squares)


def middle_kernel(
    z, pattern_in, held16_in, held32_in, carry_in, refined, _a, _b, _c, _d, pattern, held16, held32, d_far,
    square, tiles, cells, sems,
):
    first, _ = half_starts(z)
    moves = (
        (pattern_in, pattern),
        (carry_in.at[pl.ds(3, 2)], d_far),
        (held16_in.at[pl.ds(0, 1)], held16.at[pl.ds(0, 1)]),
        (held32_in.at[pl.ds(3, 3)], held32.at[pl.ds(3, 3)]),
        (held16_in.at[pl.ds(3, 7)], held16.at[pl.ds(3, 7)]),
        (held32_in.at[pl.ds(0, 3)], held32.at[pl.ds(0, 3)]),
    )
    copies = [
        pltpu.make_async_copy(source, target, sems.at[k]) for k, (source, target) in enumerate(moves)
    ]
    for copy in copies:
        copy.start()
    for copy in copies[:4]:
        copy.wait()
    for i in (1, 2, 3):
        value = held32[2 + i]
        if i < 3:
            value = value + dot(d_far[i - 1], held16[0])
        square[i - 1] = own_masked(z, pattern, first, i - 1, value).astype(square.dtype)
    for copy in copies[4:]:
        copy.wait()
    for i in (1, 2, 3):
        total = None
        for k in range(max(1, i - 1), min(3, i + 1) + 1):
            term = dot(held16[3 * k - 1 + i - k + 1], square[k - 1])
            total = term if total is None else total + term
        tiles[i - 1] = own_masked(z, pattern, first, i - 1, held32[i - 1] + 0.375 * total)
    store_half(z, tiles, cells)
    copy = pltpu.make_async_copy(cells, refined.at[pl.ds(first, z.half)], sems.at[6])
    copy.start()
    copy.wait()


def middle_step(z, pattern, held16, held32, carry):
    kind = held16.dtype
    shape = (z.columns, z.offsets, z.block, z.block)
    return pl.pallas_call(
        functools.partial(middle_kernel, z),
        out_shape=(
            jax.ShapeDtypeStruct(shape, kind),
            jax.ShapeDtypeStruct(held16.shape, kind),
            jax.ShapeDtypeStruct(held32.shape, jnp.float32),
            jax.ShapeDtypeStruct(carry.shape, kind),
            jax.ShapeDtypeStruct(pattern.shape, pattern.dtype),
        ),
        in_specs=[HBM] * 4,
        out_specs=(HBM,) * 5,
        scratch_shapes=[
            pltpu.SMEM(pattern.shape, pattern.dtype),
            pltpu.VMEM(held16.shape, kind),
            pltpu.VMEM(held32.shape, jnp.float32),
            pltpu.VMEM((2, z.tile, z.tile), kind),
            pltpu.VMEM((3, z.tile, z.tile), kind),
            pltpu.VMEM((3, z.tile, z.tile), jnp.float32),
            pltpu.VMEM((z.half,) + shape[1:], kind),
            pltpu.SemaphoreType.DMA((7,)),
        ],
        input_output_aliases={1: 1, 2: 2, 3: 3, 0: 4},
        compiler_params=PARAMS,
        cost_estimate=z.cost(9, 6),
        name="middle",
    )(pattern, held16, held32, carry)


def last_kernel(
    z, pattern_in, held16, carry, d_in, _, refined, _a, _b, _c, _d, pattern, narrow, d_beyond, square,
    tiles, cells, sems,
):
    _, first = half_starts(z)
    moves = (
        (pattern_in, pattern),
        (d_in, d_beyond),
        (carry.at[pl.ds(2, 3)], narrow.at[pl.ds(0, 3)]),
        (held16.at[pl.ds(0, 2)], narrow.at[pl.ds(3, 2)]),
        (carry.at[pl.ds(0, 2)], narrow.at[pl.ds(5, 2)]),
        (held16.at[pl.ds(2, 5)], narrow.at[pl.ds(7, 5)]),
    )
    copies = [
        pltpu.make_async_copy(source, target, sems.at[k]) for k, (source, target) in enumerate(moves)
    ]
    for copy in copies:
        copy.start()
    for copy in copies[:4]:
        copy.wait()
    values = (
        dot(d_beyond[1], narrow[0]) + dot(narrow[0], narrow[1]),
        dot(d_beyond[0], narrow[0]) + dot(narrow[1], narrow[1]) + dot(narrow[3], narrow[2]),
        dot(narrow[2], narrow[1]) + dot(narrow[4], narrow[2]),
    )
    for i, value in enumerate(values):
        square[i] = own_masked(z, pattern, first, i, value).astype(square.dtype)
    for copy in copies[4:]:
        copy.wait()
    base = (4, 7, 10)
    for i in (0, 1, 2):
        half = None
        rest = None
        for k in range(max(0, i - 1), min(2, i + 1) + 1):
            left = narrow[base[k] + i - k + 1]
            term = dot(left, narrow[k])
            half = term if half is None else half + term
            term = dot(left, square[k])
            rest = term if rest is None else rest + term
        value = narrow[7 + i].astype(jnp.float32) + 0.5 * half + 0.375 * rest
        tiles[i] = own_masked(z, pattern, first, i, value)
    store_half(z, tiles, cells)
    copy = pltpu.make_async_copy(cells, refined.at[pl.ds(first, z.half)], sems.at[6])
    copy.start()
    copy.wait()


def last_step(z, pattern, held16, carry, d_in, refined):
    kind = refined.dtype
    return pl.pallas_call(
        functools.partial(last_kernel, z),
        out_shape=tuple(
            jax.ShapeDtypeStruct(held.shape, held.dtype) for held in (refined, held16, carry, d_in, pattern)
        ),
        in_specs=[HBM] * 5,
        out_specs=(HBM,) * 5,
        scratch_shapes=[
            pltpu.SMEM(pattern.shape, pattern.dtype),
            pltpu.VMEM((12, z.tile, z.tile), kind),
            pltpu.VMEM(d_in.shape, kind),
            pltpu.VMEM((3, z.tile, z.tile), kind),
            pltpu.VMEM((3, z.tile, z.tile), jnp.float32),
            pltpu.VMEM((z.half,) + refined.shape[1:], kind),
            pltpu.SemaphoreType.DMA((7,)),
        ],
        input_output_aliases={4: 0, 1: 1, 2: 2, 3: 3, 0: 4},
        compiler_params=PARAMS,
        cost_estimate=z.cost(21, 4),
        name="last",
    )(pattern, held16, carry, d_in, refined)


def norm_kernel(z, gathered, _, norm):
    mean = jnp.sum(gathered[...]) * (1.0 / z.entries)
    norm[...] = jnp.sqrt(jnp.full(norm.shape, mean, jnp.float32))


def norm_step(z, gathered, after):
    return pl.pallas_call(
        functools.partial(norm_kernel, z),
        out_shape=jax.ShapeDtypeStruct((1, z.block), jnp.float32),
        in_specs=[VMEM, HBM],
        out_specs=VMEM,
        compiler_params=PARAMS,
        name="norm",
    )(gathered, after)


def swaps(pairs):
    return [pair for i, j in pairs for pair in ((i, j), (j, i))]


def per_device(margin, factor, pattern):
    slabs = lax.axis_size("slab")
    devices = lax.axis_size("grp") * slabs
    z = Sizes(margin.shape, margin.shape[0] * slabs, devices)
    if slabs % 2 or z.columns != 2 * z.half:
        raise ValueError("sizes")
    near_pairs = [(i, i + 1) for i in range(0, devices - 1, 2)]
    far_pairs = [(i, i + 1) for i in range(1, devices - 1, 2)]
    inner_pairs = [(i, j) for i, j in far_pairs if j % slabs]
    cross_pairs = [(i, j) for i, j in far_pairs if not j % slabs]
    unit = unit_tile(z)
    near, far, cross = pack(z, margin, factor, pattern, unit)
    beyond = lax.ppermute(far, AXES, swaps(inner_pairs))
    across = lax.ppermute(cross, AXES, swaps(cross_pairs))
    beside = lax.ppermute(near, AXES, swaps(near_pairs))
    z_cols, turned, p_part, d_part, squares, held16, held32, flags = inner_step(
        z, pattern, unit, near, far, beside
    )
    d_out, carry, spread = outer_step(
        z, pattern, unit, beyond, across, z_cols, turned, p_part, d_part, squares
    )
    gathered = lax.all_to_all(spread, AXES, 0, 0, tiled=True)
    d_in = lax.ppermute(d_out, AXES, swaps(far_pairs))
    refined, held16, _, carry, flags = middle_step(z, flags, held16, held32, carry)
    refined, held16, _, _, _ = last_step(z, flags, held16, carry, d_in, refined)
    norm = norm_step(z, gathered, held16)
    return refined, norm[0, 0]


def solution(mesh):
    return jax.shard_map(
        per_device,
        mesh=mesh,
        in_specs=(
            P(AXES, None, None, None),
            P(AXES, None, None, None),
            P(AXES, None),
        ),
        out_specs=(P(AXES, None, None, None), P()),
        check_vma=False,
    )
```

```python
import functools

import jax
import jax.numpy as jnp
from jax import lax
from jax.experimental import pallas as pl
from jax.experimental.pallas import tpu as pltpu
from jax.sharding import PartitionSpec as P


AXES = ("grp", "slab")
HBM = pl.BlockSpec(memory_space=pltpu.HBM)
VMEM = pl.BlockSpec(memory_space=pltpu.VMEM)
SMEM = pl.BlockSpec(memory_space=pltpu.SMEM)
PARAMS = pltpu.CompilerParams(vmem_limit_bytes=32 * 1024 * 1024)
FLAG_ROWS = 16


class Sizes:
    def __init__(self, shape, quarter_len, devices):
        self.columns, self.offsets, self.block, _ = shape
        self.half = (self.offsets - 1) // 2
        self.tile = self.half * self.block
        self.cells = self.half * self.offsets
        self.flag_blocks = -(-self.half * self.half * FLAG_ROWS // self.block)
        self.quarter_len = quarter_len
        self.devices = devices
        self.entries = self.columns * devices * self.block

    def cost(self, products, moved):
        return pl.CostEstimate(
            flops=products * 2 * self.tile**3, bytes_accessed=moved * 2**20, transcendentals=0
        )

    def tiles(self, count, dtype):
        return jax.ShapeDtypeStruct((count, self.tile, self.tile), dtype)


def odd_device():
    return lax.rem(lax.axis_index("slab"), 2)


def half_starts(z):
    near = jnp.where(odd_device() == 1, 0, z.columns - z.half)
    return near, z.columns - z.half - near


def keep(flag, value):
    return jnp.where(flag, value, jnp.zeros_like(value))


def dot(left, right):
    return jnp.dot(left, right, preferred_element_type=jnp.float32)


def chain_tile(true_tile):
    return jnp.where(odd_device() == 1, 2 - true_tile, true_tile)


def expand(z, out, read):
    block = z.block
    for t in range(z.half):
        for a in range(3 * z.half):
            o = a - t
            u = a % z.half
            if 0 <= o < z.offsets:
                value = read(t, o)
            else:
                value = jnp.zeros((block, block), out.dtype)
            out[
                chain_tile(a // z.half),
                u * block : (u + 1) * block,
                t * block : (t + 1) * block,
            ] = value


def offset_of(z, e, t, u):
    return jnp.where(odd_device() == 1, 1 - e, e - 1) * z.half + u - t + z.half


def flag_of(z, pattern, first, e, t, u):
    o = offset_of(z, e, t, u)
    inside = jnp.logical_and(o >= 0, o < z.offsets)
    return jnp.logical_and(inside, pattern[first + t, jnp.clip(o, 0, z.offsets - 1)] != 0)


def masked(z, value, flag):
    block = z.block
    rows = []
    for u in range(z.half):
        rows.append(
            jnp.concatenate(
                [
                    keep(
                        flag(t, u),
                        value[u * block : (u + 1) * block, t * block : (t + 1) * block],
                    )
                    for t in range(z.half)
                ],
                axis=1,
            )
        )
    return jnp.concatenate(rows, axis=0)


def own_masked(z, pattern, first, e, value):
    return masked(z, value, lambda t, u: flag_of(z, pattern, first, e, t, u))


def identity(z):
    shape = (z.tile, z.tile)
    rows = lax.broadcasted_iota(jnp.int32, shape, 0)
    return (rows == lax.broadcasted_iota(jnp.int32, shape, 1)).astype(jnp.float32)


def tile_product(left, right, i, c, low, high):
    total = None
    for k in range(max(low, i - 1, c - 1), min(high, i + 1, c + 1) + 1):
        term = dot(left[k][i - k + 1], right[k - c + 1])
        total = term if total is None else total + term
    return total


def sum_squares(z, value):
    wide = value.astype(jnp.float32)
    return jnp.sum((wide * wide).reshape(-1, 8, z.tile), axis=0)


def store_half(z, tiles, cells):
    block = z.block
    for t in range(z.half):
        for o in range(z.offsets):
            a = t + o
            u = a % z.half
            value = tiles[
                chain_tile(a // z.half),
                u * block : (u + 1) * block,
                t * block : (t + 1) * block,
            ]
            cells[t, o] = value.astype(cells.dtype)


def unit_kernel(z, unit):
    unit[...] = identity(z)


def unit_tile(z):
    return pl.pallas_call(
        functools.partial(unit_kernel, z),
        out_shape=jax.ShapeDtypeStruct((z.tile, z.tile), jnp.float32),
        out_specs=VMEM,
        compiler_params=PARAMS,
        cost_estimate=z.cost(20, 1),
        name="unit",
    )()


def pack_kernel(z, margin, factor, pattern, _, near, far_s, far_z, cross):
    near_first, far_first = half_starts(z)
    first_row = lax.axis_index("slab") * z.columns
    plan = ((margin, far_first), (factor, far_first), (margin, near_first), (factor, near_first))
    for k, (source, first) in enumerate(plan):
        for t in range(z.half):
            for o in range(z.offsets):
                flag = pattern[first + t, o] != 0
                if k % 2:
                    row = first_row + first + t + o - z.half
                    inside = jnp.logical_and(row >= 0, row < z.quarter_len)
                    flag = jnp.logical_and(flag, inside)
                value = keep(flag, source[first + t, o])
                cell = t * z.offsets + o
                u = o + t - z.half
                if k == 0:
                    far_s[cell] = value
                    near[2 * z.cells + cell] = value
                elif k == 1:
                    far_z[cell] = value
                    if 0 <= u < z.half:
                        cross[t, u] = value
                else:
                    near[(k - 2) * z.cells + cell] = value
    per_block = z.block // FLAG_ROWS
    for f in range(z.flag_blocks * per_block):
        t, u = f // z.half, f % z.half
        value = jnp.zeros((FLAG_ROWS, z.block), near.dtype)
        if t < z.half:
            value = keep(pattern[near_first + t, u - t + z.half] != 0, jnp.ones_like(value))
        low = f % per_block * FLAG_ROWS
        near[3 * z.cells + f // per_block, low : low + FLAG_ROWS] = value


def pack(z, margin, factor, pattern, unit):
    kind = margin.dtype
    return pl.pallas_call(
        functools.partial(pack_kernel, z),
        out_shape=(
            jax.ShapeDtypeStruct((3 * z.cells + z.flag_blocks, z.block, z.block), kind),
            jax.ShapeDtypeStruct((z.cells, z.block, z.block), kind),
            jax.ShapeDtypeStruct((z.cells, z.block, z.block), kind),
            jax.ShapeDtypeStruct((z.half, z.half, z.block, z.block), kind),
        ),
        in_specs=[VMEM, VMEM, SMEM, VMEM],
        out_specs=(VMEM,) * 4,
        compiler_params=PARAMS,
        name="pack",
    )(margin, factor, pattern, unit)


def inner_kernel(
    z, pattern, unit, near, far_s, far_z, beside, z_cols, turned, p_part, d_part, squares, held16, held32,
    flags, s_cols, z_turned, image, d_near, d_beside, sums, sems,
):
    near_first, _ = half_starts(z)
    kind = near.dtype

    def cells_of(ref, base):
        return lambda t, o: ref[base + t * z.offsets + o]

    expand(z, s_cols.at[0], cells_of(far_s, 0))
    expand(z, s_cols.at[1], cells_of(near, 0))
    expand(z, s_cols.at[2], cells_of(beside, 0))
    expand(z, s_cols.at[3], cells_of(beside, 2 * z.cells))
    expand(z, z_cols.at[0], cells_of(far_z, 0))
    expand(z, z_cols.at[1], cells_of(near, z.cells))
    expand(z, z_cols.at[2], cells_of(beside, z.cells))
    moves = [
        (z_cols.at[0], held16.at[pl.ds(2, 3)]),
        (z_cols.at[1], held16.at[pl.ds(5, 3)]),
        (z_cols.at[2, pl.ds(0, 2)], held16.at[pl.ds(8, 2)]),
        (pattern, flags),
        (d_near.at[pl.ds(0, 2)], held16.at[pl.ds(0, 2)]),
        (sums, held32),
    ]
    copies = [
        pltpu.make_async_copy(source, target, sems.at[k]) for k, (source, target) in enumerate(moves)
    ]
    for copy in copies[:4]:
        copy.start()
    for x in range(3):
        for e in range(3):
            z_turned[x, e] = z_cols[x, e].T
    turned[0] = z_turned[0, 0]
    turned[1] = z_turned[0, 1]
    turned[2] = z_turned[1, 0]

    def image_tile(y, c):
        total = None
        for inner in range(max(c - 1, y - 1, 1), min(c + 1, y + 1) + 1):
            term = dot(s_cols[inner - 1, y - inner + 1], z_cols[c - 1, inner - c + 1])
            total = term if total is None else total + term
        return total

    def turned_sum(i, c, rows):
        total = None
        for m in rows:
            term = dot(z_turned[i - 1, m - i + 1], image[c - 1, m])
            total = term if total is None else total + term
        return total

    p_part[0] = image_tile(0, 1)
    p_part[1] = image_tile(1, 1)
    for c, rows in ((1, (2, 3)), (2, (0, 1, 2, 3, 4)), (3, (1, 2, 3, 4))):
        for y in rows:
            image[c - 1, y] = image_tile(y, c).astype(kind)
    d_part[0] = turned_sum(1, 1, (2,))
    d_part[1] = turned_sum(2, 1, (2, 3))
    eye = unit[...]
    total = jnp.zeros((8, z.tile), jnp.float32)
    for i in (1, 2, 3):
        value = -turned_sum(i, 2, (i - 1, i, i + 1))
        if i == 2:
            value = eye + value
        value = own_masked(z, pattern, near_first, i - 1, value).astype(kind)
        d_near[i - 1] = value
        total = total + sum_squares(z, value)
    squares[...] = total
    copies[4].start()

    def side_flag(t, u):
        o = offset_of(z, 0, t, u)
        inside = jnp.logical_and(o >= 0, o < z.offsets)
        back = jnp.clip(z.offsets - 1 - o, 0, z.offsets - 1)
        return jnp.logical_and(inside, pattern[near_first + u, back] != 0)

    d_beside[0] = masked(z, -turned_sum(2, 3, (1, 2, 3)), side_flag).astype(kind)
    value = eye - turned_sum(3, 3, (2, 3, 4))
    block = z.block
    per_block = block // FLAG_ROWS
    for t in range(z.half):
        for u in range(z.half):
            f = t * z.half + u
            low = f % per_block * FLAG_ROWS
            flags = beside[3 * z.cells + f // per_block, low : low + FLAG_ROWS]
            flag = flags.astype(jnp.float32)[:1]
            part = (slice(u * block, (u + 1) * block), slice(t * block, (t + 1) * block))
            d_beside[1, part[0], part[1]] = (value[part] * flag).astype(kind)

    factor = (None, z_cols.at[0], z_cols.at[1], z_cols.at[2])
    defect = (None, None, d_near, d_beside)
    for i in (1, 2, 3):
        sums[i - 1] = z_cols[1, i - 1].astype(jnp.float32) + 0.5 * tile_product(
            factor, d_near, i, 2, 1, 3
        )
        sums[2 + i] = tile_product(defect, d_near, i, 2, 2, 3)
    copies[5].start()
    for copy in copies:
        copy.wait()


def inner_step(z, pattern, unit, near, far_s, far_z, beside):
    kind = near.dtype
    tile = z.tile
    return pl.pallas_call(
        functools.partial(inner_kernel, z),
        out_shape=(
            jax.ShapeDtypeStruct((3, 3, tile, tile), kind),
            z.tiles(3, kind),
            z.tiles(2, jnp.float32),
            z.tiles(2, jnp.float32),
            jax.ShapeDtypeStruct((8, tile), jnp.float32),
            z.tiles(10, kind),
            z.tiles(6, jnp.float32),
            jax.ShapeDtypeStruct(pattern.shape, pattern.dtype),
        ),
        in_specs=[SMEM] + [VMEM] * 5,
        out_specs=(VMEM,) * 5 + (HBM,) * 3,
        scratch_shapes=[
            pltpu.VMEM((4, 3, tile, tile), kind),
            pltpu.VMEM((3, 3, tile, tile), kind),
            pltpu.VMEM((3, 5, tile, tile), kind),
            pltpu.VMEM((3, tile, tile), kind),
            pltpu.VMEM((2, tile, tile), kind),
            pltpu.VMEM((6, tile, tile), jnp.float32),
            pltpu.SemaphoreType.DMA((6,)),
        ],
        compiler_params=PARAMS,
        cost_estimate=z.cost(54, 8),
        name="inner",
    )(pattern, unit, near, far_s, far_z, beside)


def outer_kernel(
    z, pattern, unit, far, far_z, cross, z_cols, turned, p_part, d_part, squares, d_out, carry, spread, s_far,
    z_far, d_pair, sem,
):
    _, far_first = half_starts(z)
    kind = far.dtype

    def factor_cell(t, o):
        value = far_z[t * z.offsets + o]
        u = o + t - z.half
        if 0 <= u < z.half:
            value = value + cross[t, u]
        return value

    expand(z, s_far, lambda t, o: far[t * z.offsets + o])
    expand(z, z_far, factor_cell)
    carry[0] = z_far[1]
    carry[1] = z_far[2]
    copy = pltpu.make_async_copy(d_pair, d_out, sem)
    link = z_cols[0, 0]
    image = (
        dot(s_far[0], link).astype(kind),
        (dot(s_far[1], link) + p_part[0]).astype(kind),
        (dot(s_far[2], link) + p_part[1]).astype(kind),
    )
    values = (
        -(dot(z_far[0].T, image[0]) + dot(z_far[1].T, image[1]) + dot(z_far[2].T, image[2])),
        unit[...] - (dot(turned[0], image[1]) + dot(turned[1], image[2]) + d_part[0]),
        -(dot(turned[2], image[2]) + d_part[1]),
    )
    total = squares[...]
    for e, value in enumerate(values):
        value = own_masked(z, pattern, far_first, e, value).astype(kind)
        carry[2 + e] = value
        if e < 2:
            d_pair[e] = value
        if e == 1:
            copy.start()
        total = total + sum_squares(z, value)
    lanes = jnp.sum(total, axis=0, keepdims=True)
    folded = lanes[:, : z.block]
    for t in range(1, z.half):
        folded = folded + lanes[:, t * z.block : (t + 1) * z.block]
    spread[...] = jnp.broadcast_to(folded[None], spread.shape)
    copy.wait()


def outer_step(z, pattern, unit, far, far_z, cross, z_cols, turned, p_part, d_part, squares):
    kind = far.dtype
    return pl.pallas_call(
        functools.partial(outer_kernel, z),
        out_shape=(
            z.tiles(2, kind),
            z.tiles(5, kind),
            jax.ShapeDtypeStruct((z.devices, 1, z.block), jnp.float32),
        ),
        in_specs=[SMEM] + [VMEM] * 9,
        out_specs=(HBM, VMEM, VMEM),
        scratch_shapes=[
            pltpu.VMEM((3, z.tile, z.tile), kind),
            pltpu.VMEM((3, z.tile, z.tile), kind),
            pltpu.VMEM((2, z.tile, z.tile), kind),
            pltpu.SemaphoreType.DMA(()),
        ],
        compiler_params=PARAMS,
        cost_estimate=z.cost(9, 4),
        name="outer",
    )(pattern, unit, far, far_z, cross, z_cols, turned, p_part, d_part, squares)


def middle_kernel(
    z, pattern_in, held16_in, held32_in, carry_in, refined, _a, _b, _c, _d, pattern, held16, held32, d_far,
    square, tiles, cells, sems,
):
    first, _ = half_starts(z)
    moves = (
        (pattern_in, pattern),
        (carry_in.at[pl.ds(3, 2)], d_far),
        (held16_in.at[pl.ds(0, 1)], held16.at[pl.ds(0, 1)]),
        (held32_in.at[pl.ds(3, 3)], held32.at[pl.ds(3, 3)]),
        (held16_in.at[pl.ds(3, 7)], held16.at[pl.ds(3, 7)]),
        (held32_in.at[pl.ds(0, 3)], held32.at[pl.ds(0, 3)]),
    )
    copies = [
        pltpu.make_async_copy(source, target, sems.at[k]) for k, (source, target) in enumerate(moves)
    ]
    for copy in copies:
        copy.start()
    for copy in copies[:4]:
        copy.wait()
    for i in (1, 2, 3):
        value = held32[2 + i]
        if i < 3:
            value = value + dot(d_far[i - 1], held16[0])
        square[i - 1] = own_masked(z, pattern, first, i - 1, value).astype(square.dtype)
    for copy in copies[4:]:
        copy.wait()
    for i in (1, 2, 3):
        total = None
        for k in range(max(1, i - 1), min(3, i + 1) + 1):
            term = dot(held16[3 * k - 1 + i - k + 1], square[k - 1])
            total = term if total is None else total + term
        tiles[i - 1] = own_masked(z, pattern, first, i - 1, held32[i - 1] + 0.375 * total)
    store_half(z, tiles, cells)
    copy = pltpu.make_async_copy(cells, refined.at[pl.ds(first, z.half)], sems.at[6])
    copy.start()
    copy.wait()


def middle_step(z, pattern, held16, held32, carry):
    kind = held16.dtype
    shape = (z.columns, z.offsets, z.block, z.block)
    return pl.pallas_call(
        functools.partial(middle_kernel, z),
        out_shape=(
            jax.ShapeDtypeStruct(shape, kind),
            jax.ShapeDtypeStruct(held16.shape, kind),
            jax.ShapeDtypeStruct(held32.shape, jnp.float32),
            jax.ShapeDtypeStruct(carry.shape, kind),
            jax.ShapeDtypeStruct(pattern.shape, pattern.dtype),
        ),
        in_specs=[HBM] * 4,
        out_specs=(HBM,) * 5,
        scratch_shapes=[
            pltpu.SMEM(pattern.shape, pattern.dtype),
            pltpu.VMEM(held16.shape, kind),
            pltpu.VMEM(held32.shape, jnp.float32),
            pltpu.VMEM((2, z.tile, z.tile), kind),
            pltpu.VMEM((3, z.tile, z.tile), kind),
            pltpu.VMEM((3, z.tile, z.tile), jnp.float32),
            pltpu.VMEM((z.half,) + shape[1:], kind),
            pltpu.SemaphoreType.DMA((7,)),
        ],
        input_output_aliases={1: 1, 2: 2, 3: 3, 0: 4},
        compiler_params=PARAMS,
        cost_estimate=z.cost(9, 6),
        name="middle",
    )(pattern, held16, held32, carry)


def last_kernel(
    z, pattern_in, held16, carry, d_in, _, refined, _a, _b, _c, _d, pattern, narrow, d_beyond, square,
    tiles, cells, sems,
):
    _, first = half_starts(z)
    moves = (
        (pattern_in, pattern),
        (d_in, d_beyond),
        (carry.at[pl.ds(2, 3)], narrow.at[pl.ds(0, 3)]),
        (held16.at[pl.ds(0, 2)], narrow.at[pl.ds(3, 2)]),
        (carry.at[pl.ds(0, 2)], narrow.at[pl.ds(5, 2)]),
        (held16.at[pl.ds(2, 5)], narrow.at[pl.ds(7, 5)]),
    )
    copies = [
        pltpu.make_async_copy(source, target, sems.at[k]) for k, (source, target) in enumerate(moves)
    ]
    for copy in copies:
        copy.start()
    for copy in copies[:4]:
        copy.wait()
    values = (
        dot(d_beyond[1], narrow[0]) + dot(narrow[0], narrow[1]),
        dot(d_beyond[0], narrow[0]) + dot(narrow[1], narrow[1]) + dot(narrow[3], narrow[2]),
        dot(narrow[2], narrow[1]) + dot(narrow[4], narrow[2]),
    )
    for i, value in enumerate(values):
        square[i] = own_masked(z, pattern, first, i, value).astype(square.dtype)
    for copy in copies[4:]:
        copy.wait()
    base = (4, 7, 10)
    for i in (0, 1, 2):
        half = None
        rest = None
        for k in range(max(0, i - 1), min(2, i + 1) + 1):
            left = narrow[base[k] + i - k + 1]
            term = dot(left, narrow[k])
            half = term if half is None else half + term
            term = dot(left, square[k])
            rest = term if rest is None else rest + term
        value = narrow[7 + i].astype(jnp.float32) + 0.5 * half + 0.375 * rest
        tiles[i] = own_masked(z, pattern, first, i, value)
    store_half(z, tiles, cells)
    copy = pltpu.make_async_copy(cells, refined.at[pl.ds(first, z.half)], sems.at[6])
    copy.start()
    copy.wait()


def last_step(z, pattern, held16, carry, d_in, refined):
    kind = refined.dtype
    return pl.pallas_call(
        functools.partial(last_kernel, z),
        out_shape=tuple(
            jax.ShapeDtypeStruct(held.shape, held.dtype) for held in (refined, held16, carry, d_in, pattern)
        ),
        in_specs=[HBM] * 5,
        out_specs=(HBM,) * 5,
        scratch_shapes=[
            pltpu.SMEM(pattern.shape, pattern.dtype),
            pltpu.VMEM((12, z.tile, z.tile), kind),
            pltpu.VMEM(d_in.shape, kind),
            pltpu.VMEM((3, z.tile, z.tile), kind),
            pltpu.VMEM((3, z.tile, z.tile), jnp.float32),
            pltpu.VMEM((z.half,) + refined.shape[1:], kind),
            pltpu.SemaphoreType.DMA((7,)),
        ],
        input_output_aliases={4: 0, 1: 1, 2: 2, 3: 3, 0: 4},
        compiler_params=PARAMS,
        cost_estimate=z.cost(21, 4),
        name="last",
    )(pattern, held16, carry, d_in, refined)


def norm_kernel(z, gathered, _, norm):
    mean = jnp.sum(gathered[...]) * (1.0 / z.entries)
    norm[...] = jnp.sqrt(jnp.full(norm.shape, mean, jnp.float32))


def norm_step(z, gathered, after):
    return pl.pallas_call(
        functools.partial(norm_kernel, z),
        out_shape=jax.ShapeDtypeStruct((1, z.block), jnp.float32),
        in_specs=[VMEM, HBM],
        out_specs=VMEM,
        compiler_params=PARAMS,
        name="norm",
    )(gathered, after)


def swaps(pairs):
    return [pair for i, j in pairs for pair in ((i, j), (j, i))]


def per_device(margin, factor, pattern):
    slabs = lax.axis_size("slab")
    devices = lax.axis_size("grp") * slabs
    z = Sizes(margin.shape, margin.shape[0] * slabs, devices)
    if slabs % 2 or z.columns != 2 * z.half:
        raise ValueError("sizes")
    near_pairs = [(i, i + 1) for i in range(0, devices - 1, 2)]
    far_pairs = [(i, i + 1) for i in range(1, devices - 1, 2)]
    inner_pairs = [(i, j) for i, j in far_pairs if j % slabs]
    cross_pairs = [(i, j) for i, j in far_pairs if not j % slabs]
    unit = unit_tile(z)
    near, far_s, far_z, cross = pack(z, margin, factor, pattern, unit)
    beyond_s = lax.ppermute(far_s, AXES, swaps(inner_pairs))
    beyond_z = lax.ppermute(far_z, AXES, swaps(inner_pairs))
    across = lax.ppermute(cross, AXES, swaps(cross_pairs))
    beside = lax.ppermute(near, AXES, swaps(near_pairs))
    z_cols, turned, p_part, d_part, squares, held16, held32, flags = inner_step(
        z, pattern, unit, near, far_s, far_z, beside
    )
    d_out, carry, spread = outer_step(
        z, pattern, unit, beyond_s, beyond_z, across, z_cols, turned, p_part, d_part, squares
    )
    gathered = lax.all_to_all(spread, AXES, 0, 0, tiled=True)
    d_in = lax.ppermute(d_out, AXES, swaps(far_pairs))
    refined, held16, _, carry, flags = middle_step(z, flags, held16, held32, carry)
    refined, held16, _, _, _ = last_step(z, flags, held16, carry, d_in, refined)
    norm = norm_step(z, gathered, held16)
    return refined, norm[0, 0]


def solution(mesh):
    return jax.shard_map(
        per_device,
        mesh=mesh,
        in_specs=(
            P(AXES, None, None, None),
            P(AXES, None, None, None),
            P(AXES, None),
        ),
        out_specs=(P(AXES, None, None, None), P()),
        check_vma=False,
    )
```

```python
import functools

import jax
import jax.numpy as jnp
from jax import lax
from jax.experimental import pallas as pl
from jax.experimental.pallas import tpu as pltpu
from jax.sharding import PartitionSpec as P


AXES = ("grp", "slab")
HBM = pl.BlockSpec(memory_space=pltpu.HBM)
VMEM = pl.BlockSpec(memory_space=pltpu.VMEM)
SMEM = pl.BlockSpec(memory_space=pltpu.SMEM)
PARAMS = pltpu.CompilerParams(vmem_limit_bytes=32 * 1024 * 1024)
FLAG_ROWS = 16


class Sizes:
    def __init__(self, shape, quarter_len, devices):
        self.columns, self.offsets, self.block, _ = shape
        self.half = (self.offsets - 1) // 2
        self.tile = self.half * self.block
        self.cells = self.half * self.offsets
        self.flag_blocks = -(-self.half * self.half * FLAG_ROWS // self.block)
        self.quarter_len = quarter_len
        self.devices = devices
        self.entries = self.columns * devices * self.block

    def cost(self, products, moved):
        return pl.CostEstimate(
            flops=products * 2 * self.tile**3, bytes_accessed=moved * 2**20, transcendentals=0
        )

    def tiles(self, count, dtype):
        return jax.ShapeDtypeStruct((count, self.tile, self.tile), dtype)


def odd_device():
    return lax.rem(lax.axis_index("slab"), 2)


def half_starts(z):
    near = jnp.where(odd_device() == 1, 0, z.columns - z.half)
    return near, z.columns - z.half - near


def keep(flag, value):
    return jnp.where(flag, value, jnp.zeros_like(value))


def dot(left, right):
    return jnp.dot(left, right, preferred_element_type=jnp.float32)


def chain_tile(true_tile):
    return jnp.where(odd_device() == 1, 2 - true_tile, true_tile)


def expand(z, out, read):
    block = z.block
    for t in range(z.half):
        for a in range(3 * z.half):
            o = a - t
            u = a % z.half
            if 0 <= o < z.offsets:
                value = read(t, o)
            else:
                value = jnp.zeros((block, block), out.dtype)
            out[
                chain_tile(a // z.half),
                u * block : (u + 1) * block,
                t * block : (t + 1) * block,
            ] = value


def offset_of(z, e, t, u):
    return jnp.where(odd_device() == 1, 1 - e, e - 1) * z.half + u - t + z.half


def flag_of(z, pattern, first, e, t, u):
    o = offset_of(z, e, t, u)
    inside = jnp.logical_and(o >= 0, o < z.offsets)
    return jnp.logical_and(inside, pattern[first + t, jnp.clip(o, 0, z.offsets - 1)] != 0)


def masked(z, value, flag):
    block = z.block
    rows = []
    for u in range(z.half):
        rows.append(
            jnp.concatenate(
                [
                    keep(
                        flag(t, u),
                        value[u * block : (u + 1) * block, t * block : (t + 1) * block],
                    )
                    for t in range(z.half)
                ],
                axis=1,
            )
        )
    return jnp.concatenate(rows, axis=0)


def own_masked(z, pattern, first, e, value):
    return masked(z, value, lambda t, u: flag_of(z, pattern, first, e, t, u))


def identity(z):
    shape = (z.tile, z.tile)
    rows = lax.broadcasted_iota(jnp.int32, shape, 0)
    return (rows == lax.broadcasted_iota(jnp.int32, shape, 1)).astype(jnp.float32)


def tile_product(left, right, i, c, low, high):
    total = None
    for k in range(max(low, i - 1, c - 1), min(high, i + 1, c + 1) + 1):
        term = dot(left[k][i - k + 1], right[k - c + 1])
        total = term if total is None else total + term
    return total


def sum_squares(z, value):
    wide = value.astype(jnp.float32)
    return jnp.sum((wide * wide).reshape(-1, 8, z.tile), axis=0)


def store_half(z, tiles, cells):
    block = z.block
    for t in range(z.half):
        for o in range(z.offsets):
            a = t + o
            u = a % z.half
            value = tiles[
                chain_tile(a // z.half),
                u * block : (u + 1) * block,
                t * block : (t + 1) * block,
            ]
            cells[t, o] = value.astype(cells.dtype)


def unit_kernel(z, unit):
    unit[...] = identity(z)


def unit_tile(z):
    return pl.pallas_call(
        functools.partial(unit_kernel, z),
        out_shape=jax.ShapeDtypeStruct((z.tile, z.tile), jnp.float32),
        out_specs=VMEM,
        compiler_params=PARAMS,
        cost_estimate=z.cost(20, 1),
        name="unit",
    )()


def pack_kernel(z, margin, factor, pattern, _, near, far_s, far_z, cross):
    near_first, far_first = half_starts(z)
    first_row = lax.axis_index("slab") * z.columns
    plan = ((margin, far_first), (factor, far_first), (margin, near_first), (factor, near_first))
    for k, (source, first) in enumerate(plan):
        for t in range(z.half):
            for o in range(z.offsets):
                flag = pattern[first + t, o] != 0
                if k % 2:
                    row = first_row + first + t + o - z.half
                    inside = jnp.logical_and(row >= 0, row < z.quarter_len)
                    flag = jnp.logical_and(flag, inside)
                value = keep(flag, source[first + t, o])
                cell = t * z.offsets + o
                u = o + t - z.half
                if k == 0:
                    far_s[cell] = value
                    near[2 * z.cells + cell] = value
                elif k == 1:
                    far_z[cell] = value
                    if 0 <= u < z.half:
                        cross[t, u] = value
                else:
                    near[(k - 2) * z.cells + cell] = value
    per_block = z.block // FLAG_ROWS
    for f in range(z.flag_blocks * per_block):
        t, u = f // z.half, f % z.half
        value = jnp.zeros((FLAG_ROWS, z.block), near.dtype)
        if t < z.half:
            value = keep(pattern[near_first + t, u - t + z.half] != 0, jnp.ones_like(value))
        low = f % per_block * FLAG_ROWS
        near[3 * z.cells + f // per_block, low : low + FLAG_ROWS] = value


def pack(z, margin, factor, pattern, unit):
    kind = margin.dtype
    return pl.pallas_call(
        functools.partial(pack_kernel, z),
        out_shape=(
            jax.ShapeDtypeStruct((3 * z.cells + z.flag_blocks, z.block, z.block), kind),
            jax.ShapeDtypeStruct((z.cells, z.block, z.block), kind),
            jax.ShapeDtypeStruct((z.cells, z.block, z.block), kind),
            jax.ShapeDtypeStruct((z.half, z.half, z.block, z.block), kind),
        ),
        in_specs=[VMEM, VMEM, SMEM, VMEM],
        out_specs=(VMEM,) * 4,
        compiler_params=PARAMS,
        name="pack",
    )(margin, factor, pattern, unit)


def inner_kernel(
    z, pattern, unit, near, far_s, far_z, beside, z_cols, turned, p_part, d_part, squares, held16, held32,
    flags, s_cols, z_turned, image, d_near, d_beside, sums, sems,
):
    near_first, _ = half_starts(z)
    kind = near.dtype

    def cells_of(ref, base):
        return lambda t, o: ref[base + t * z.offsets + o]

    expand(z, s_cols.at[0], cells_of(far_s, 0))
    expand(z, s_cols.at[1], cells_of(near, 0))
    expand(z, s_cols.at[2], cells_of(beside, 0))
    expand(z, s_cols.at[3], cells_of(beside, 2 * z.cells))
    expand(z, z_cols.at[0], cells_of(far_z, 0))
    expand(z, z_cols.at[1], cells_of(near, z.cells))
    expand(z, z_cols.at[2], cells_of(beside, z.cells))
    moves = [
        (z_cols.at[0], held16.at[pl.ds(2, 3)]),
        (z_cols.at[1], held16.at[pl.ds(5, 3)]),
        (z_cols.at[2, pl.ds(0, 2)], held16.at[pl.ds(8, 2)]),
        (pattern, flags),
        (d_near.at[pl.ds(0, 2)], held16.at[pl.ds(0, 2)]),
        (sums, held32),
    ]
    copies = [
        pltpu.make_async_copy(source, target, sems.at[k]) for k, (source, target) in enumerate(moves)
    ]
    for copy in copies[:4]:
        copy.start()
    for x in range(3):
        for e in range(3):
            z_turned[x, e] = z_cols[x, e].T
    turned[0] = z_turned[0, 0]
    turned[1] = z_turned[0, 1]
    turned[2] = z_turned[1, 0]

    def image_tile(y, c):
        total = None
        for inner in range(max(c - 1, y - 1, 1), min(c + 1, y + 1) + 1):
            term = dot(s_cols[inner - 1, y - inner + 1], z_cols[c - 1, inner - c + 1])
            total = term if total is None else total + term
        return total

    def turned_sum(i, c, rows):
        total = None
        for m in rows:
            term = dot(z_turned[i - 1, m - i + 1], image[c - 1, m])
            total = term if total is None else total + term
        return total

    p_part[0] = image_tile(0, 1)
    p_part[1] = image_tile(1, 1)
    for c, rows in ((1, (2, 3)), (2, (0, 1, 2, 3, 4)), (3, (1, 2, 3, 4))):
        for y in rows:
            image[c - 1, y] = image_tile(y, c).astype(kind)
    d_part[0] = turned_sum(1, 1, (2,))
    d_part[1] = turned_sum(2, 1, (2, 3))
    eye = unit[...]
    total = jnp.zeros((8, z.tile), jnp.float32)
    for i in (1, 2, 3):
        value = -turned_sum(i, 2, (i - 1, i, i + 1))
        if i == 2:
            value = eye + value
        value = own_masked(z, pattern, near_first, i - 1, value).astype(kind)
        d_near[i - 1] = value
        total = total + sum_squares(z, value)
    squares[...] = total
    copies[4].start()

    def side_flag(t, u):
        o = offset_of(z, 0, t, u)
        inside = jnp.logical_and(o >= 0, o < z.offsets)
        back = jnp.clip(z.offsets - 1 - o, 0, z.offsets - 1)
        return jnp.logical_and(inside, pattern[near_first + u, back] != 0)

    d_beside[0] = masked(z, -turned_sum(2, 3, (1, 2, 3)), side_flag).astype(kind)
    value = eye - turned_sum(3, 3, (2, 3, 4))
    block = z.block
    per_block = block // FLAG_ROWS
    for t in range(z.half):
        for u in range(z.half):
            f = t * z.half + u
            low = f % per_block * FLAG_ROWS
            flags = beside[3 * z.cells + f // per_block, low : low + FLAG_ROWS]
            flag = flags.astype(jnp.float32)[:1]
            part = (slice(u * block, (u + 1) * block), slice(t * block, (t + 1) * block))
            d_beside[1, part[0], part[1]] = (value[part] * flag).astype(kind)

    factor = (None, z_cols.at[0], z_cols.at[1], z_cols.at[2])
    defect = (None, None, d_near, d_beside)
    for i in (1, 2, 3):
        sums[i - 1] = z_cols[1, i - 1].astype(jnp.float32) + 0.5 * tile_product(
            factor, d_near, i, 2, 1, 3
        )
        sums[2 + i] = tile_product(defect, d_near, i, 2, 2, 3)
    copies[5].start()
    for copy in copies:
        copy.wait()


def inner_step(z, pattern, unit, near, far_s, far_z, beside):
    kind = near.dtype
    tile = z.tile
    return pl.pallas_call(
        functools.partial(inner_kernel, z),
        out_shape=(
            jax.ShapeDtypeStruct((3, 3, tile, tile), kind),
            z.tiles(3, kind),
            z.tiles(2, jnp.float32),
            z.tiles(2, jnp.float32),
            jax.ShapeDtypeStruct((8, tile), jnp.float32),
            z.tiles(10, kind),
            z.tiles(6, jnp.float32),
            jax.ShapeDtypeStruct(pattern.shape, pattern.dtype),
        ),
        in_specs=[SMEM] + [VMEM] * 5,
        out_specs=(VMEM,) * 5 + (HBM,) * 3,
        scratch_shapes=[
            pltpu.VMEM((4, 3, tile, tile), kind),
            pltpu.VMEM((3, 3, tile, tile), kind),
            pltpu.VMEM((3, 5, tile, tile), kind),
            pltpu.VMEM((3, tile, tile), kind),
            pltpu.VMEM((2, tile, tile), kind),
            pltpu.VMEM((6, tile, tile), jnp.float32),
            pltpu.SemaphoreType.DMA((6,)),
        ],
        compiler_params=PARAMS,
        cost_estimate=z.cost(54, 8),
        name="inner",
    )(pattern, unit, near, far_s, far_z, beside)


def outer_kernel(
    z, pattern, unit, far, far_z, cross, z_cols, turned, p_part, d_part, squares, d_out, carry, spread, s_far,
    z_far, d_pair, sem,
):
    _, far_first = half_starts(z)
    kind = far.dtype

    def factor_cell(t, o):
        value = far_z[t * z.offsets + o]
        u = o + t - z.half
        if 0 <= u < z.half:
            value = value + cross[t, u]
        return value

    expand(z, s_far, lambda t, o: far[t * z.offsets + o])
    expand(z, z_far, factor_cell)
    carry[0] = z_far[1]
    carry[1] = z_far[2]
    copy = pltpu.make_async_copy(d_pair, d_out, sem)
    link = z_cols[0, 0]
    image = (
        dot(s_far[0], link).astype(kind),
        (dot(s_far[1], link) + p_part[0]).astype(kind),
        (dot(s_far[2], link) + p_part[1]).astype(kind),
    )
    values = (
        -(dot(z_far[0].T, image[0]) + dot(z_far[1].T, image[1]) + dot(z_far[2].T, image[2])),
        unit[...] - (dot(turned[0], image[1]) + dot(turned[1], image[2]) + d_part[0]),
        -(dot(turned[2], image[2]) + d_part[1]),
    )
    total = squares[...]
    for e, value in enumerate(values):
        value = own_masked(z, pattern, far_first, e, value).astype(kind)
        carry[2 + e] = value
        if e < 2:
            d_pair[e] = value
        if e == 1:
            copy.start()
        total = total + sum_squares(z, value)
    lanes = jnp.sum(total, axis=0, keepdims=True)
    folded = lanes[:, : z.block]
    for t in range(1, z.half):
        folded = folded + lanes[:, t * z.block : (t + 1) * z.block]
    spread[...] = jnp.broadcast_to(folded[None], spread.shape)
    copy.wait()


def outer_step(z, pattern, unit, far, far_z, cross, z_cols, turned, p_part, d_part, squares):
    kind = far.dtype
    return pl.pallas_call(
        functools.partial(outer_kernel, z),
        out_shape=(
            z.tiles(2, kind),
            z.tiles(5, kind),
            jax.ShapeDtypeStruct((z.devices, 1, z.block), jnp.float32),
        ),
        in_specs=[SMEM] + [VMEM] * 9,
        out_specs=(HBM, VMEM, VMEM),
        scratch_shapes=[
            pltpu.VMEM((3, z.tile, z.tile), kind),
            pltpu.VMEM((3, z.tile, z.tile), kind),
            pltpu.VMEM((2, z.tile, z.tile), kind),
            pltpu.SemaphoreType.DMA(()),
        ],
        compiler_params=PARAMS,
        cost_estimate=z.cost(9, 4),
        name="outer",
    )(pattern, unit, far, far_z, cross, z_cols, turned, p_part, d_part, squares)


def middle_kernel(
    z, pattern_in, held16_in, held32_in, carry_in, refined, _a, _b, _c, _d, pattern, held16, held32, d_far,
    square, tiles, cells, sems,
):
    first, _ = half_starts(z)
    moves = (
        (pattern_in, pattern),
        (carry_in.at[pl.ds(3, 2)], d_far),
        (held16_in.at[pl.ds(0, 1)], held16.at[pl.ds(0, 1)]),
        (held32_in.at[pl.ds(3, 3)], held32.at[pl.ds(3, 3)]),
        (held16_in.at[pl.ds(3, 7)], held16.at[pl.ds(3, 7)]),
        (held32_in.at[pl.ds(0, 3)], held32.at[pl.ds(0, 3)]),
    )
    copies = [
        pltpu.make_async_copy(source, target, sems.at[k]) for k, (source, target) in enumerate(moves)
    ]
    for copy in copies:
        copy.start()
    for copy in copies[:4]:
        copy.wait()
    for i in (1, 2, 3):
        value = held32[2 + i]
        if i < 3:
            value = value + dot(d_far[i - 1], held16[0])
        square[i - 1] = own_masked(z, pattern, first, i - 1, value).astype(square.dtype)
    for copy in copies[4:]:
        copy.wait()
    for i in (1, 2, 3):
        total = None
        for k in range(max(1, i - 1), min(3, i + 1) + 1):
            term = dot(held16[3 * k - 1 + i - k + 1], square[k - 1])
            total = term if total is None else total + term
        tiles[i - 1] = own_masked(z, pattern, first, i - 1, held32[i - 1] + 0.375 * total)
    store_half(z, tiles, cells)
    copy = pltpu.make_async_copy(cells, refined.at[pl.ds(first, z.half)], sems.at[6])
    copy.start()
    copy.wait()


def middle_step(z, pattern, held16, held32, carry):
    kind = held16.dtype
    shape = (z.columns, z.offsets, z.block, z.block)
    return pl.pallas_call(
        functools.partial(middle_kernel, z),
        out_shape=(
            jax.ShapeDtypeStruct(shape, kind),
            jax.ShapeDtypeStruct(held16.shape, kind),
            jax.ShapeDtypeStruct(held32.shape, jnp.float32),
            jax.ShapeDtypeStruct(carry.shape, kind),
            jax.ShapeDtypeStruct(pattern.shape, pattern.dtype),
        ),
        in_specs=[HBM] * 4,
        out_specs=(HBM,) * 5,
        scratch_shapes=[
            pltpu.SMEM(pattern.shape, pattern.dtype),
            pltpu.VMEM(held16.shape, kind),
            pltpu.VMEM(held32.shape, jnp.float32),
            pltpu.VMEM((2, z.tile, z.tile), kind),
            pltpu.VMEM((3, z.tile, z.tile), kind),
            pltpu.VMEM((3, z.tile, z.tile), jnp.float32),
            pltpu.VMEM((z.half,) + shape[1:], kind),
            pltpu.SemaphoreType.DMA((7,)),
        ],
        input_output_aliases={1: 1, 2: 2, 3: 3, 0: 4},
        compiler_params=PARAMS,
        cost_estimate=z.cost(9, 6),
        name="middle",
    )(pattern, held16, held32, carry)


def last_kernel(
    z, pattern_in, held16, carry, d_in, _, refined, _a, _b, _c, _d, pattern, narrow, d_beyond, square,
    tiles, cells, sems,
):
    _, first = half_starts(z)
    moves = (
        (pattern_in, pattern),
        (d_in, d_beyond),
        (carry.at[pl.ds(2, 3)], narrow.at[pl.ds(0, 3)]),
        (held16.at[pl.ds(0, 2)], narrow.at[pl.ds(3, 2)]),
        (carry.at[pl.ds(0, 2)], narrow.at[pl.ds(5, 2)]),
        (held16.at[pl.ds(2, 5)], narrow.at[pl.ds(7, 5)]),
    )
    copies = [
        pltpu.make_async_copy(source, target, sems.at[k]) for k, (source, target) in enumerate(moves)
    ]
    for copy in copies:
        copy.start()
    for copy in copies[:4]:
        copy.wait()
    values = (
        dot(d_beyond[1], narrow[0]) + dot(narrow[0], narrow[1]),
        dot(d_beyond[0], narrow[0]) + dot(narrow[1], narrow[1]) + dot(narrow[3], narrow[2]),
        dot(narrow[2], narrow[1]) + dot(narrow[4], narrow[2]),
    )
    for i, value in enumerate(values):
        square[i] = own_masked(z, pattern, first, i, value).astype(square.dtype)
    for copy in copies[4:]:
        copy.wait()
    base = (4, 7, 10)
    for i in (0, 1, 2):
        half = None
        rest = None
        for k in range(max(0, i - 1), min(2, i + 1) + 1):
            left = narrow[base[k] + i - k + 1]
            term = dot(left, narrow[k])
            half = term if half is None else half + term
            term = dot(left, square[k])
            rest = term if rest is None else rest + term
        value = narrow[7 + i].astype(jnp.float32) + 0.5 * half + 0.375 * rest
        tiles[i] = own_masked(z, pattern, first, i, value)
    store_half(z, tiles, cells)
    copy = pltpu.make_async_copy(cells, refined.at[pl.ds(first, z.half)], sems.at[6])
    copy.start()
    copy.wait()


def last_step(z, pattern, held16, carry, d_in, refined):
    kind = refined.dtype
    return pl.pallas_call(
        functools.partial(last_kernel, z),
        out_shape=tuple(
            jax.ShapeDtypeStruct(held.shape, held.dtype) for held in (refined, held16, carry, d_in, pattern)
        ),
        in_specs=[HBM] * 5,
        out_specs=(HBM,) * 5,
        scratch_shapes=[
            pltpu.SMEM(pattern.shape, pattern.dtype),
            pltpu.VMEM((12, z.tile, z.tile), kind),
            pltpu.VMEM(d_in.shape, kind),
            pltpu.VMEM((3, z.tile, z.tile), kind),
            pltpu.VMEM((3, z.tile, z.tile), jnp.float32),
            pltpu.VMEM((z.half,) + refined.shape[1:], kind),
            pltpu.SemaphoreType.DMA((7,)),
        ],
        input_output_aliases={4: 0, 1: 1, 2: 2, 3: 3, 0: 4},
        compiler_params=PARAMS,
        cost_estimate=z.cost(21, 4),
        name="last",
    )(pattern, held16, carry, d_in, refined)


def norm_kernel(z, gathered, _, norm):
    mean = jnp.sum(jnp.sum(gathered[...], axis=0)) * (1.0 / z.entries)
    norm[...] = jnp.sqrt(jnp.full(norm.shape, mean, jnp.float32))


def norm_step(z, gathered, after):
    return pl.pallas_call(
        functools.partial(norm_kernel, z),
        out_shape=jax.ShapeDtypeStruct((1, z.block), jnp.float32),
        in_specs=[VMEM, HBM],
        out_specs=VMEM,
        compiler_params=PARAMS,
        name="norm",
    )(gathered, after)


def swaps(pairs):
    return [pair for i, j in pairs for pair in ((i, j), (j, i))]


def per_device(margin, factor, pattern):
    slabs = lax.axis_size("slab")
    devices = lax.axis_size("grp") * slabs
    z = Sizes(margin.shape, margin.shape[0] * slabs, devices)
    if slabs % 2 or z.columns != 2 * z.half:
        raise ValueError("sizes")
    near_pairs = [(i, i + 1) for i in range(0, devices - 1, 2)]
    far_pairs = [(i, i + 1) for i in range(1, devices - 1, 2)]
    inner_pairs = [(i, j) for i, j in far_pairs if j % slabs]
    cross_pairs = [(i, j) for i, j in far_pairs if not j % slabs]
    unit = unit_tile(z)
    near, far_s, far_z, cross = pack(z, margin, factor, pattern, unit)
    beyond_s = lax.ppermute(far_s, AXES, swaps(inner_pairs))
    beyond_z = lax.ppermute(far_z, AXES, swaps(inner_pairs))
    across = lax.ppermute(cross, AXES, swaps(cross_pairs))
    beside = lax.ppermute(near, AXES, swaps(near_pairs))
    z_cols, turned, p_part, d_part, squares, held16, held32, flags = inner_step(
        z, pattern, unit, near, far_s, far_z, beside
    )
    d_out, carry, spread = outer_step(
        z, pattern, unit, beyond_s, beyond_z, across, z_cols, turned, p_part, d_part, squares
    )
    gathered = lax.all_to_all(spread, AXES, 0, 0, tiled=True)
    d_in = lax.ppermute(d_out, AXES, swaps(far_pairs))
    refined, held16, _, carry, flags = middle_step(z, flags, held16, held32, carry)
    refined, held16, _, _, _ = last_step(z, flags, held16, carry, d_in, refined)
    norm = norm_step(z, gathered, held16)
    return refined, norm[0, 0]


def solution(mesh):
    return jax.shard_map(
        per_device,
        mesh=mesh,
        in_specs=(
            P(AXES, None, None, None),
            P(AXES, None, None, None),
            P(AXES, None),
        ),
        out_specs=(P(AXES, None, None, None), P()),
        check_vma=False,
    )
```
